256 devices in a mesh: tm: 4 (over y), space: 64 (over x, z, core).
Axes of the slice: x: 4, y: 4, z: 8, core: 2. Of those that a mesh axis runs over, the one named last changes fastest.
Arguments:
- forcing: float32 [12, 8, 512, 512], P('tm', None, 'space'), may hold values from -6 to 6
- courant: float32 [2, 8, 512, 512], P(None, None, 'space'), may hold values from 0.05 to 0.45
- innovation: bfloat16 [12, 256, 16384], P('tm', None, 'space'), may hold values from -6 to 6
- obs_cells: int32 [12, 4, 16384], P('tm', None, 'space'), may hold values from 0 to 4095
- obs_weight: bfloat16 [12, 4, 16384], P('tm', None, 'space'), may hold values from 0 to 1
- obs_owner: int32 [12, 16384, 1], P('tm', 'space'), may hold values from 0 to 63; in each aligned block of 256 rows (0 to 255, 256 to 511, ..., all dimensions but the last counted through in order) at most 16 rows name the same one
- channel_weight: float32 [256, 8], replicated, may hold values from -2 to 2
- channel_rinv: float32 [256], replicated, may hold values from 0.1 to 0.5
Outputs:
- gradient: float32 [12, 8, 512, 512], P('tm', None, 'space')
The draws below stay inside these ranges and needn't reach their ends.
Inputs may be any that keep to these rules, and one draw needn't show every extreme that they name: `obs_owner`: in each sub-window, no tile is named by more than 16 of the 256 records of one device (the rows of one device form an aligned block), a bound that some block reaches.
All inputs are finite; a program needn't handle non-finite values.
Results may differ from the reference program's by a relative error of at most 0.00075.
Values may be sent and summed in bfloat16 or wider, within the bound.
No kernel may reach another device: no remote copies, remote signals or barrier semaphores. Data moves between devices by JAX's collectives and lax.ppermute only.
A program may use at most 64 MiB of HBM per device.

```python
import math
import jax
import jax.numpy as jnp
import numpy as np
from jax import lax

L = 8
CH = 256
STEPS = 2
TY = 8
NX = 512
OBS_DEV = 256
NSUB = 12
NY = 512
OBS_TOTAL = 16384
CAP = 16
N_SPACE = 64


def plant(result, rng, least, top_value):
    dims = result.shape
    spot = [jax.random.randint(jax.random.fold_in(rng, axis), (), 0, dims[axis]) for axis in range(len(dims))]
    result = result.at[tuple(spot)].set(least)
    longest = dims.index(max(dims))
    spot[longest] = (spot[longest] + 1) % dims[longest]
    return result.at[tuple(spot)].set(top_value)


def block_scale(stream_key, shape, shards, least, high):
    factor_of = 1.0
    for position, parts in shards:
        draws = jax.random.uniform(jax.random.fold_in(jax.random.fold_in(stream_key, 6), position), (parts,), jnp.float32, least / len(shards), high / len(shards))
        factor_of = factor_of * jnp.repeat(jnp.exp(draws), shape[position] // parts).reshape((-1,) + (1,) * (len(shape) - 1 - position))
    return factor_of


def assign_block(stream_key, own, number, rows, count, top, limit, slope):
    order = jax.random.permutation(stream_key, count)
    crowded, common = portions_of(count, rows * top, limit, slope, True), portions_of(count, rows * top, limit, slope, False)
    places = jnp.arange(count)

    def named(lengths, turn):
        used = int((lengths > 0).sum())
        fixed = max(1, used // 4)
        shifted = fixed + (places - fixed + turn * (used - fixed)) % max(1, count - fixed)
        return jnp.zeros((count,), jnp.int32).at[order[jnp.where(places < fixed, places, shifted)]].set(jnp.asarray(lengths, jnp.int32))

    lengths = jnp.where(number % 4 == 0, named(crowded, number // 4), named(common, number - number // 4 - 1))
    mixed = jax.random.permutation(jax.random.fold_in(own, 3), count)
    donor, receiver = mixed[0:count // 2 * 2:2], mixed[1:count // 2 * 2:2]
    margin = jnp.minimum(lengths[donor] - 1, limit - lengths[receiver]) // 2
    margin = jnp.where((donor == order[0]) | (receiver == order[0]) | (lengths[receiver] == 0), 0, jnp.maximum(margin, 0))
    shifted = jax.random.randint(jax.random.fold_in(own, 4), (count // 2,), 0, 1 << 20) % (margin + 1)
    lengths = lengths.at[donor].add(-shifted).at[receiver].add(shifted)
    items = jnp.searchsorted(jnp.cumsum(lengths), jnp.arange(rows * top), side="right").astype(jnp.int32)
    grid = items.reshape(top, rows).T
    grid = grid[jax.random.permutation(jax.random.fold_in(own, 1), rows)]
    turn = jax.random.randint(jax.random.fold_in(own, 2), (rows, 1), 0, top)
    return jnp.take_along_axis(grid, (jnp.arange(top)[None, :] + turn) % top, axis=1)


def portions_of(number_of, total, most, slope, full):
    weights = [(1 << 20) // math.isqrt(standing ** slope) + 1 for standing in range(1, number_of + 1)]
    largest = most if full else min(most, max(-(-total // number_of), total * weights[0] // sum(weights)))
    least = 1 if total - largest >= number_of - 1 else 0
    given, rest = [largest] + [least] * (number_of - 1), total - largest - least * (number_of - 1)
    while rest > 0:
        movable = [i for i in range(1, number_of) if given[i] < largest] or [i for i in range(1, number_of) if given[i] < most]
        pool, remaining = sum([weights[i] for i in movable]), rest
        for i in movable:
            more = min(most - given[i], max(1, remaining * weights[i] // pool), rest)
            given[i] = given[i] + more
            rest = rest - more
    return np.array(given)


def gaussian(own_key, dims, width, most, split=(), kind=jnp.bfloat16):
    values = jax.random.normal(own_key, dims, jnp.float32) * width
    if len(split) > 0:
        values = block_scale(own_key, dims, split, -0.22, 0.18) * values
    return jnp.clip(values, min=-most, max=most).astype(kind)


def setup_inputs(seed: int = 0) -> dict:
    arg_keys = jax.random.split(jax.random.key(seed), 9)
    forcing = gaussian(arg_keys[0], (NSUB, L, NY, NX), 1.0, 6.0, ((0, 4), (2, 64)), jnp.float32)
    courant = jnp.clip(0.05 + 0.39999999 * jax.random.uniform(arg_keys[1], (2, L, NY, NX), jnp.float32) ** block_scale(arg_keys[1], (2, L, NY, NX), ((2, 64),), -0.2, 0.2), 0.05, 0.45)
    innovation = gaussian(arg_keys[2], (NSUB, CH, OBS_TOTAL), 1.0, 6.0, ((0, 4), (2, 64)))
    obs_cells = plant(jax.random.randint(arg_keys[3], (NSUB, 4, OBS_TOTAL), 0, TY * NX), jax.random.fold_in(arg_keys[3], 1), 0, (TY * NX) - 1).astype(jnp.int32)
    obs_weight = jnp.clip(1.0 * jax.random.uniform(arg_keys[4], (NSUB, 4, OBS_TOTAL), jnp.float32) ** block_scale(arg_keys[4], (NSUB, 4, OBS_TOTAL), ((0, 4), (2, 64)), -0.2, 0.2), 0.0, 1.0).astype(jnp.bfloat16)
    obs_owner_keys = jax.random.split(jax.random.fold_in(arg_keys[5], 1), NSUB * OBS_TOTAL // OBS_DEV)
    obs_owner_turns = jax.random.permutation(jax.random.fold_in(arg_keys[5], 3), NSUB * OBS_TOTAL // OBS_DEV)
    obs_owner = jax.vmap(lambda own, number: assign_block(jax.random.fold_in(arg_keys[5], 2), own, number, OBS_DEV, N_SPACE, 1, CAP, 2))(obs_owner_keys, obs_owner_turns).reshape((NSUB, OBS_TOTAL, 1))
    channel_weight = gaussian(arg_keys[6], (CH, L), L ** -0.5, 2.0, (), jnp.float32)
    channel_rinv = jnp.clip(jnp.exp(jax.random.uniform(arg_keys[7], (CH,), jnp.float32, math.log(0.1), math.log(0.5))), 0.1, 0.5)
    return {"forcing": forcing, "courant": courant, "innovation": innovation, "obs_cells": obs_cells, "obs_weight": obs_weight, "obs_owner": obs_owner, "channel_weight": channel_weight, "channel_rinv": channel_rinv}


highest = lax.Precision.HIGHEST


def forward_step(current, wind_x, wind_y):
    previous_y = jnp.concatenate([jnp.zeros_like(current[:, :1, :]), current[:, :-1, :]], axis=1)
    previous_x = jnp.roll(current, 1, axis=2)
    return current - wind_x * (current - previous_x) - wind_y * (current - previous_y)


def adjoint_step(current, wind_x, wind_y):
    carried = wind_y * current
    following = jnp.concatenate([carried[:, 1:, :], jnp.zeros_like(carried[:, :1, :])], axis=1)
    return current * (1.0 - wind_x - wind_y) + jnp.roll(wind_x * current, -1, axis=2) + following


def reference(forcing, courant, innovation, obs_cells, obs_weight, obs_owner, channel_weight, channel_rinv):
    wind_x = courant[0]
    wind_y = courant[1]
    tile_cells = TY * NX
    current = jnp.zeros((L, NY, NX), jnp.float32)
    adjoint_terms = []
    for sub_index in range(NSUB):
        current = current + forcing[sub_index]
        for step_index in range(STEPS):
            current = forward_step(current, wind_x, wind_y)
        global_cell = (obs_owner[sub_index, :, 0][None, :] * tile_cells + obs_cells[sub_index]).astype(jnp.int32)
        weights = obs_weight[sub_index].astype(jnp.float32)
        flat_state = current.reshape(L, NY * NX)
        columns = jnp.sum(flat_state[:, global_cell] * weights[None], axis=1)
        evolved = jnp.dot(channel_weight, columns, precision=highest)
        departure = channel_rinv[:, None] * (evolved - innovation[sub_index].astype(jnp.float32))
        adjoint_cols = jnp.dot(channel_weight.T, channel_rinv[:, None] * departure, precision=highest)
        contribution = (weights[None] * adjoint_cols[:, None, :]).reshape(L, -1)
        term_field = jnp.zeros((L, NY * NX), jnp.float32).at[:, global_cell.reshape(-1)].add(contribution)
        adjoint_terms.append(term_field.reshape(L, NY, NX))
    gradients = [None] * NSUB
    current = jnp.zeros((L, NY, NX), jnp.float32)
    for sub_index in reversed(range(NSUB)):
        current = current + adjoint_terms[sub_index]
        for step_index in range(STEPS):
            current = adjoint_step(current, wind_x, wind_y)
        gradients[sub_index] = current
    return jnp.stack(gradients)
```

```python
import functools

import jax
import jax.numpy as jnp
from jax import lax
from jax.experimental import pallas as pl
from jax.experimental.pallas import tpu as pltpu
from jax.sharding import PartitionSpec as P

LEVELS = 8
ROWS = 8
WIDTH = 512
SUBS = 3
TILES = 64
PARTS = 4
RECORDS = 256
CORNERS = 4
HALF = 256
PIECES = WIDTH // HALF * ROWS
CHUNKS = 8
LANES = 128

f32 = jnp.float32
bf16 = jnp.bfloat16
highest = lax.Precision.HIGHEST


def struct(*shape, dtype=f32):
    return jax.ShapeDtypeStruct(shape, dtype)


def split(value):
    top = value.astype(bf16)
    return top, (value - top.astype(f32)).astype(bf16)


def forward_step(current, wind_x, wind_y, low):
    result = {}
    for row in range(low + 1, ROWS):
        here = current[row]
        left = pltpu.roll(here, 1, 1)
        result[row] = (
            here - wind_x(row) * (here - left) - wind_y(row) * (here - current[row - 1])
        )
    return result


def adjoint_step(current, wind_x, wind_y, high):
    result = {}
    for row in range(high - 1):
        here = current[row]
        along, across = wind_x(row), wind_y(row)
        result[row] = (
            here * (1.0 - along - across)
            + pltpu.roll(along * here, WIDTH - 1, 1)
            + wind_y(row + 1) * current[row + 1]
        )
    return result


def forward_steps(current, winds, low, count):
    for _ in range(count):
        current = forward_step(current, winds[0], winds[1], low)
        low += 1
    return current, low


def adjoint_steps(current, winds, high, count):
    for _ in range(count):
        current = adjoint_step(current, winds[0], winds[1], high)
        high -= 1
    return current, high


WINDS = 2
FIELDS = WINDS + SUBS
DOWN_EDGE = 3
UP_EDGE = 4
EXTRA = 4


def lower_reader(own, below, edge, field):
    def read(row):
        if row >= 0:
            return own[field * ROWS + row]
        if row >= -ROWS:
            return below[field * ROWS + row + ROWS]
        return edge[field * DOWN_EDGE + row + ROWS + DOWN_EDGE]

    return read


def upper_reader(own, above, edge, field):
    def read(row):
        if row < ROWS:
            return own[field * ROWS + row]
        if row < 2 * ROWS:
            return above[field * ROWS + row - ROWS]
        return edge[field * UP_EDGE + row - 2 * ROWS]

    return read


def lower_fields(fields, below, edge):
    readers = [lower_reader(fields, below, edge, field) for field in range(FIELDS)]
    return readers[:WINDS], readers[WINDS:]


def upper_winds(fields, above, edge):
    return [upper_reader(fields, above, edge, field) for field in range(WINDS)]


def add_rows(current, other, low, high):
    return {row: current[row] + other(row) for row in range(low, high)}


def rows_kernel(forcing, courant, fields, winds, down_edge, up_edge):
    for field in range(FIELDS):
        source = courant[field] if field < WINDS else forcing[field - WINDS]
        turned = jnp.swapaxes(source, 0, 1)
        fields[pl.ds(field * ROWS, ROWS)] = turned
        if field < WINDS:
            winds[pl.ds(field * ROWS, ROWS)] = turned
            up_edge[pl.ds(field * UP_EDGE, UP_EDGE)] = turned[:UP_EDGE]
        if field <= WINDS:
            down_edge[pl.ds(field * DOWN_EDGE, DOWN_EDGE)] = turned[ROWS - DOWN_EDGE :]


def pack_kernel(innovation, cells, weight, owner, channel_weight, rinv, send, mixing):
    sub_id = lax.broadcasted_iota(jnp.int32, (RECORDS, RECORDS), 0)
    lane_id = lax.broadcasted_iota(jnp.int32, (RECORDS, RECORDS), 1)
    same_place = sub_id == lane_id
    not_later = lane_id <= sub_id

    eye = (
        lax.broadcasted_iota(jnp.int32, (LEVELS, LEVELS), 0)
        == lax.broadcasted_iota(jnp.int32, (LEVELS, LEVELS), 1)
    ).astype(f32)
    turned = lax.dot_general(
        eye, channel_weight[...], (((1,), (1,)), ((), ())),
        precision=highest, preferred_element_type=f32,
    )
    scaled = turned * (rinv[...] * rinv[...])
    matrix = jnp.dot(scaled, channel_weight[...], precision=highest, preferred_element_type=f32)
    for level in range(LEVELS):
        mixing[level] = jnp.broadcast_to(matrix[:, level : level + 1], (LEVELS, LANES))
    top = scaled.astype(bf16)
    rest = scaled - top.astype(f32)
    middle = rest.astype(bf16)
    low = (rest - middle.astype(f32)).astype(bf16)

    spread_row = lax.broadcasted_iota(jnp.int32, (2 * LEVELS, LANES), 0)
    spread_lane = lax.broadcasted_iota(jnp.int32, (2 * LEVELS, LANES), 1)
    repeat = (
        (spread_lane // 64 == spread_row // LEVELS) & (spread_lane % LEVELS == spread_row % LEVELS)
    ).astype(f32)
    slot_lane = lax.broadcasted_iota(jnp.int32, (RECORDS, LANES), 1)
    slot_rank = ((slot_lane % 64) // LEVELS) * 2
    tile_id = lax.broadcasted_iota(jnp.int32, (TILES, RECORDS), 0)
    ones = jnp.ones((RECORDS, LANES), bf16)
    for sub in range(SUBS):
        data = innovation[sub]
        projected = (
            jnp.dot(top, data, preferred_element_type=f32)
            + jnp.dot(middle, data, preferred_element_type=f32)
            + jnp.dot(low, data, preferred_element_type=f32)
        )
        payload = jnp.concatenate(
            [cells[sub].astype(f32), weight[sub].astype(f32), projected], axis=0
        )
        owner_column = jnp.broadcast_to(owner[sub], (RECORDS, RECORDS))
        owner_row = jnp.sum(jnp.where(same_place, owner_column, 0), axis=0, keepdims=True)
        earlier = jnp.where((owner_column == owner_row) & not_later, 1.0, 0.0).astype(bf16)
        rank = jnp.dot(earlier, ones, preferred_element_type=f32).astype(jnp.int32) - 1
        repeated = lax.dot_general(
            payload, repeat, (((0,), (0,)), ((), ())),
            precision=highest, preferred_element_type=f32,
        )
        target = (tile_id == owner_row).astype(f32)
        for half in range(2):
            chosen = jnp.where(rank == slot_rank + half, repeated, 0.0)
            send[pl.ds(2 * sub + half, TILES, stride=8), :] = jnp.dot(
                target, chosen, precision=highest, preferred_element_type=f32
            )
    for spare in range(2 * SUBS, 8):
        send[pl.ds(spare, TILES, stride=8), :] = jnp.zeros((TILES, LANES), f32)


def observe(received, mixing, states, slots, pieces, total):
    rows_id = lax.broadcasted_iota(jnp.int32, (HALF, LANES), 0)

    def one_sub(sub, _):
        for half in range(2):
            pieces[pl.ds(half * TILES, TILES), :] = received[
                pl.ds(2 * sub + half, TILES, stride=8), :
            ]
        slots[...] = pieces[...].T
        top, low = split(states[sub])
        left = jnp.concatenate([top, low], axis=0)
        total[...] = jnp.zeros_like(total)

        def one_chunk(chunk, _):
            place = pl.multiple_of(chunk * LEVELS, LEVELS)
            record = slots[pl.ds(place, LEVELS), :]
            projected = slots[pl.ds(TILES + place, LEVELS), :]
            cell = record.astype(jnp.int32)
            piece = cell // HALF
            column = cell - piece * HALF
            stencil = jnp.concatenate(
                [
                    jnp.where(
                        rows_id == column[corner : corner + 1],
                        record[CORNERS + corner : CORNERS + corner + 1],
                        0.0,
                    ).astype(bf16)
                    for corner in range(CORNERS)
                ],
                axis=1,
            )
            found = jnp.dot(left, stencil, preferred_element_type=f32)
            values = jnp.zeros((LEVELS, LANES), f32)
            marks = []
            for corner in range(CORNERS):
                wanted = jnp.broadcast_to(piece[corner : corner + 1], (LEVELS, LANES))
                part = slice(corner * LANES, (corner + 1) * LANES)
                for number in range(PIECES):
                    hit = wanted == number
                    marks.append(hit)
                    high = number * LEVELS
                    lowest = (PIECES + number) * LEVELS
                    both = found[high : high + LEVELS, part] + found[lowest : lowest + LEVELS, part]
                    values = values + jnp.where(hit, both, 0.0)
            adjoint = -projected
            for level in range(LEVELS):
                adjoint = adjoint + mixing[level] * values[level : level + 1]
            first, second = split(adjoint)
            first, second = first.astype(f32), second.astype(f32)
            spread = jnp.concatenate(
                [
                    jnp.concatenate(
                        [
                            jnp.where(marks[corner * PIECES + number], source, 0.0)
                            for source in (first, second)
                            for number in range(PIECES)
                        ],
                        axis=0,
                    ).astype(bf16)
                    for corner in range(CORNERS)
                ],
                axis=1,
            )
            total[...] += lax.dot_general(
                spread, stencil, (((1,), (1,)), ((), ())), preferred_element_type=f32
            )
            return 0

        lax.fori_loop(0, CHUNKS, one_chunk, 0)
        size = PIECES * LEVELS
        states[sub] = total[pl.ds(0, size), :] + total[pl.ds(size, size), :]
        return 0

    lax.fori_loop(0, SUBS, one_sub, 0)


def forward_local_kernel(fields, below, edge, own, extended):
    winds, forces = lower_fields(fields, below, edge)
    low = -(ROWS + 2)
    current = {row: forces[0](row) for row in range(low, ROWS)}
    current, low = forward_steps(current, winds, low, 2)
    for sub in range(1, SUBS):
        current = add_rows(current, forces[sub], low, ROWS)
        current, low = forward_steps(current, winds, low, 2)
    for row in range(ROWS):
        own[row] = current[row]
    for row in range(-EXTRA, ROWS):
        extended[row + EXTRA] = current[row]


def lower_state(own, extended, low):
    return {row: own[row] if row >= 0 else extended[row + ROWS + EXTRA] for row in range(low, ROWS)}


def forward_pair_kernel(
    fields, below, edge, mine, before_own, before_extended, own, extended
):
    winds, _ = lower_fields(fields, below, edge)
    low = -(ROWS + 2)
    current, low = forward_steps(lower_state(before_own, before_extended, low), winds, low, 6)
    for row in range(-EXTRA, ROWS):
        value = current[row] + mine[row + EXTRA]
        extended[row + EXTRA] = value
        if row >= 0:
            own[row] = value


def forward_final_kernel(
    fields, below, edge,
    before_own, before_extended, pair_own, pair_extended, received, mixing,
    result, result_edge,
    states, slots, pieces, total,
):
    winds, forces = lower_fields(fields, below, edge)
    low = -(ROWS + EXTRA)
    current, low = forward_steps(lower_state(pair_own, pair_extended, low), winds, low, 6)
    before = lower_state(before_own, before_extended, low)
    current = {row: current[row] + before[row] for row in current}
    for sub in range(SUBS):
        current = add_rows(current, forces[sub], low, ROWS)
        current, low = forward_steps(current, winds, low, 2)
        for row in range(ROWS):
            for half in range(2):
                place = (2 * row + half) * LEVELS
                states[sub, place : place + LEVELS, :] = current[row][
                    :, half * HALF : (half + 1) * HALF
                ]
    observe(received, mixing, states, slots, pieces, total)
    for sub in range(SUBS):
        for row in range(ROWS):
            for half in range(2):
                place = (2 * row + half) * LEVELS
                value = states[sub, place : place + LEVELS, :]
                result[sub, row, :, half * HALF : (half + 1) * HALF] = value
                if sub == SUBS - 1 and row < 2:
                    result_edge[row, :, half * HALF : (half + 1) * HALF] = value


def source_reader(own, above, edge, sub):
    def read(row):
        if row < ROWS:
            return own[sub, row]
        if row < 2 * ROWS:
            return above[sub, row - ROWS]
        return edge[row - 2 * ROWS]

    return read


def adjoint_local_kernel(
    source, source_above, source_edge, fields, above, edge, own, extended
):
    winds = upper_winds(fields, above, edge)
    high = 2 * ROWS + 2
    sources = [source_reader(source, source_above, source_edge, sub) for sub in range(SUBS)]
    current = {row: sources[SUBS - 1](row) for row in range(high)}
    current, high = adjoint_steps(current, winds, high, 2)
    for sub in reversed(range(SUBS - 1)):
        current = add_rows(current, sources[sub], 0, high)
        current, high = adjoint_steps(current, winds, high, 2)
    for row in range(ROWS):
        own[row] = current[row]
    for row in range(ROWS + EXTRA):
        extended[row] = current[row]


def upper_state(own, extended, high):
    return {row: own[row] if row < ROWS else extended[row - ROWS] for row in range(high)}


def adjoint_pair_kernel(
    fields, above, edge, mine, after_own, after_extended, own, extended
):
    winds = upper_winds(fields, above, edge)
    high = 2 * ROWS + 2
    current, high = adjoint_steps(upper_state(after_own, after_extended, high), winds, high, 6)
    for row in range(ROWS + EXTRA):
        value = current[row] + mine[row]
        extended[row] = value
        if row < ROWS:
            own[row] = value


def adjoint_final_kernel(
    source, source_above, fields, above, edge,
    after_own, after_extended, pair_own, pair_extended, gradient,
):
    winds = upper_winds(fields, above, edge)
    high = 2 * ROWS + EXTRA
    current, high = adjoint_steps(upper_state(pair_own, pair_extended, high), winds, high, 6)
    after = upper_state(after_own, after_extended, high)
    current = {row: current[row] + after[row] for row in current}
    for sub in reversed(range(SUBS)):
        current = add_rows(current, source_reader(source, source_above, None, sub), 0, high)
        current, high = adjoint_steps(current, winds, high, 2)
        gradient[sub] = jnp.swapaxes(jnp.stack([current[row] for row in range(ROWS)]), 0, 1)


def run(kernel, outputs, arguments, scratch=(), name=None, flops=2_000_000):
    moved = sum(a.size * a.dtype.itemsize for a in arguments)
    return pl.pallas_call(
        kernel,
        out_shape=outputs,
        scratch_shapes=scratch,
        compiler_params=pltpu.CompilerParams(vmem_limit_bytes=40 * 1024 * 1024),
        cost_estimate=pl.CostEstimate(flops=flops, bytes_accessed=moved, transcendentals=0),
        name=name,
    )(*arguments)


def moved(array, parts, tiles):
    pairs = []
    for part in range(PARTS):
        for tile in range(TILES):
            to_part, to_tile = part + parts, tile + tiles
            if 0 <= to_part < PARTS and 0 <= to_tile < TILES:
                pairs.append((part * TILES + tile, to_part * TILES + to_tile))
    return lax.ppermute(array, ("tm", "space"), pairs)


def shards(
    forcing, courant, innovation, obs_cells, obs_weight, obs_owner, channel_weight, channel_rinv
):
    fields, winds, down_edge, up_edge = run(
        rows_kernel,
        (
            struct(FIELDS * ROWS, LEVELS, WIDTH),
            struct(WINDS * ROWS, LEVELS, WIDTH),
            struct((WINDS + 1) * DOWN_EDGE, LEVELS, WIDTH),
            struct(WINDS * UP_EDGE, LEVELS, WIDTH),
        ),
        (forcing, courant),
        name="rows",
    )
    below = moved(fields, 0, 1)
    above = moved(winds, 0, -1)
    down_edge = moved(down_edge, 0, 2)
    up_edge = moved(up_edge, 0, -2)
    send, mixing = run(
        pack_kernel,
        (struct(TILES * 8, LANES), struct(LEVELS, LEVELS, LANES)),
        (
            innovation, obs_cells, obs_weight, obs_owner, channel_weight,
            channel_rinv.reshape(1, -1),
        ),
        name="pack",
    )
    received = lax.all_to_all(
        send.reshape(TILES, 8, LANES), "space", split_axis=0, concat_axis=0, tiled=True
    ).reshape(TILES * 8, LANES)

    pair_shapes = (struct(ROWS, LEVELS, WIDTH), struct(ROWS + EXTRA, LEVELS, WIDTH))
    own, extended = run(
        forward_local_kernel,
        pair_shapes,
        (fields, below, down_edge),
        name="forward_local",
    )
    before = (moved(own, 1, 0), moved(extended, 1, 1))
    own, extended = run(
        forward_pair_kernel,
        pair_shapes,
        (fields, below, down_edge, extended, *before),
        name="forward_pair",
    )
    pair = (moved(own, 2, 0), moved(extended, 2, 1))
    size = PIECES * LEVELS
    source, source_edge = run(
        forward_final_kernel,
        (struct(SUBS, ROWS, LEVELS, WIDTH), struct(2, LEVELS, WIDTH)),
        (
            fields, below, down_edge, *before, *pair, received, mixing,
        ),
        scratch=(
            pltpu.VMEM((SUBS, size, HALF), f32),
            pltpu.VMEM((LANES, LANES), f32),
            pltpu.VMEM((LANES, LANES), f32),
            pltpu.VMEM((2 * size, HALF), f32),
        ),
        name="forward_final",
    )

    source_above = moved(source, 0, -1)
    source_edge = moved(source_edge, 0, -2)
    own, extended = run(
        adjoint_local_kernel,
        pair_shapes,
        (source, source_above, source_edge, fields, above, up_edge),
        name="adjoint_local",
    )
    after = (moved(own, -1, 0), moved(extended, -1, -1))
    own, extended = run(
        adjoint_pair_kernel,
        pair_shapes,
        (fields, above, up_edge, extended, *after),
        name="adjoint_pair",
    )
    pair = (moved(own, -2, 0), moved(extended, -2, -1))
    gradient = run(
        adjoint_final_kernel,
        struct(SUBS, LEVELS, ROWS, WIDTH),
        (source, source_above, fields, above, up_edge, *after, *pair),
        name="adjoint_final",
    )
    return gradient


def solution(mesh):
    return jax.shard_map(
        shards,
        mesh=mesh,
        in_specs=(
            P("tm", None, "space", None),
            P(None, None, "space", None),
            P("tm", None, "space"),
            P("tm", None, "space"),
            P("tm", None, "space"),
            P("tm", "space", None),
            P(),
            P(),
        ),
        out_specs=P("tm", None, "space", None),
        check_vma=False,
    )
```

```python
import functools

import jax
import jax.numpy as jnp
from jax import lax
from jax.experimental import pallas as pl
from jax.experimental.pallas import tpu as pltpu
from jax.sharding import PartitionSpec as P

LEVELS = 8
ROWS = 8
WIDTH = 512
SUBS = 3
TILES = 64
PARTS = 4
RECORDS = 256
CORNERS = 4
HALF = 256
PIECES = WIDTH // HALF * ROWS
CHUNKS = 8
LANES = 128

f32 = jnp.float32
bf16 = jnp.bfloat16
highest = lax.Precision.HIGHEST


def struct(*shape, dtype=f32):
    return jax.ShapeDtypeStruct(shape, dtype)


def split(value):
    top = value.astype(bf16)
    return top, (value - top.astype(f32)).astype(bf16)


LEVEL_TOP = 32766.0
SCALE_BITS = 22
SCALE_BIAS = 256
WIND_MIDDLE = 0.25
WIND_REACH = 0.21


def nearest(value):
    return jnp.floor(value + 0.5).astype(jnp.int32)


def join(first, second):
    return jnp.left_shift(first, 16) | (second & 0xFFFF)


def parted(both):
    return jnp.right_shift(both, 16), jnp.right_shift(jnp.left_shift(both, 16), 16)


def scale_of(code):
    exponent = (jnp.right_shift(code, SCALE_BITS) - SCALE_BIAS).astype(f32)
    mantissa = (code & ((1 << SCALE_BITS) - 1)).astype(f32) * (0.5 ** 20)
    return mantissa * jnp.exp2(exponent)


def encode(values, message):
    count = len(values)
    lane = lax.broadcasted_iota(jnp.int32, (LEVELS, LANES), 1)
    largest = jnp.full((LEVELS, LANES), 1e-30, f32)
    for number, value in enumerate(values):
        top = jnp.max(jnp.abs(value), axis=1, keepdims=True)
        largest = jnp.where(lane == number, jnp.maximum(top, 1e-30), largest)
    exponent = jnp.floor(jnp.log2(largest))
    mantissa = (largest * jnp.exp2(-exponent) * 2.0 ** 20).astype(jnp.int32) + 16
    code = jnp.left_shift(exponent.astype(jnp.int32) + SCALE_BIAS, SCALE_BITS) + mantissa
    factor = LEVEL_TOP / scale_of(code)
    half = count // 2
    whole = [nearest(value * factor[:, n : n + 1]) for n, value in enumerate(values)]
    for number in range(half):
        message[number] = join(whole[number], whole[number + half])
    message[half] = jnp.concatenate([code] * (WIDTH // LANES), axis=1)


def decode(message, count):
    half = count // 2
    factor = scale_of(message[half][:, :LANES]) * (1.0 / LEVEL_TOP)
    values = [None] * count
    for number in range(half):
        pair = parted(message[number])
        for place, value in zip((number, number + half), pair):
            values[place] = value.astype(f32) * factor[:, place : place + 1]
    return values


def encode_wind(first, second):
    steps = LEVEL_TOP / WIND_REACH
    return join(nearest((first - WIND_MIDDLE) * steps), nearest((second - WIND_MIDDLE) * steps))


def decode_wind(both):
    step = WIND_REACH / LEVEL_TOP
    return [value.astype(f32) * step + WIND_MIDDLE for value in parted(both)]


def forward_step(current, wind_x, wind_y, low):
    result = {}
    for row in range(low + 1, ROWS):
        here = current[row]
        left = pltpu.roll(here, 1, 1)
        result[row] = (
            here - wind_x(row) * (here - left) - wind_y(row) * (here - current[row - 1])
        )
    return result


def adjoint_step(current, wind_x, wind_y, high):
    result = {}
    for row in range(high - 1):
        here = current[row]
        along, across = wind_x(row), wind_y(row)
        result[row] = (
            here * (1.0 - along - across)
            + pltpu.roll(along * here, WIDTH - 1, 1)
            + wind_y(row + 1) * current[row + 1]
        )
    return result


def forward_steps(current, winds, low, count):
    for _ in range(count):
        current = forward_step(current, winds[0], winds[1], low)
        low += 1
    return current, low


def adjoint_steps(current, winds, high, count):
    for _ in range(count):
        current = adjoint_step(current, winds[0], winds[1], high)
        high -= 1
    return current, high


WINDS = 2
FIELDS = WINDS + SUBS
DOWN_EDGE = 3
UP_EDGE = 4
EXTRA = 4
OWN_MESSAGE = ROWS // 2 + 1
EXTENDED_MESSAGE = (ROWS + EXTRA) // 2 + 1
FORCE_MESSAGE = SUBS * ROWS // 2 + 1


def lower_winds(winds, winds_below, edge):
    def reader(field):
        def read(row):
            if row >= 0:
                return winds[field * ROWS + row]
            if row >= -ROWS:
                return winds_below[field * ROWS + row + ROWS]
            return edge[field * DOWN_EDGE + row + ROWS + DOWN_EDGE]

        return read

    return [reader(field) for field in range(WINDS)]


def upper_winds(winds, winds_above, edge):
    def reader(field):
        def read(row):
            if row < ROWS:
                return winds[field * ROWS + row]
            if row < 2 * ROWS:
                return winds_above[field * ROWS + row - ROWS]
            return edge[field * UP_EDGE + row - 2 * ROWS]

        return read

    return [reader(field) for field in range(WINDS)]


def lower_forces(forces, forces_below):
    def reader(sub):
        def read(row):
            if row >= 0:
                return forces[sub * ROWS + row]
            return forces_below[sub * ROWS + row + ROWS]

        return read

    return [reader(sub) for sub in range(SUBS)]


def add_rows(current, other, low, high):
    return {row: current[row] + other(row) for row in range(low, high)}


def fetch(pairs, sems):
    copies = [
        pltpu.make_async_copy(source, target, sems.at[number])
        for number, (source, target) in enumerate(pairs)
    ]
    for copy in copies:
        copy.start()
    return copies


def rows_kernel(
    forcing_far, courant_far, winds, forces, below, down_edge, forcing, courant, sems
):
    copies = fetch(
        [(courant_far.at[field], courant.at[field]) for field in range(WINDS)]
        + [(forcing_far.at[sub], forcing.at[sub]) for sub in range(SUBS)],
        sems,
    )
    for copy in copies[:WINDS]:
        copy.wait()
    for field in range(WINDS):
        winds[pl.ds(field * ROWS, ROWS)] = jnp.swapaxes(courant[field], 0, 1)
    encode_winds(winds, range(ROWS), below, 0)
    encode_winds(winds, range(ROWS - DOWN_EDGE, ROWS), down_edge, 0)
    rows = []
    for sub in range(SUBS):
        copies[WINDS + sub].wait()
        turned = jnp.swapaxes(forcing[sub], 0, 1)
        forces[pl.ds(sub * ROWS, ROWS)] = turned
        rows += [turned[row] for row in range(ROWS)]
    encode(rows, below.at[pl.ds(ROWS, FORCE_MESSAGE)])
    encode(rows[ROWS - 2 : ROWS], down_edge.at[pl.ds(DOWN_EDGE, 2)])


def encode_winds(winds, rows, message, start):
    for number, row in enumerate(rows):
        message[start + number] = encode_wind(winds[row], winds[ROWS + row])


def unpack_winds(message, rows, result, start=0):
    for row in range(rows):
        first, second = decode_wind(message[start + row])
        result[row] = first
        result[rows + row] = second


def choose_kernel(
    innovation_far, cells_far, weight_far, owner_far, channel_far, rinv_far,
    chosen, target, mixing,
    innovation, cells, weight, owner, channel_weight, rinv, sems,
):
    copies = fetch(
        [
            (channel_far, channel_weight), (rinv_far, rinv), (owner_far, owner),
            (cells_far, cells), (weight_far, weight),
        ]
        + [(innovation_far.at[sub], innovation.at[sub]) for sub in range(SUBS)],
        sems,
    )
    for copy in copies:
        copy.wait()
    sub_id = lax.broadcasted_iota(jnp.int32, (RECORDS, RECORDS), 0)
    lane_id = lax.broadcasted_iota(jnp.int32, (RECORDS, RECORDS), 1)
    not_later = lane_id <= sub_id

    scaled = channel_weight[...] * (rinv[...] * rinv[...])
    matrix = lax.dot_general(
        scaled, channel_weight[...], (((1,), (1,)), ((), ())),
        precision=highest, preferred_element_type=f32,
    )
    for level in range(LEVELS):
        mixing[level] = jnp.broadcast_to(matrix[:, level : level + 1], (LEVELS, LANES))
    top = scaled.astype(bf16)
    rest = scaled - top.astype(f32)
    middle = rest.astype(bf16)
    low = (rest - middle.astype(f32)).astype(bf16)

    spread_row = lax.broadcasted_iota(jnp.int32, (2 * LEVELS, LANES), 0)
    spread_lane = lax.broadcasted_iota(jnp.int32, (2 * LEVELS, LANES), 1)
    repeat = (
        (spread_lane // 64 == spread_row // LEVELS) & (spread_lane % LEVELS == spread_row % LEVELS)
    ).astype(f32)
    slot_lane = lax.broadcasted_iota(jnp.int32, (RECORDS, LANES), 1)
    slot_rank = ((slot_lane % 64) // LEVELS) * 2
    tile_id = lax.broadcasted_iota(jnp.int32, (TILES, RECORDS), 0)
    ones = jnp.ones((RECORDS, LANES), bf16)
    for sub in range(SUBS):
        data = innovation[sub]
        projected = (
            jnp.dot(top, data, preferred_element_type=f32)
            + jnp.dot(middle, data, preferred_element_type=f32)
            + jnp.dot(low, data, preferred_element_type=f32)
        )
        payload = jnp.concatenate(
            [cells[sub].astype(f32), weight[sub].astype(f32), projected], axis=0
        )
        owner_row = owner[sub]
        owner_rows = jnp.broadcast_to(owner_row, (RECORDS, RECORDS))
        earlier = jnp.where((owner_rows.T == owner_rows) & not_later, 1.0, 0.0).astype(bf16)
        rank = jnp.dot(earlier, ones, preferred_element_type=f32).astype(jnp.int32) - 1
        repeated = lax.dot_general(
            payload, repeat, (((0,), (0,)), ((), ())),
            precision=highest, preferred_element_type=f32,
        )
        target[sub] = (tile_id == owner_row).astype(f32)
        for half in range(2):
            chosen[2 * sub + half] = jnp.where(rank == slot_rank + half, repeated, 0.0)


def place_kernel(chosen, target, after, send):
    del after
    for sub in range(SUBS):
        for half in range(2):
            send[pl.ds(2 * sub + half, TILES, stride=8), :] = jnp.dot(
                target[sub], chosen[2 * sub + half],
                precision=highest, preferred_element_type=f32,
            )
    for spare in range(2 * SUBS, 8):
        send[pl.ds(spare, TILES, stride=8), :] = jnp.zeros((TILES, LANES), f32)


def stencil_kernel(received, slots, stencil, pieces):
    rows_id = lax.broadcasted_iota(jnp.int32, (HALF, LANES), 0)

    def one_sub(sub, _):
        for half in range(2):
            pieces[pl.ds(half * TILES, TILES), :] = received[
                pl.ds(2 * sub + half, TILES, stride=8), :
            ]
        slots[sub] = pieces[...].T
        for chunk in range(CHUNKS):
            record = slots[sub, pl.ds(chunk * LEVELS, LEVELS), :]
            column = record.astype(jnp.int32) & (HALF - 1)
            for corner in range(CORNERS):
                stencil[sub, chunk, :, corner * LANES : (corner + 1) * LANES] = jnp.where(
                    rows_id == column[corner : corner + 1],
                    record[CORNERS + corner : CORNERS + corner + 1],
                    0.0,
                ).astype(bf16)
        return 0

    lax.fori_loop(0, SUBS, one_sub, 0)


def observe(slots, stencil, mixing, states, found, spread):
    size = PIECES * LEVELS

    def one_sub(sub, _):
        top, low = split(states[sub])
        left = jnp.concatenate([top, low], axis=0)
        for chunk in range(CHUNKS):
            found[chunk] = jnp.dot(left, stencil[sub, chunk], preferred_element_type=f32)
        for chunk in range(CHUNKS):
            record = slots[sub, pl.ds(chunk * LEVELS, LEVELS), :]
            adjoint = -slots[sub, pl.ds(TILES + chunk * LEVELS, LEVELS), :]
            piece = jnp.right_shift(record.astype(jnp.int32), 8)
            sums = []
            wanted = []
            for corner in range(CORNERS):
                wanted.append(jnp.broadcast_to(piece[corner : corner + 1], (LEVELS, LANES)))
                part = pl.ds(corner * LANES, LANES)
                value = None
                for number in range(PIECES):
                    both = (
                        found[chunk, pl.ds(number * LEVELS, LEVELS), part]
                        + found[chunk, pl.ds(size + number * LEVELS, LEVELS), part]
                    )
                    value = both if value is None else jnp.where(wanted[corner] == number, both, value)
                sums.append(value)
            values = (sums[0] + sums[1]) + (sums[2] + sums[3])
            for level in range(LEVELS):
                adjoint = adjoint + mixing[level] * values[level : level + 1]
            first, second = split(adjoint)
            sources = first.astype(f32), second.astype(f32)
            for corner in range(CORNERS):
                part = pl.ds(corner * LANES, LANES)
                for place, source in enumerate(sources):
                    spread[chunk, pl.ds(place * size, size), part] = jnp.concatenate(
                        [jnp.where(wanted[corner] == number, source, 0.0) for number in range(PIECES)],
                        axis=0,
                    ).astype(bf16)
        total = jnp.zeros((2 * size, HALF), f32)
        for chunk in range(CHUNKS):
            total = total + lax.dot_general(
                spread[chunk], stencil[sub, chunk], (((1,), (1,)), ((), ())),
                preferred_element_type=f32,
            )
        states[sub] = total[:size] + total[size:]
        return 0

    lax.fori_loop(0, SUBS, one_sub, 0)


def forward_local_kernel(
    winds, forces, below, down_edge,
    own, extended, mine, winds_below, lower_edge, forces_below,
):
    unpack_winds(below, ROWS, winds_below)
    unpack_winds(down_edge, DOWN_EDGE, lower_edge)
    rows = decode(below.at[pl.ds(ROWS, FORCE_MESSAGE)], SUBS * ROWS)
    for number, row in enumerate(rows):
        forces_below[number] = row
    edge = decode(down_edge.at[pl.ds(DOWN_EDGE, 2)], 2)
    across = lower_winds(winds, winds_below, lower_edge)
    forced = lower_forces(forces, forces_below)
    low = -(ROWS + 2)
    current = {row: edge[row - low] for row in (low, low + 1)}
    for row in range(-ROWS, ROWS):
        current[row] = forced[0](row)
    current, low = forward_steps(current, across, low, 2)
    for sub in range(1, SUBS):
        current = add_rows(current, forced[sub], low, ROWS)
        current, low = forward_steps(current, across, low, 2)
    listed = [current[row] for row in range(-EXTRA, ROWS)]
    for number, row in enumerate(listed):
        mine[number] = row
    encode(listed[EXTRA:], own)
    encode(listed, extended)


def lower_state(own, extended, low):
    here = decode(own, ROWS)
    under = decode(extended, ROWS + EXTRA)
    return {row: here[row] if row >= 0 else under[row + ROWS + EXTRA] for row in range(low, ROWS)}


def forward_pair_kernel(
    winds, winds_below, lower_edge, mine, before_own, before_extended, own, extended
):
    across = lower_winds(winds, winds_below, lower_edge)
    low = -(ROWS + 2)
    current, low = forward_steps(lower_state(before_own, before_extended, low), across, low, 6)
    listed = [current[row] + mine[row + EXTRA] for row in range(-EXTRA, ROWS)]
    encode(listed[EXTRA:], own)
    encode(listed, extended)


def forward_final_kernel(
    winds, forces, winds_below, lower_edge, forces_below,
    before_own, before_extended, pair_own, pair_extended, slots, stencil, mixing,
    result, result_above, result_edge,
    states, found, spread,
):
    across = lower_winds(winds, winds_below, lower_edge)
    forced = lower_forces(forces, forces_below)
    low = -(ROWS + EXTRA)
    current, low = forward_steps(lower_state(pair_own, pair_extended, low), across, low, 6)
    before = lower_state(before_own, before_extended, low)
    current = {row: current[row] + before[row] for row in current}
    for sub in range(SUBS):
        current = add_rows(current, forced[sub], low, ROWS)
        current, low = forward_steps(current, across, low, 2)
        for row in range(ROWS):
            for half in range(2):
                place = (2 * row + half) * LEVELS
                states[sub, place : place + LEVELS, :] = current[row][
                    :, half * HALF : (half + 1) * HALF
                ]
    observe(slots, stencil, mixing, states, found, spread)
    listed = []
    for sub in range(SUBS):
        for row in range(ROWS):
            places = [(2 * row + half) * LEVELS for half in range(2)]
            value = jnp.concatenate(
                [states[sub, place : place + LEVELS, :] for place in places], axis=1
            )
            result[sub, row] = value
            listed.append(value)
    encode(listed, result_above.at[pl.ds(0, FORCE_MESSAGE)])
    encode_winds(winds, range(ROWS), result_above, FORCE_MESSAGE)
    encode(listed[-ROWS : 2 - ROWS], result_edge.at[pl.ds(0, 2)])
    encode_winds(winds, range(UP_EDGE), result_edge, 2)


def adjoint_local_kernel(
    source, source_above, source_edge, winds,
    own, extended, mine, unpacked, winds_above, upper_edge,
):
    unpack_winds(source_above, ROWS, winds_above, FORCE_MESSAGE)
    unpack_winds(source_edge, UP_EDGE, upper_edge, 2)
    across = upper_winds(winds, winds_above, upper_edge)
    high = 2 * ROWS + 2
    above = decode(source_above.at[pl.ds(0, FORCE_MESSAGE)], SUBS * ROWS)
    edge = decode(source_edge.at[pl.ds(0, 2)], 2)
    for number, row in enumerate(above):
        unpacked[number] = row

    def source_row(sub):
        return lambda row: source[sub, row] if row < ROWS else unpacked[sub * ROWS + row - ROWS]

    current = {row: source_row(SUBS - 1)(row) for row in range(2 * ROWS)}
    for number, row in enumerate(edge):
        current[2 * ROWS + number] = row
    current, high = adjoint_steps(current, across, high, 2)
    for sub in reversed(range(SUBS - 1)):
        current = add_rows(current, source_row(sub), 0, high)
        current, high = adjoint_steps(current, across, high, 2)
    listed = [current[row] for row in range(ROWS + EXTRA)]
    for number, row in enumerate(listed):
        mine[number] = row
    encode(listed[:ROWS], own)
    encode(listed, extended)


def upper_state(own, extended, high):
    here = decode(own, ROWS)
    over = decode(extended, ROWS + EXTRA)
    return {row: here[row] if row < ROWS else over[row - ROWS] for row in range(high)}


def adjoint_pair_kernel(
    winds, winds_above, upper_edge, mine, after_own, after_extended, own, extended
):
    across = upper_winds(winds, winds_above, upper_edge)
    high = 2 * ROWS + 2
    current, high = adjoint_steps(upper_state(after_own, after_extended, high), across, high, 6)
    listed = [current[row] + mine[row] for row in range(ROWS + EXTRA)]
    encode(listed[:ROWS], own)
    encode(listed, extended)


def adjoint_final_kernel(
    source, unpacked, winds, winds_above, upper_edge,
    after_own, after_extended, pair_own, pair_extended, gradient,
):
    across = upper_winds(winds, winds_above, upper_edge)
    high = 2 * ROWS + EXTRA
    current, high = adjoint_steps(upper_state(pair_own, pair_extended, high), across, high, 6)
    after = upper_state(after_own, after_extended, high)
    current = {row: current[row] + after[row] for row in current}

    def source_row(sub):
        return lambda row: source[sub, row] if row < ROWS else unpacked[sub * ROWS + row - ROWS]

    for sub in reversed(range(SUBS)):
        current = add_rows(current, source_row(sub), 0, high)
        current, high = adjoint_steps(current, across, high, 2)
        gradient[sub] = jnp.swapaxes(jnp.stack([current[row] for row in range(ROWS)]), 0, 1)


def run(kernel, outputs, arguments, scratch=(), name=None, flops=2_000_000, far=False):
    size = sum(a.size * a.dtype.itemsize for a in arguments)
    place = pltpu.HBM if far else pltpu.VMEM
    if far:
        arguments = [pltpu.with_memory_space_constraint(a, pltpu.HBM) for a in arguments]
    return pl.pallas_call(
        kernel,
        out_shape=outputs,
        in_specs=[pl.BlockSpec(memory_space=place)] * len(arguments),
        scratch_shapes=scratch,
        compiler_params=pltpu.CompilerParams(vmem_limit_bytes=40 * 1024 * 1024),
        cost_estimate=pl.CostEstimate(flops=flops, bytes_accessed=size, transcendentals=0),
        name=name,
    )(*arguments)


def moved(array, parts, tiles):
    pairs = []
    for part in range(PARTS):
        for tile in range(TILES):
            to_part, to_tile = part + parts, tile + tiles
            if 0 <= to_part < PARTS and 0 <= to_tile < TILES:
                pairs.append((part * TILES + tile, to_part * TILES + to_tile))
    return lax.ppermute(array, ("tm", "space"), pairs)


def shards(
    forcing, courant, innovation, obs_cells, obs_weight, obs_owner, channel_weight, channel_rinv
):
    message = functools.partial(struct, dtype=jnp.int32)
    winds, forces, below, down_edge = run(
        rows_kernel,
        (
            struct(WINDS * ROWS, LEVELS, WIDTH),
            struct(SUBS * ROWS, LEVELS, WIDTH),
            message(ROWS + FORCE_MESSAGE, LEVELS, WIDTH),
            message(DOWN_EDGE + 2, LEVELS, WIDTH),
        ),
        (forcing, courant),
        scratch=(
            pltpu.VMEM(forcing.shape, f32),
            pltpu.VMEM(courant.shape, f32),
            pltpu.SemaphoreType.DMA((FIELDS,)),
        ),
        name="rows",
        far=True,
    )
    below = moved(below, 0, 1)
    down_edge = moved(down_edge, 0, 2)
    records = (
        innovation, obs_cells, obs_weight, jnp.swapaxes(obs_owner, 1, 2),
        channel_weight.T, channel_rinv.reshape(1, -1),
    )
    chosen, target, mixing = run(
        choose_kernel,
        (
            struct(2 * SUBS, RECORDS, LANES),
            struct(SUBS, TILES, RECORDS),
            struct(LEVELS, LEVELS, LANES),
        ),
        records,
        scratch=(
            *[pltpu.VMEM(array.shape, array.dtype) for array in records],
            pltpu.SemaphoreType.DMA((len(records) + SUBS - 1,)),
        ),
        name="choose",
        far=True,
    )
    below, down_edge, chosen, target = lax.optimization_barrier(
        (below, down_edge, chosen, target)
    )
    pair_shapes = (
        message(OWN_MESSAGE, LEVELS, WIDTH), message(EXTENDED_MESSAGE, LEVELS, WIDTH)
    )
    own, extended, mine, winds_below, lower_edge, forces_below = run(
        forward_local_kernel,
        (
            *pair_shapes,
            struct(ROWS + EXTRA, LEVELS, WIDTH),
            struct(WINDS * ROWS, LEVELS, WIDTH),
            struct(WINDS * DOWN_EDGE, LEVELS, WIDTH),
            struct(SUBS * ROWS, LEVELS, WIDTH),
        ),
        (winds, forces, below, down_edge),
        name="forward_local",
    )
    before = (moved(own, 1, 0), moved(extended, 1, 1))
    send = run(
        place_kernel,
        struct(TILES * 8, LANES),
        (chosen, target, lower_edge),
        name="place",
    )
    received = lax.all_to_all(
        send.reshape(TILES, 8, LANES), "space", split_axis=0, concat_axis=0, tiled=True
    ).reshape(TILES * 8, LANES)
    own, extended = run(
        forward_pair_kernel,
        pair_shapes,
        (winds, winds_below, lower_edge, mine, *before),
        name="forward_pair",
    )
    pair = (moved(own, 2, 0), moved(extended, 2, 1))
    slots, stencil = run(
        stencil_kernel,
        (
            struct(SUBS, LANES, LANES),
            struct(SUBS, CHUNKS, HALF, CORNERS * LANES, dtype=bf16),
        ),
        (received,),
        scratch=(pltpu.VMEM((LANES, LANES), f32),),
        name="stencil",
    )
    size = PIECES * LEVELS
    source, source_above, source_edge = run(
        forward_final_kernel,
        (
            struct(SUBS, ROWS, LEVELS, WIDTH),
            message(FORCE_MESSAGE + ROWS, LEVELS, WIDTH),
            message(2 + UP_EDGE, LEVELS, WIDTH),
        ),
        (
            winds, forces, winds_below, lower_edge, forces_below,
            *before, *pair, slots, stencil, mixing,
        ),
        scratch=(
            pltpu.VMEM((SUBS, size, HALF), f32),
            pltpu.VMEM((CHUNKS, 2 * size, CORNERS * LANES), f32),
            pltpu.VMEM((CHUNKS, 2 * size, CORNERS * LANES), bf16),
        ),
        name="forward_final",
    )

    source_above = moved(source_above, 0, -1)
    source_edge = moved(source_edge, 0, -2)
    own, extended, mine, unpacked, winds_above, upper_edge = run(
        adjoint_local_kernel,
        (
            *pair_shapes,
            struct(ROWS + EXTRA, LEVELS, WIDTH),
            struct(SUBS * ROWS, LEVELS, WIDTH),
            struct(WINDS * ROWS, LEVELS, WIDTH),
            struct(WINDS * UP_EDGE, LEVELS, WIDTH),
        ),
        (source, source_above, source_edge, winds),
        name="adjoint_local",
    )
    after = (moved(own, -1, 0), moved(extended, -1, -1))
    own, extended = run(
        adjoint_pair_kernel,
        pair_shapes,
        (winds, winds_above, upper_edge, mine, *after),
        name="adjoint_pair",
    )
    pair = (moved(own, -2, 0), moved(extended, -2, -1))
    return run(
        adjoint_final_kernel,
        struct(SUBS, LEVELS, ROWS, WIDTH),
        (source, unpacked, winds, winds_above, upper_edge, *after, *pair),
        name="adjoint_final",
    )


def solution(mesh):
    return jax.shard_map(
        shards,
        mesh=mesh,
        in_specs=(
            P("tm", None, "space", None),
            P(None, None, "space", None),
            P("tm", None, "space"),
            P("tm", None, "space"),
            P("tm", None, "space"),
            P("tm", "space", None),
            P(),
            P(),
        ),
        out_specs=P("tm", None, "space", None),
        check_vma=False,
    )
```

```python
import jax
import jax.numpy as jnp
from jax import lax
from jax.experimental import pallas as pl
from jax.experimental.pallas import tpu as pltpu
from jax.sharding import PartitionSpec as P

LEVELS = 8
ROWS = 8
WIDTH = 512
SUBS = 3
TILES = 64
PARTS = 4
RECORDS = 256
CORNERS = 4
HALF = 256
PIECES = WIDTH // HALF * ROWS
CHUNKS = 8
LANES = 128

f32 = jnp.float32
bf16 = jnp.bfloat16
highest = lax.Precision.HIGHEST


def struct(*shape, dtype=f32):
    return jax.ShapeDtypeStruct(shape, dtype)


def split(value):
    top = value.astype(bf16)
    return top, (value - top.astype(f32)).astype(bf16)


LEVEL_TOP = 32766.0
SCALE_BITS = 22
SCALE_BIAS = 256
WIND_MIDDLE = 0.25
WIND_REACH = 0.21


def nearest(value):
    return jnp.floor(value + 0.5).astype(jnp.int32)


def join(first, second):
    return jnp.left_shift(first, 16) | (second & 0xFFFF)


def parted(both):
    return jnp.right_shift(both, 16), jnp.right_shift(jnp.left_shift(both, 16), 16)


def scale_of(code):
    exponent = (jnp.right_shift(code, SCALE_BITS) - SCALE_BIAS).astype(f32)
    mantissa = (code & ((1 << SCALE_BITS) - 1)).astype(f32) * (0.5 ** 20)
    return mantissa * jnp.exp2(exponent)


TILE_COLUMNS = WIDTH // LANES


def message_tiles(count):
    return count // 2 * TILE_COLUMNS + 1


def put_row(message, start, value):
    for part in range(TILE_COLUMNS):
        message[start + part] = value[:, part * LANES : (part + 1) * LANES]


def get_row(message, start):
    return jnp.concatenate([message[start + part] for part in range(TILE_COLUMNS)], axis=1)


def encode(values, message, start=0):
    count = len(values)
    lane = lax.broadcasted_iota(jnp.int32, (LEVELS, LANES), 1)
    largest = jnp.full((LEVELS, LANES), 1e-30, f32)
    for number, value in enumerate(values):
        top = jnp.max(jnp.abs(value), axis=1, keepdims=True)
        largest = jnp.where(lane == number, jnp.maximum(top, 1e-30), largest)
    exponent = jnp.floor(jnp.log2(largest))
    mantissa = (largest * jnp.exp2(-exponent) * 2.0 ** 20).astype(jnp.int32) + 16
    code = jnp.left_shift(exponent.astype(jnp.int32) + SCALE_BIAS, SCALE_BITS) + mantissa
    factor = LEVEL_TOP / scale_of(code)
    half = count // 2
    whole = [nearest(value * factor[:, n : n + 1]) for n, value in enumerate(values)]
    for number in range(half):
        put_row(message, start + number * TILE_COLUMNS, join(whole[number], whole[number + half]))
    message[start + half * TILE_COLUMNS] = code


def decode(message, count, start=0):
    half = count // 2
    factor = scale_of(message[start + half * TILE_COLUMNS]) * (1.0 / LEVEL_TOP)
    values = [None] * count
    for number in range(half):
        pair = parted(get_row(message, start + number * TILE_COLUMNS))
        for place, value in zip((number, number + half), pair):
            values[place] = value.astype(f32) * factor[:, place : place + 1]
    return values


def encode_wind(first, second):
    steps = LEVEL_TOP / WIND_REACH
    return join(nearest((first - WIND_MIDDLE) * steps), nearest((second - WIND_MIDDLE) * steps))


def decode_wind(both):
    step = WIND_REACH / LEVEL_TOP
    return [value.astype(f32) * step + WIND_MIDDLE for value in parted(both)]


def forward_step(current, wind_x, wind_y, low):
    result = {}
    for row in range(low + 1, ROWS):
        here = current[row]
        left = pltpu.roll(here, 1, 1)
        result[row] = (
            here - wind_x(row) * (here - left) - wind_y(row) * (here - current[row - 1])
        )
    return result


def adjoint_step(current, wind_x, wind_y, high):
    result = {}
    for row in range(high - 1):
        here = current[row]
        along, across = wind_x(row), wind_y(row)
        result[row] = (
            here * (1.0 - along - across)
            + pltpu.roll(along * here, WIDTH - 1, 1)
            + wind_y(row + 1) * current[row + 1]
        )
    return result


def forward_steps(current, winds, low, count):
    for _ in range(count):
        current = forward_step(current, winds[0], winds[1], low)
        low += 1
    return current, low


def adjoint_steps(current, winds, high, count):
    for _ in range(count):
        current = adjoint_step(current, winds[0], winds[1], high)
        high -= 1
    return current, high


WINDS = 2
FIELDS = WINDS + SUBS
UP_EDGE = 4
EXTRA = 4
REACH = 10
DOWN_ROWS = [(sub, row) for sub in range(SUBS) for row in range(2 * sub, ROWS)]
WIND_TILES = ROWS * TILE_COLUMNS
FORCE_TILES = message_tiles(SUBS * ROWS)
EDGE_TILES = message_tiles(2)


def lower_winds(winds, winds_below, edge):
    def reader(field):
        def read(row):
            if row >= 0:
                return winds[field * ROWS + row]
            if row >= -ROWS:
                return winds_below[field * ROWS + row + ROWS]
            return edge[field * ROWS + row + 2 * ROWS]

        return read

    return [reader(field) for field in range(WINDS)]


def upper_winds(winds, winds_above, edge):
    def reader(field):
        def read(row):
            if row < ROWS:
                return winds[field * ROWS + row]
            if row < 2 * ROWS:
                return winds_above[field * ROWS + row - ROWS]
            return edge[field * UP_EDGE + row - 2 * ROWS]

        return read

    return [reader(field) for field in range(WINDS)]


def lower_forces(forces, forces_below, edge=None):
    def reader(sub):
        def read(row):
            if row >= 0:
                return forces[sub * ROWS + row]
            if row >= -ROWS:
                return forces_below[sub * ROWS + row + ROWS]
            return edge[sub, row + 2 * ROWS]

        return read

    return [reader(sub) for sub in range(SUBS)]


def add_rows(current, other, low, high):
    return {row: current[row] + other(row) for row in range(low, high)}


def fetch(pairs, sems):
    copies = [
        pltpu.make_async_copy(source, target, sems.at[number])
        for number, (source, target) in enumerate(pairs)
    ]
    for copy in copies:
        copy.start()
    return copies


def rows_kernel(
    forcing_far, courant_far, winds, forces, below, down_edge, forcing, courant, sems
):
    copies = fetch(
        [(courant_far.at[field], courant.at[field]) for field in range(WINDS)]
        + [(forcing_far.at[sub], forcing.at[sub]) for sub in range(SUBS)],
        sems,
    )
    for copy in copies[:WINDS]:
        copy.wait()
    for field in range(WINDS):
        winds[pl.ds(field * ROWS, ROWS)] = jnp.swapaxes(courant[field], 0, 1)
    encode_winds(winds, range(ROWS), below, 0)
    encode_winds(winds, range(ROWS), down_edge, 0)
    rows = []
    for sub in range(SUBS):
        copies[WINDS + sub].wait()
        turned = jnp.swapaxes(forcing[sub], 0, 1)
        forces[pl.ds(sub * ROWS, ROWS)] = turned
        rows += [turned[row] for row in range(ROWS)]
    encode(rows, below, WIND_TILES)
    encode([rows[sub * ROWS + row] for sub, row in DOWN_ROWS], down_edge, WIND_TILES)


def encode_winds(winds, rows, message, start):
    for number, row in enumerate(rows):
        both = encode_wind(winds[row], winds[ROWS + row])
        put_row(message, start + number * TILE_COLUMNS, both)


def unpack_winds(message, rows, result, start=0):
    for row in range(rows):
        first, second = decode_wind(get_row(message, start + row * TILE_COLUMNS))
        result[row] = first
        result[rows + row] = second


def choose_kernel(
    innovation_far, cells_far, weight_far, owner_far, channel_far, rinv_far,
    chosen, target, mixing,
    innovation, cells, weight, owner, channel_weight, rinv, sems,
):
    copies = fetch(
        [
            (channel_far, channel_weight), (rinv_far, rinv), (owner_far, owner),
            (cells_far, cells), (weight_far, weight),
        ]
        + [(innovation_far.at[sub], innovation.at[sub]) for sub in range(SUBS)],
        sems,
    )
    for copy in copies:
        copy.wait()
    sub_id = lax.broadcasted_iota(jnp.int32, (RECORDS, RECORDS), 0)
    lane_id = lax.broadcasted_iota(jnp.int32, (RECORDS, RECORDS), 1)
    not_later = lane_id <= sub_id

    scaled = channel_weight[...] * (rinv[...] * rinv[...])
    matrix = lax.dot_general(
        scaled, channel_weight[...], (((1,), (1,)), ((), ())),
        precision=highest, preferred_element_type=f32,
    )
    for level in range(LEVELS):
        mixing[level] = jnp.broadcast_to(matrix[:, level : level + 1], (LEVELS, LANES))
    top = scaled.astype(bf16)
    rest = scaled - top.astype(f32)
    middle = rest.astype(bf16)
    low = (rest - middle.astype(f32)).astype(bf16)

    spread_row = lax.broadcasted_iota(jnp.int32, (2 * LEVELS, LANES), 0)
    spread_lane = lax.broadcasted_iota(jnp.int32, (2 * LEVELS, LANES), 1)
    repeat = (
        (spread_lane // 64 == spread_row // LEVELS) & (spread_lane % LEVELS == spread_row % LEVELS)
    ).astype(f32)
    slot_lane = lax.broadcasted_iota(jnp.int32, (RECORDS, LANES), 1)
    slot_rank = ((slot_lane % 64) // LEVELS) * 2
    tile_id = lax.broadcasted_iota(jnp.int32, (TILES, RECORDS), 0)
    ones = jnp.ones((RECORDS, LANES), bf16)
    for sub in range(SUBS):
        data = innovation[sub]
        projected = (
            jnp.dot(top, data, preferred_element_type=f32)
            + jnp.dot(middle, data, preferred_element_type=f32)
            + jnp.dot(low, data, preferred_element_type=f32)
        )
        payload = jnp.concatenate(
            [cells[sub].astype(f32), weight[sub].astype(f32), projected], axis=0
        )
        owner_row = owner[sub]
        owner_rows = jnp.broadcast_to(owner_row, (RECORDS, RECORDS))
        earlier = jnp.where((owner_rows.T == owner_rows) & not_later, 1.0, 0.0).astype(bf16)
        rank = jnp.dot(earlier, ones, preferred_element_type=f32).astype(jnp.int32) - 1
        repeated = lax.dot_general(
            payload, repeat, (((0,), (0,)), ((), ())),
            precision=highest, preferred_element_type=f32,
        )
        target[sub] = (tile_id == owner_row).astype(f32)
        for half in range(2):
            chosen[2 * sub + half] = jnp.where(rank == slot_rank + half, repeated, 0.0)


def place_kernel(chosen, target, send):
    for sub in range(SUBS):
        for half in range(2):
            send[pl.ds(2 * sub + half, TILES, stride=8), :] = jnp.dot(
                target[sub], chosen[2 * sub + half],
                precision=highest, preferred_element_type=f32,
            )
    for spare in range(2 * SUBS, 8):
        send[pl.ds(spare, TILES, stride=8), :] = jnp.zeros((TILES, LANES), f32)


def stencil_kernel(received, slots, stencil, pieces):
    rows_id = lax.broadcasted_iota(jnp.int32, (HALF, LANES), 0)

    def one_sub(sub, _):
        for half in range(2):
            pieces[pl.ds(half * TILES, TILES), :] = received[
                pl.ds(2 * sub + half, TILES, stride=8), :
            ]
        slots[sub] = pieces[...].T
        for chunk in range(CHUNKS):
            record = slots[sub, pl.ds(chunk * LEVELS, LEVELS), :]
            column = record.astype(jnp.int32) & (HALF - 1)
            for corner in range(CORNERS):
                stencil[sub, chunk, :, corner * LANES : (corner + 1) * LANES] = jnp.where(
                    rows_id == column[corner : corner + 1],
                    record[CORNERS + corner : CORNERS + corner + 1],
                    0.0,
                ).astype(bf16)
        return 0

    lax.fori_loop(0, SUBS, one_sub, 0)


def observe(slots, stencil, mixing, states, found, spread):
    size = PIECES * LEVELS

    def one_sub(sub, _):
        top, low = split(states[sub])
        left = jnp.concatenate([top, low], axis=0)
        for chunk in range(CHUNKS):
            found[chunk] = jnp.dot(left, stencil[sub, chunk], preferred_element_type=f32)
        for chunk in range(CHUNKS):
            record = slots[sub, pl.ds(chunk * LEVELS, LEVELS), :]
            adjoint = -slots[sub, pl.ds(TILES + chunk * LEVELS, LEVELS), :]
            piece = jnp.right_shift(record.astype(jnp.int32), 8)
            sums = []
            wanted = []
            for corner in range(CORNERS):
                wanted.append(jnp.broadcast_to(piece[corner : corner + 1], (LEVELS, LANES)))
                part = pl.ds(corner * LANES, LANES)
                value = None
                for number in range(PIECES):
                    both = (
                        found[chunk, pl.ds(number * LEVELS, LEVELS), part]
                        + found[chunk, pl.ds(size + number * LEVELS, LEVELS), part]
                    )
                    value = both if value is None else jnp.where(wanted[corner] == number, both, value)
                sums.append(value)
            values = (sums[0] + sums[1]) + (sums[2] + sums[3])
            for level in range(LEVELS):
                adjoint = adjoint + mixing[level] * values[level : level + 1]
            first, second = split(adjoint)
            sources = first.astype(f32), second.astype(f32)
            for corner in range(CORNERS):
                part = pl.ds(corner * LANES, LANES)
                for place, source in enumerate(sources):
                    spread[chunk, pl.ds(place * size, size), part] = jnp.concatenate(
                        [jnp.where(wanted[corner] == number, source, 0.0) for number in range(PIECES)],
                        axis=0,
                    ).astype(bf16)
        total = jnp.zeros((2 * size, HALF), f32)
        for chunk in range(CHUNKS):
            total = total + lax.dot_general(
                spread[chunk], stencil[sub, chunk], (((1,), (1,)), ((), ())),
                preferred_element_type=f32,
            )
        states[sub] = total[:size] + total[size:]
        return 0

    lax.fori_loop(0, SUBS, one_sub, 0)


def forward_local_kernel(
    winds, forces, below, down_edge, own, mine, winds_below, lower_edge, forces_below
):
    unpack_winds(below, ROWS, winds_below)
    unpack_winds(down_edge, ROWS, lower_edge)
    for number, row in enumerate(decode(below, SUBS * ROWS, WIND_TILES)):
        forces_below[number] = row
    edge = dict(zip(DOWN_ROWS, decode(down_edge, len(DOWN_ROWS), WIND_TILES)))
    across = lower_winds(winds, winds_below, lower_edge)
    forced = lower_forces(forces, forces_below, edge)
    low = -2 * ROWS
    current = {row: forced[0](row) for row in range(low, ROWS)}
    current, low = forward_steps(current, across, low, 2)
    for sub in range(1, SUBS):
        current = add_rows(current, forced[sub], low, ROWS)
        current, low = forward_steps(current, across, low, 2)
    listed = [current[row] for row in range(-REACH, ROWS)]
    for number, row in enumerate(listed[REACH - EXTRA :]):
        mine[number] = row
    encode(listed, own)


def before_state(message, low):
    rows = decode(message, REACH + ROWS)
    return {row: rows[row + REACH] for row in range(low, ROWS)}


def lower_state(own, extended, low):
    here = decode(own, ROWS)
    under = decode(extended, ROWS + EXTRA)
    return {row: here[row] if row >= 0 else under[row + ROWS + EXTRA] for row in range(low, ROWS)}


def forward_pair_kernel(winds, winds_below, lower_edge, mine, before, own, extended):
    across = lower_winds(winds, winds_below, lower_edge)
    current, low = forward_steps(before_state(before, -REACH), across, -REACH, 6)
    listed = [current[row] + mine[row + EXTRA] for row in range(-EXTRA, ROWS)]
    encode(listed[EXTRA:], own)
    encode(listed, extended)


def forward_final_kernel(
    winds, forces, winds_below, lower_edge, forces_below,
    before, pair_own, pair_extended, slots, stencil, mixing,
    result, result_above, result_edge,
    states, found, spread,
):
    across = lower_winds(winds, winds_below, lower_edge)
    forced = lower_forces(forces, forces_below)
    low = -(ROWS + EXTRA)
    current, low = forward_steps(lower_state(pair_own, pair_extended, low), across, low, 6)
    before = before_state(before, low)
    current = {row: current[row] + before[row] for row in current}
    for sub in range(SUBS):
        current = add_rows(current, forced[sub], low, ROWS)
        current, low = forward_steps(current, across, low, 2)
        for row in range(ROWS):
            for half in range(2):
                place = (2 * row + half) * LEVELS
                states[sub, place : place + LEVELS, :] = current[row][
                    :, half * HALF : (half + 1) * HALF
                ]
    observe(slots, stencil, mixing, states, found, spread)
    listed = []
    for sub in range(SUBS):
        for row in range(ROWS):
            places = [(2 * row + half) * LEVELS for half in range(2)]
            value = jnp.concatenate(
                [states[sub, place : place + LEVELS, :] for place in places], axis=1
            )
            result[sub, row] = value
            listed.append(value)
    encode(listed, result_above)
    encode_winds(winds, range(ROWS), result_above, FORCE_TILES)
    encode(listed[-ROWS : 2 - ROWS], result_edge)
    encode_winds(winds, range(UP_EDGE), result_edge, EDGE_TILES)


def adjoint_local_kernel(
    source, source_above, source_edge, winds,
    own, extended, mine, unpacked, winds_above, upper_edge,
):
    unpack_winds(source_above, ROWS, winds_above, FORCE_TILES)
    unpack_winds(source_edge, UP_EDGE, upper_edge, EDGE_TILES)
    across = upper_winds(winds, winds_above, upper_edge)
    high = 2 * ROWS + 2
    above = decode(source_above, SUBS * ROWS)
    edge = decode(source_edge, 2)
    for number, row in enumerate(above):
        unpacked[number] = row

    def source_row(sub):
        return lambda row: source[sub, row] if row < ROWS else unpacked[sub * ROWS + row - ROWS]

    current = {row: source_row(SUBS - 1)(row) for row in range(2 * ROWS)}
    for number, row in enumerate(edge):
        current[2 * ROWS + number] = row
    current, high = adjoint_steps(current, across, high, 2)
    for sub in reversed(range(SUBS - 1)):
        current = add_rows(current, source_row(sub), 0, high)
        current, high = adjoint_steps(current, across, high, 2)
    listed = [current[row] for row in range(ROWS + EXTRA)]
    for number, row in enumerate(listed):
        mine[number] = row
    encode(listed[:ROWS], own)
    encode(listed[:REACH], extended)


def upper_state(own, extended, high, count):
    here = decode(own, ROWS)
    over = decode(extended, count)
    return {row: here[row] if row < ROWS else over[row - ROWS] for row in range(high)}


def adjoint_pair_kernel(
    winds, winds_above, upper_edge, mine, after_own, after_extended, own, extended
):
    across = upper_winds(winds, winds_above, upper_edge)
    high = 2 * ROWS + 2
    current, high = adjoint_steps(upper_state(after_own, after_extended, high, REACH), across, high, 6)
    listed = [current[row] + mine[row] for row in range(ROWS + EXTRA)]
    encode(listed[:ROWS], own)
    encode(listed, extended)


def adjoint_final_kernel(
    source, unpacked, winds, winds_above, upper_edge,
    after_own, after_extended, pair_own, pair_extended, gradient_far, gradient, sems,
):
    across = upper_winds(winds, winds_above, upper_edge)
    high = 2 * ROWS + EXTRA
    current, high = adjoint_steps(upper_state(pair_own, pair_extended, high, ROWS + EXTRA), across, high, 6)
    after = upper_state(after_own, after_extended, high, REACH)
    current = {row: current[row] + after[row] for row in current}

    def source_row(sub):
        return lambda row: source[sub, row] if row < ROWS else unpacked[sub * ROWS + row - ROWS]

    copies = []
    for sub in reversed(range(SUBS)):
        current = add_rows(current, source_row(sub), 0, high)
        current, high = adjoint_steps(current, across, high, 2)
        gradient[sub] = jnp.swapaxes(jnp.stack([current[row] for row in range(ROWS)]), 0, 1)
        copies.append(
            pltpu.make_async_copy(gradient.at[sub], gradient_far.at[sub], sems.at[sub])
        )
        copies[-1].start()
    for copy in copies:
        copy.wait()


def run(kernel, outputs, arguments, scratch=(), name=None, flops=2_000_000, far=False, far_out=False):
    size = sum(a.size * a.dtype.itemsize for a in arguments)
    place = pltpu.HBM if far else pltpu.VMEM
    if far:
        arguments = [pltpu.with_memory_space_constraint(a, pltpu.HBM) for a in arguments]
    return pl.pallas_call(
        kernel,
        out_shape=outputs,
        in_specs=[pl.BlockSpec(memory_space=place)] * len(arguments),
        **({"out_specs": pl.BlockSpec(memory_space=pltpu.HBM)} if far_out else {}),
        scratch_shapes=scratch,
        compiler_params=pltpu.CompilerParams(vmem_limit_bytes=40 * 1024 * 1024),
        cost_estimate=pl.CostEstimate(flops=flops, bytes_accessed=size, transcendentals=0),
        name=name,
    )(*arguments)


def moved(array, parts, tiles):
    pairs = []
    for part in range(PARTS):
        for tile in range(TILES):
            to_part, to_tile = part + parts, tile + tiles
            if 0 <= to_part < PARTS and 0 <= to_tile < TILES:
                pairs.append((part * TILES + tile, to_part * TILES + to_tile))
    return lax.ppermute(array, ("tm", "space"), pairs)


def shards(
    forcing, courant, innovation, obs_cells, obs_weight, obs_owner, channel_weight, channel_rinv
):
    def message(tiles):
        return struct(tiles, LEVELS, LANES, dtype=jnp.int32)

    winds, forces, below, down_edge = run(
        rows_kernel,
        (
            struct(WINDS * ROWS, LEVELS, WIDTH),
            struct(SUBS * ROWS, LEVELS, WIDTH),
            message(WIND_TILES + FORCE_TILES),
            message(WIND_TILES + message_tiles(len(DOWN_ROWS))),
        ),
        (forcing, courant),
        scratch=(
            pltpu.VMEM(forcing.shape, f32),
            pltpu.VMEM(courant.shape, f32),
            pltpu.SemaphoreType.DMA((FIELDS,)),
        ),
        name="rows",
        far=True,
    )
    below = moved(below, 0, 1)
    down_edge = moved(down_edge, 0, 2)
    records = (
        innovation, obs_cells, obs_weight, jnp.swapaxes(obs_owner, 1, 2),
        channel_weight.T, channel_rinv.reshape(1, -1),
    )
    chosen, target, mixing = run(
        choose_kernel,
        (
            struct(2 * SUBS, RECORDS, LANES),
            struct(SUBS, TILES, RECORDS),
            struct(LEVELS, LEVELS, LANES),
        ),
        records,
        scratch=(
            *[pltpu.VMEM(array.shape, array.dtype) for array in records],
            pltpu.SemaphoreType.DMA((len(records) + SUBS - 1,)),
        ),
        name="choose",
        far=True,
    )
    send = run(place_kernel, struct(TILES * 8, LANES), (chosen, target), name="place")
    received = lax.all_to_all(
        send.reshape(TILES, 8, LANES), "space", split_axis=0, concat_axis=0, tiled=True
    ).reshape(TILES * 8, LANES)
    below, down_edge, _ = lax.optimization_barrier((below, down_edge, send))
    own, mine, winds_below, lower_edge, forces_below = run(
        forward_local_kernel,
        (
            message(message_tiles(REACH + ROWS)),
            struct(ROWS + EXTRA, LEVELS, WIDTH),
            struct(WINDS * ROWS, LEVELS, WIDTH),
            struct(WINDS * ROWS, LEVELS, WIDTH),
            struct(SUBS * ROWS, LEVELS, WIDTH),
        ),
        (winds, forces, below, down_edge),
        name="forward_local",
    )
    before = moved(own, 1, 0)
    pair_shapes = (message(message_tiles(ROWS)), message(message_tiles(ROWS + EXTRA)))
    own, extended = run(
        forward_pair_kernel,
        pair_shapes,
        (winds, winds_below, lower_edge, mine, before),
        name="forward_pair",
    )
    pair = (moved(own, 2, 0), moved(extended, 2, 1))
    slots, stencil = run(
        stencil_kernel,
        (
            struct(SUBS, LANES, LANES),
            struct(SUBS, CHUNKS, HALF, CORNERS * LANES, dtype=bf16),
        ),
        (received,),
        scratch=(pltpu.VMEM((LANES, LANES), f32),),
        name="stencil",
    )
    size = PIECES * LEVELS
    source, source_above, source_edge = run(
        forward_final_kernel,
        (
            struct(SUBS, ROWS, LEVELS, WIDTH),
            message(FORCE_TILES + WIND_TILES),
            message(EDGE_TILES + UP_EDGE * TILE_COLUMNS),
        ),
        (
            winds, forces, winds_below, lower_edge, forces_below,
            before, *pair, slots, stencil, mixing,
        ),
        scratch=(
            pltpu.VMEM((SUBS, size, HALF), f32),
            pltpu.VMEM((CHUNKS, 2 * size, CORNERS * LANES), f32),
            pltpu.VMEM((CHUNKS, 2 * size, CORNERS * LANES), bf16),
        ),
        name="forward_final",
    )

    source_above = moved(source_above, 0, -1)
    source_edge = moved(source_edge, 0, -2)
    own, extended, mine, unpacked, winds_above, upper_edge = run(
        adjoint_local_kernel,
        (
            message(message_tiles(ROWS)),
            message(message_tiles(REACH)),
            struct(ROWS + EXTRA, LEVELS, WIDTH),
            struct(SUBS * ROWS, LEVELS, WIDTH),
            struct(WINDS * ROWS, LEVELS, WIDTH),
            struct(WINDS * UP_EDGE, LEVELS, WIDTH),
        ),
        (source, source_above, source_edge, winds),
        name="adjoint_local",
    )
    after = (moved(own, -1, 0), moved(extended, -1, -1))
    own, extended = run(
        adjoint_pair_kernel,
        pair_shapes,
        (winds, winds_above, upper_edge, mine, *after),
        name="adjoint_pair",
    )
    pair = (moved(own, -2, 0), moved(extended, -2, -1))
    return run(
        adjoint_final_kernel,
        struct(SUBS, LEVELS, ROWS, WIDTH),
        (source, unpacked, winds, winds_above, upper_edge, *after, *pair),
        scratch=(
            pltpu.VMEM((SUBS, LEVELS, ROWS, WIDTH), f32),
            pltpu.SemaphoreType.DMA((SUBS,)),
        ),
        name="adjoint_final",
        far_out=True,
    )


def solution(mesh):
    return jax.shard_map(
        shards,
        mesh=mesh,
        in_specs=(
            P("tm", None, "space", None),
            P(None, None, "space", None),
            P("tm", None, "space"),
            P("tm", None, "space"),
            P("tm", None, "space"),
            P("tm", "space", None),
            P(),
            P(),
        ),
        out_specs=P("tm", None, "space", None),
        check_vma=False,
    )
```

```python
import jax
import jax.numpy as jnp
from jax import lax
from jax.experimental import pallas as pl
from jax.experimental.pallas import tpu as pltpu
from jax.sharding import PartitionSpec as P

LEVELS = 8
ROWS = 8
WIDTH = 512
SUBS = 3
TILES = 64
PARTS = 4
RECORDS = 256
CORNERS = 4
HALF = 256
PIECES = WIDTH // HALF * ROWS
CHUNKS = 8
LANES = 128

f32 = jnp.float32
bf16 = jnp.bfloat16
highest = lax.Precision.HIGHEST


def struct(*shape, dtype=f32):
    return jax.ShapeDtypeStruct(shape, dtype)


def split(value):
    top = value.astype(bf16)
    return top, (value - top.astype(f32)).astype(bf16)


LEVEL_TOP = 32766.0
SCALE_BITS = 22
SCALE_BIAS = 256
WIND_MIDDLE = 0.25
WIND_REACH = 0.21


def nearest(value):
    return jnp.floor(value + 0.5).astype(jnp.int32)


def join(first, second):
    return jnp.left_shift(first, 16) | (second & 0xFFFF)


def parted(both):
    return jnp.right_shift(both, 16), jnp.right_shift(jnp.left_shift(both, 16), 16)


def scale_of(code):
    exponent = (jnp.right_shift(code, SCALE_BITS) - SCALE_BIAS).astype(f32)
    mantissa = (code & ((1 << SCALE_BITS) - 1)).astype(f32) * (0.5 ** 20)
    return mantissa * jnp.exp2(exponent)


TILE_COLUMNS = WIDTH // LANES


def message_tiles(count):
    return count // 2 * TILE_COLUMNS + 1


def put_row(message, start, value):
    for part in range(TILE_COLUMNS):
        message[start + part] = value[:, part * LANES : (part + 1) * LANES]


def get_row(message, start):
    return jnp.concatenate([message[start + part] for part in range(TILE_COLUMNS)], axis=1)


def encode(values, message, start=0):
    count = len(values)
    lane = lax.broadcasted_iota(jnp.int32, (LEVELS, LANES), 1)
    largest = jnp.full((LEVELS, LANES), 1e-30, f32)
    for number, value in enumerate(values):
        top = jnp.max(jnp.abs(value), axis=1, keepdims=True)
        largest = jnp.where(lane == number, jnp.maximum(top, 1e-30), largest)
    exponent = jnp.floor(jnp.log2(largest))
    mantissa = (largest * jnp.exp2(-exponent) * 2.0 ** 20).astype(jnp.int32) + 16
    code = jnp.left_shift(exponent.astype(jnp.int32) + SCALE_BIAS, SCALE_BITS) + mantissa
    factor = LEVEL_TOP / scale_of(code)
    half = count // 2
    whole = [nearest(value * factor[:, n : n + 1]) for n, value in enumerate(values)]
    for number in range(half):
        put_row(message, start + number * TILE_COLUMNS, join(whole[number], whole[number + half]))
    message[start + half * TILE_COLUMNS] = code


def decode(message, count, start=0):
    half = count // 2
    factor = scale_of(message[start + half * TILE_COLUMNS]) * (1.0 / LEVEL_TOP)
    values = [None] * count
    for number in range(half):
        pair = parted(get_row(message, start + number * TILE_COLUMNS))
        for place, value in zip((number, number + half), pair):
            values[place] = value.astype(f32) * factor[:, place : place + 1]
    return values


def encode_wind(first, second):
    steps = LEVEL_TOP / WIND_REACH
    return join(nearest((first - WIND_MIDDLE) * steps), nearest((second - WIND_MIDDLE) * steps))


def decode_wind(both):
    step = WIND_REACH / LEVEL_TOP
    return [value.astype(f32) * step + WIND_MIDDLE for value in parted(both)]


def forward_step(current, wind_x, wind_y, low):
    result = {}
    for row in range(low + 1, ROWS):
        here = current[row]
        left = pltpu.roll(here, 1, 1)
        result[row] = (
            here - wind_x(row) * (here - left) - wind_y(row) * (here - current[row - 1])
        )
    return result


def adjoint_step(current, wind_x, wind_y, low):
    result = {low - 1: wind_y(low) * current[low]}
    for row in range(low, ROWS):
        here = current[row]
        along = wind_x(row)
        value = here * (1.0 - along - wind_y(row)) + pltpu.roll(along * here, WIDTH - 1, 1)
        if row + 1 < ROWS:
            value = value + wind_y(row + 1) * current[row + 1]
        result[row] = value
    return result


def forward_steps(current, winds, low, count):
    for _ in range(count):
        current = forward_step(current, winds[0], winds[1], low)
        low += 1
    return current, low


def adjoint_steps(current, winds, low, count):
    for _ in range(count):
        current = adjoint_step(current, winds[0], winds[1], low)
        low -= 1
    return current, low


WINDS = 2
FIELDS = WINDS + SUBS
EXTRA = 4
REACH = 10
DROP = 6
DOWN_ROWS = [(sub, row) for sub in range(SUBS) for row in range(2 * sub, ROWS)]
WIND_TILES = ROWS * TILE_COLUMNS


def lower_winds(winds, winds_below, edge):
    def reader(field):
        def read(row):
            if row >= 0:
                return winds[field * ROWS + row]
            if row >= -ROWS:
                return winds_below[field * ROWS + row + ROWS]
            return edge[field * ROWS + row + 2 * ROWS]

        return read

    return [reader(field) for field in range(WINDS)]


def lower_forces(forces, forces_below, edge=None):
    def reader(sub):
        def read(row):
            if row >= 0:
                return forces[sub * ROWS + row]
            if row >= -ROWS:
                return forces_below[sub * ROWS + row + ROWS]
            return edge[sub, row + 2 * ROWS]

        return read

    return [reader(sub) for sub in range(SUBS)]


def add_rows(current, other, low, high):
    return {row: current[row] + other(row) for row in range(low, high)}


def fetch(pairs, sems):
    copies = [
        pltpu.make_async_copy(source, target, sems.at[number])
        for number, (source, target) in enumerate(pairs)
    ]
    for copy in copies:
        copy.start()
    return copies


def rows_kernel(
    forcing_far, courant_far, winds, forces, below, down_edge, forcing, courant, sems
):
    copies = fetch(
        [(courant_far.at[field], courant.at[field]) for field in range(WINDS)]
        + [(forcing_far.at[sub], forcing.at[sub]) for sub in range(SUBS)],
        sems,
    )
    for copy in copies[:WINDS]:
        copy.wait()
    for field in range(WINDS):
        winds[pl.ds(field * ROWS, ROWS)] = jnp.swapaxes(courant[field], 0, 1)
    encode_winds(winds, range(ROWS), below, 0)
    encode_winds(winds, range(ROWS), down_edge, 0)
    rows = []
    for sub in range(SUBS):
        copies[WINDS + sub].wait()
        turned = jnp.swapaxes(forcing[sub], 0, 1)
        forces[pl.ds(sub * ROWS, ROWS)] = turned
        rows += [turned[row] for row in range(ROWS)]
    encode(rows, below, WIND_TILES)
    encode([rows[sub * ROWS + row] for sub, row in DOWN_ROWS], down_edge, WIND_TILES)


def encode_winds(winds, rows, message, start):
    for number, row in enumerate(rows):
        both = encode_wind(winds[row], winds[ROWS + row])
        put_row(message, start + number * TILE_COLUMNS, both)


def unpack_winds(message, rows, result, start=0):
    for row in range(rows):
        first, second = decode_wind(get_row(message, start + row * TILE_COLUMNS))
        result[row] = first
        result[rows + row] = second


def choose_kernel(
    innovation_far, cells_far, weight_far, owner_far, channel_far, rinv_far,
    chosen, target, mixing,
    innovation, cells, weight, owner, channel_weight, rinv, sems,
):
    copies = fetch(
        [
            (channel_far, channel_weight), (rinv_far, rinv), (owner_far, owner),
            (cells_far, cells), (weight_far, weight),
        ]
        + [(innovation_far.at[sub], innovation.at[sub]) for sub in range(SUBS)],
        sems,
    )
    for copy in copies:
        copy.wait()
    sub_id = lax.broadcasted_iota(jnp.int32, (RECORDS, RECORDS), 0)
    lane_id = lax.broadcasted_iota(jnp.int32, (RECORDS, RECORDS), 1)
    not_later = lane_id <= sub_id

    scaled = channel_weight[...] * (rinv[...] * rinv[...])
    matrix = lax.dot_general(
        scaled, channel_weight[...], (((1,), (1,)), ((), ())),
        precision=highest, preferred_element_type=f32,
    )
    for level in range(LEVELS):
        mixing[level] = jnp.broadcast_to(matrix[:, level : level + 1], (LEVELS, LANES))
    top = scaled.astype(bf16)
    rest = scaled - top.astype(f32)
    middle = rest.astype(bf16)
    low = (rest - middle.astype(f32)).astype(bf16)

    spread_row = lax.broadcasted_iota(jnp.int32, (2 * LEVELS, LANES), 0)
    spread_lane = lax.broadcasted_iota(jnp.int32, (2 * LEVELS, LANES), 1)
    repeat = (
        (spread_lane // 64 == spread_row // LEVELS) & (spread_lane % LEVELS == spread_row % LEVELS)
    ).astype(f32)
    slot_lane = lax.broadcasted_iota(jnp.int32, (RECORDS, LANES), 1)
    slot_rank = ((slot_lane % 64) // LEVELS) * 2
    tile_id = lax.broadcasted_iota(jnp.int32, (TILES, RECORDS), 0)
    ones = jnp.ones((RECORDS, LANES), bf16)
    for sub in range(SUBS):
        data = innovation[sub]
        projected = (
            jnp.dot(top, data, preferred_element_type=f32)
            + jnp.dot(middle, data, preferred_element_type=f32)
            + jnp.dot(low, data, preferred_element_type=f32)
        )
        payload = jnp.concatenate(
            [cells[sub].astype(f32), weight[sub].astype(f32), projected], axis=0
        )
        owner_row = owner[sub]
        owner_rows = jnp.broadcast_to(owner_row, (RECORDS, RECORDS))
        earlier = jnp.where((owner_rows.T == owner_rows) & not_later, 1.0, 0.0).astype(bf16)
        rank = jnp.dot(earlier, ones, preferred_element_type=f32).astype(jnp.int32) - 1
        repeated = lax.dot_general(
            payload, repeat, (((0,), (0,)), ((), ())),
            precision=highest, preferred_element_type=f32,
        )
        target[sub] = (tile_id == owner_row).astype(f32)
        for half in range(2):
            chosen[2 * sub + half] = jnp.where(rank == slot_rank + half, repeated, 0.0)


def place_kernel(chosen, target, send):
    for sub in range(SUBS):
        for half in range(2):
            send[pl.ds(2 * sub + half, TILES, stride=8), :] = jnp.dot(
                target[sub], chosen[2 * sub + half],
                precision=highest, preferred_element_type=f32,
            )
    for spare in range(2 * SUBS, 8):
        send[pl.ds(spare, TILES, stride=8), :] = jnp.zeros((TILES, LANES), f32)


def stencil_kernel(received, slots, stencil, pieces):
    rows_id = lax.broadcasted_iota(jnp.int32, (HALF, LANES), 0)

    def one_sub(sub, _):
        for half in range(2):
            pieces[pl.ds(half * TILES, TILES), :] = received[
                pl.ds(2 * sub + half, TILES, stride=8), :
            ]
        slots[sub] = pieces[...].T
        for chunk in range(CHUNKS):
            record = slots[sub, pl.ds(chunk * LEVELS, LEVELS), :]
            column = record.astype(jnp.int32) & (HALF - 1)
            for corner in range(CORNERS):
                stencil[sub, chunk, :, corner * LANES : (corner + 1) * LANES] = jnp.where(
                    rows_id == column[corner : corner + 1],
                    record[CORNERS + corner : CORNERS + corner + 1],
                    0.0,
                ).astype(bf16)
        return 0

    lax.fori_loop(0, SUBS, one_sub, 0)


def respond(slots, mixing, sub, chunk, found, spread):
    size = PIECES * LEVELS
    record = slots[sub, pl.ds(chunk * LEVELS, LEVELS), :]
    adjoint = -slots[sub, pl.ds(TILES + chunk * LEVELS, LEVELS), :]
    piece = jnp.right_shift(record.astype(jnp.int32), 8)
    sums = []
    wanted = []
    for corner in range(CORNERS):
        wanted.append(jnp.broadcast_to(piece[corner : corner + 1], (LEVELS, LANES)))
        part = pl.ds(corner * LANES, LANES)
        value = None
        for number in range(PIECES):
            both = (
                found[sub, chunk, pl.ds(number * LEVELS, LEVELS), part]
                + found[sub, chunk, pl.ds(size + number * LEVELS, LEVELS), part]
            )
            value = both if value is None else jnp.where(wanted[corner] == number, both, value)
        sums.append(value)
    values = (sums[0] + sums[1]) + (sums[2] + sums[3])
    for level in range(LEVELS):
        adjoint = adjoint + mixing[level] * values[level : level + 1]
    sources = [part.astype(f32) for part in split(adjoint)]
    for corner in range(CORNERS):
        part = pl.ds(corner * LANES, LANES)
        for place, source in enumerate(sources):
            spread[sub, chunk, pl.ds(place * size, size), part] = jnp.concatenate(
                [jnp.where(wanted[corner] == number, source, 0.0) for number in range(PIECES)],
                axis=0,
            ).astype(bf16)


def observe(slots, stencil, mixing, states, found, spread):
    size = PIECES * LEVELS
    for sub in range(SUBS):
        left = jnp.concatenate(split(states[sub]), axis=0)
        for chunk in range(CHUNKS):
            found[sub, chunk] = jnp.dot(left, stencil[sub, chunk], preferred_element_type=f32)
    results = []
    for sub in range(SUBS):
        for chunk in range(CHUNKS):
            respond(slots, mixing, sub, chunk, found, spread)
        total = jnp.zeros((2 * size, HALF), f32)
        for chunk in range(CHUNKS):
            total = total + lax.dot_general(
                spread[sub, chunk], stencil[sub, chunk], (((1,), (1,)), ((), ())),
                preferred_element_type=f32,
            )
        results.append(total[:size] + total[size:])
    return results


def forward_local_kernel(
    winds, forces, below, down_edge, own, mine, winds_below, lower_edge, forces_below
):
    unpack_winds(below, ROWS, winds_below)
    unpack_winds(down_edge, ROWS, lower_edge)
    for number, row in enumerate(decode(below, SUBS * ROWS, WIND_TILES)):
        forces_below[number] = row
    edge = dict(zip(DOWN_ROWS, decode(down_edge, len(DOWN_ROWS), WIND_TILES)))
    across = lower_winds(winds, winds_below, lower_edge)
    forced = lower_forces(forces, forces_below, edge)
    low = -2 * ROWS
    current = {row: forced[0](row) for row in range(low, ROWS)}
    current, low = forward_steps(current, across, low, 2)
    for sub in range(1, SUBS):
        current = add_rows(current, forced[sub], low, ROWS)
        current, low = forward_steps(current, across, low, 2)
    listed = [current[row] for row in range(-REACH, ROWS)]
    for number, row in enumerate(listed[REACH - EXTRA :]):
        mine[number] = row
    encode(listed, own)


def before_state(message, low):
    rows = decode(message, REACH + ROWS)
    return {row: rows[row + REACH] for row in range(low, ROWS)}


def lower_state(own, extended, low):
    here = decode(own, ROWS)
    under = decode(extended, ROWS + EXTRA)
    return {row: here[row] if row >= 0 else under[row + ROWS + EXTRA] for row in range(low, ROWS)}


def forward_pair_kernel(winds, winds_below, lower_edge, mine, before, own, extended):
    across = lower_winds(winds, winds_below, lower_edge)
    current, low = forward_steps(before_state(before, -REACH), across, -REACH, 6)
    listed = [current[row] + mine[row + EXTRA] for row in range(-EXTRA, ROWS)]
    encode(listed[EXTRA:], own)
    encode(listed, extended)


def forward_final_kernel(
    winds, forces, winds_below, lower_edge, forces_below,
    before, pair_own, pair_extended, slots, stencil, mixing,
    sources, mine, response,
    states, found, spread,
):
    across = lower_winds(winds, winds_below, lower_edge)
    forced = lower_forces(forces, forces_below)
    low = -(ROWS + EXTRA)
    current, low = forward_steps(lower_state(pair_own, pair_extended, low), across, low, 6)
    before = before_state(before, low)
    current = {row: current[row] + before[row] for row in current}
    for sub in range(SUBS):
        current = add_rows(current, forced[sub], low, ROWS)
        current, low = forward_steps(current, across, low, 2)
        for row in range(ROWS):
            for half in range(2):
                place = (2 * row + half) * LEVELS
                states[sub, place : place + LEVELS, :] = current[row][
                    :, half * HALF : (half + 1) * HALF
                ]
    for sub, stack in enumerate(observe(slots, stencil, mixing, states, found, spread)):
        for row in range(ROWS):
            for half in range(2):
                place = (2 * row + half) * LEVELS
                sources[sub * ROWS + row, :, half * HALF : (half + 1) * HALF] = stack[
                    place : place + LEVELS
                ]
    current = {row: sources[(SUBS - 1) * ROWS + row] for row in range(ROWS)}
    current, low = adjoint_steps(current, across, 0, 2)
    for sub in reversed(range(SUBS - 1)):
        current = add_sources(current, sources, sub)
        current, low = adjoint_steps(current, across, low, 2)
    listed = [current[row] for row in range(low, ROWS)]
    for number, row in enumerate(listed):
        mine[number] = row
    encode(listed, response)


def add_sources(current, sources, sub):
    return {
        row: value + sources[sub * ROWS + row] if row >= 0 else value
        for row, value in current.items()
    }


def after_state(message):
    rows = decode(message, DROP + ROWS)
    return {row: rows[row + DROP] for row in range(-DROP, ROWS)}


def adjoint_pair_kernel(winds, winds_below, lower_edge, mine, after, own, extended):
    across = lower_winds(winds, winds_below, lower_edge)
    current, low = adjoint_steps(after_state(after), across, -DROP, 6)
    for row in range(-DROP, ROWS):
        current[row] = current[row] + mine[row + DROP]
    encode([current[row] for row in range(ROWS)], own)
    encode([current[row] for row in range(low, 0)], extended)


PUSHED = [(sub, row) for sub in range(SUBS) for row in range(ROWS)]
PUSHED_FAR = [(sub, row) for sub in range(SUBS) for row in range(2 * sub, ROWS)]


def adjoint_final_kernel(
    sources, winds, winds_below, lower_edge, after, pair_own, pair_extended,
    gradient, pushed, pushed_far,
):
    across = lower_winds(winds, winds_below, lower_edge)
    own = decode(pair_own, ROWS)
    above = decode(pair_extended, ROWS + EXTRA)
    low = -EXTRA
    current = {
        row: above[row + EXTRA] + own[row] if row >= 0 else above[row + EXTRA]
        for row in range(low, ROWS)
    }
    current, low = adjoint_steps(current, across, low, 6)
    after = after_state(after)
    for row in after:
        current[row] = current[row] + after[row]
    results = [None] * SUBS
    for sub in reversed(range(SUBS)):
        current = add_sources(current, sources, sub)
        current, low = adjoint_steps(current, across, low, 2)
        results[sub] = current
        for row in range(ROWS):
            gradient[sub * ROWS + row] = current[row]
    encode([results[sub][row - ROWS] for sub, row in PUSHED], pushed)
    encode([results[sub][row - 2 * ROWS] for sub, row in PUSHED_FAR], pushed_far)


def finish_kernel(part, pushed, pushed_far, gradient_far, gradient, sems):
    near = dict(zip(PUSHED, decode(pushed, len(PUSHED))))
    far = dict(zip(PUSHED_FAR, decode(pushed_far, len(PUSHED_FAR))))
    copies = []
    for sub in range(SUBS):
        rows = []
        for row in range(ROWS):
            value = part[sub * ROWS + row] + near[sub, row]
            rows.append(value + far[sub, row] if (sub, row) in far else value)
        gradient[sub] = jnp.swapaxes(jnp.stack(rows), 0, 1)
        copies.append(
            pltpu.make_async_copy(gradient.at[sub], gradient_far.at[sub], sems.at[sub])
        )
        copies[-1].start()
    for copy in copies:
        copy.wait()


def run(kernel, outputs, arguments, scratch=(), name=None, flops=2_000_000, far=False, far_out=False):
    size = sum(a.size * a.dtype.itemsize for a in arguments)
    place = pltpu.HBM if far else pltpu.VMEM
    if far:
        arguments = [pltpu.with_memory_space_constraint(a, pltpu.HBM) for a in arguments]
    return pl.pallas_call(
        kernel,
        out_shape=outputs,
        in_specs=[pl.BlockSpec(memory_space=place)] * len(arguments),
        **({"out_specs": pl.BlockSpec(memory_space=pltpu.HBM)} if far_out else {}),
        scratch_shapes=scratch,
        compiler_params=pltpu.CompilerParams(vmem_limit_bytes=40 * 1024 * 1024),
        cost_estimate=pl.CostEstimate(flops=flops, bytes_accessed=size, transcendentals=0),
        name=name,
    )(*arguments)


def moved(array, parts, tiles):
    pairs = []
    for part in range(PARTS):
        for tile in range(TILES):
            to_part, to_tile = part + parts, tile + tiles
            if 0 <= to_part < PARTS and 0 <= to_tile < TILES:
                pairs.append((part * TILES + tile, to_part * TILES + to_tile))
    return lax.ppermute(array, ("tm", "space"), pairs)


def shards(
    forcing, courant, innovation, obs_cells, obs_weight, obs_owner, channel_weight, channel_rinv
):
    def message(tiles):
        return struct(tiles, LEVELS, LANES, dtype=jnp.int32)

    winds, forces, below, down_edge = run(
        rows_kernel,
        (
            struct(WINDS * ROWS, LEVELS, WIDTH),
            struct(SUBS * ROWS, LEVELS, WIDTH),
            message(WIND_TILES + message_tiles(SUBS * ROWS)),
            message(WIND_TILES + message_tiles(len(DOWN_ROWS))),
        ),
        (forcing, courant),
        scratch=(
            pltpu.VMEM(forcing.shape, f32),
            pltpu.VMEM(courant.shape, f32),
            pltpu.SemaphoreType.DMA((FIELDS,)),
        ),
        name="rows",
        far=True,
    )
    below = moved(below, 0, 1)
    down_edge = moved(down_edge, 0, 2)
    records = (
        innovation, obs_cells, obs_weight, jnp.swapaxes(obs_owner, 1, 2),
        channel_weight.T, channel_rinv.reshape(1, -1),
    )
    chosen, target, mixing = run(
        choose_kernel,
        (
            struct(2 * SUBS, RECORDS, LANES),
            struct(SUBS, TILES, RECORDS),
            struct(LEVELS, LEVELS, LANES),
        ),
        records,
        scratch=(
            *[pltpu.VMEM(array.shape, array.dtype) for array in records],
            pltpu.SemaphoreType.DMA((len(records) + SUBS - 1,)),
        ),
        name="choose",
        far=True,
    )
    send = run(place_kernel, struct(TILES * 8, LANES), (chosen, target), name="place")
    received = lax.all_to_all(
        send.reshape(TILES, 8, LANES), "space", split_axis=0, concat_axis=0, tiled=True
    ).reshape(TILES * 8, LANES)
    below, down_edge, _ = lax.optimization_barrier((below, down_edge, send))
    own, mine, winds_below, lower_edge, forces_below = run(
        forward_local_kernel,
        (
            message(message_tiles(REACH + ROWS)),
            struct(ROWS + EXTRA, LEVELS, WIDTH),
            struct(WINDS * ROWS, LEVELS, WIDTH),
            struct(WINDS * ROWS, LEVELS, WIDTH),
            struct(SUBS * ROWS, LEVELS, WIDTH),
        ),
        (winds, forces, below, down_edge),
        name="forward_local",
    )
    before = moved(own, 1, 0)
    pair_shapes = (message(message_tiles(ROWS)), message(message_tiles(ROWS + EXTRA)))
    own, extended = run(
        forward_pair_kernel,
        pair_shapes,
        (winds, winds_below, lower_edge, mine, before),
        name="forward_pair",
    )
    pair = (moved(own, 2, 0), moved(extended, 2, 1))
    slots, stencil = run(
        stencil_kernel,
        (
            struct(SUBS, LANES, LANES),
            struct(SUBS, CHUNKS, HALF, CORNERS * LANES, dtype=bf16),
        ),
        (received,),
        scratch=(pltpu.VMEM((LANES, LANES), f32),),
        name="stencil",
    )
    size = PIECES * LEVELS
    sources, mine, response = run(
        forward_final_kernel,
        (
            struct(SUBS * ROWS, LEVELS, WIDTH),
            struct(DROP + ROWS, LEVELS, WIDTH),
            message(message_tiles(DROP + ROWS)),
        ),
        (
            winds, forces, winds_below, lower_edge, forces_below,
            before, *pair, slots, stencil, mixing,
        ),
        scratch=(
            pltpu.VMEM((SUBS, size, HALF), f32),
            pltpu.VMEM((SUBS, CHUNKS, 2 * size, CORNERS * LANES), f32),
            pltpu.VMEM((SUBS, CHUNKS, 2 * size, CORNERS * LANES), bf16),
        ),
        name="forward_final",
    )

    after = moved(response, -1, 0)
    own, extended = run(
        adjoint_pair_kernel,
        pair_shapes,
        (winds, winds_below, lower_edge, mine, after),
        name="adjoint_pair",
    )
    pair = (moved(own, -2, 0), moved(extended, -2, -1))
    part, pushed, pushed_far = run(
        adjoint_final_kernel,
        (
            struct(SUBS * ROWS, LEVELS, WIDTH),
            message(message_tiles(len(PUSHED))),
            message(message_tiles(len(PUSHED_FAR))),
        ),
        (sources, winds, winds_below, lower_edge, after, *pair),
        name="adjoint_final",
    )
    pushed = moved(pushed, 0, -1)
    pushed_far = moved(pushed_far, 0, -2)
    return run(
        finish_kernel,
        struct(SUBS, LEVELS, ROWS, WIDTH),
        (part, pushed, pushed_far),
        scratch=(
            pltpu.VMEM((SUBS, LEVELS, ROWS, WIDTH), f32),
            pltpu.SemaphoreType.DMA((SUBS,)),
        ),
        name="finish",
        far_out=True,
    )


def solution(mesh):
    return jax.shard_map(
        shards,
        mesh=mesh,
        in_specs=(
            P("tm", None, "space", None),
            P(None, None, "space", None),
            P("tm", None, "space"),
            P("tm", None, "space"),
            P("tm", None, "space"),
            P("tm", "space", None),
            P(),
            P(),
        ),
        out_specs=P("tm", None, "space", None),
        check_vma=False,
    )
```

```python
import jax
import jax.numpy as jnp
from jax import lax
from jax.experimental import pallas as pl
from jax.experimental.pallas import tpu as pltpu
from jax.sharding import PartitionSpec as P

LEVELS = 8
ROWS = 8
WIDTH = 512
SUBS = 3
TILES = 64
PARTS = 4
RECORDS = 256
CORNERS = 4
HALF = 256
PIECES = WIDTH // HALF * ROWS
CHUNKS = 8
LANES = 128

f32 = jnp.float32
bf16 = jnp.bfloat16
highest = lax.Precision.HIGHEST


def struct(*shape, dtype=f32):
    return jax.ShapeDtypeStruct(shape, dtype)


def split(value):
    top = value.astype(bf16)
    return top, (value - top.astype(f32)).astype(bf16)


LEVEL_TOP = 32766.0
SCALE_BITS = 22
SCALE_BIAS = 256
WIND_MIDDLE = 0.25
WIND_REACH = 0.21


def nearest(value):
    return jnp.floor(value + 0.5).astype(jnp.int32)


def join(first, second):
    return jnp.left_shift(first, 16) | (second & 0xFFFF)


def parted(both):
    return jnp.right_shift(both, 16), jnp.right_shift(jnp.left_shift(both, 16), 16)


def scale_of(code):
    exponent = (jnp.right_shift(code, SCALE_BITS) - SCALE_BIAS).astype(f32)
    mantissa = (code & ((1 << SCALE_BITS) - 1)).astype(f32) * (0.5 ** 20)
    return mantissa * jnp.exp2(exponent)


TILE_COLUMNS = WIDTH // LANES


def message_tiles(count):
    return count // 2 * TILE_COLUMNS + 1


def put_row(message, start, value):
    for part in range(TILE_COLUMNS):
        message[start + part] = value[:, part * LANES : (part + 1) * LANES]


def get_row(message, start):
    return jnp.concatenate([message[start + part] for part in range(TILE_COLUMNS)], axis=1)


def encode(values, message, start=0):
    count = len(values)
    lane = lax.broadcasted_iota(jnp.int32, (LEVELS, LANES), 1)
    largest = jnp.full((LEVELS, LANES), 1e-30, f32)
    for number, value in enumerate(values):
        top = jnp.max(jnp.abs(value), axis=1, keepdims=True)
        largest = jnp.where(lane == number, jnp.maximum(top, 1e-30), largest)
    exponent = jnp.floor(jnp.log2(largest))
    mantissa = (largest * jnp.exp2(-exponent) * 2.0 ** 20).astype(jnp.int32) + 16
    code = jnp.left_shift(exponent.astype(jnp.int32) + SCALE_BIAS, SCALE_BITS) + mantissa
    factor = LEVEL_TOP / scale_of(code)
    half = count // 2
    whole = [nearest(value * factor[:, n : n + 1]) for n, value in enumerate(values)]
    for number in range(half):
        put_row(message, start + number * TILE_COLUMNS, join(whole[number], whole[number + half]))
    message[start + half * TILE_COLUMNS] = code


def decode(message, count, start=0):
    half = count // 2
    factor = scale_of(message[start + half * TILE_COLUMNS]) * (1.0 / LEVEL_TOP)
    values = [None] * count
    for number in range(half):
        pair = parted(get_row(message, start + number * TILE_COLUMNS))
        for place, value in zip((number, number + half), pair):
            values[place] = value.astype(f32) * factor[:, place : place + 1]
    return values


def encode_wind(first, second):
    steps = LEVEL_TOP / WIND_REACH
    return join(nearest((first - WIND_MIDDLE) * steps), nearest((second - WIND_MIDDLE) * steps))


def decode_wind(both):
    step = WIND_REACH / LEVEL_TOP
    return [value.astype(f32) * step + WIND_MIDDLE for value in parted(both)]


def forward_step(current, wind_x, wind_y, low):
    result = {}
    for row in range(low + 1, ROWS):
        here = current[row]
        left = pltpu.roll(here, 1, 1)
        result[row] = (
            here - wind_x(row) * (here - left) - wind_y(row) * (here - current[row - 1])
        )
    return result


def adjoint_step(current, wind_x, wind_y, low):
    result = {low - 1: wind_y(low) * current[low]}
    for row in range(low, ROWS):
        here = current[row]
        along = wind_x(row)
        value = here * (1.0 - along - wind_y(row)) + pltpu.roll(along * here, WIDTH - 1, 1)
        if row + 1 < ROWS:
            value = value + wind_y(row + 1) * current[row + 1]
        result[row] = value
    return result


def forward_steps(current, winds, low, count):
    for _ in range(count):
        current = forward_step(current, winds[0], winds[1], low)
        low += 1
    return current, low


def adjoint_steps(current, winds, low, count):
    for _ in range(count):
        current = adjoint_step(current, winds[0], winds[1], low)
        low -= 1
    return current, low


WINDS = 2
FIELDS = WINDS + SUBS
RECORD_ARRAYS = 6
EXTRA = 4
REACH = 10
DROP = 6
DOWN_ROWS = [(sub, row) for sub in range(SUBS) for row in range(2 * sub, ROWS)]
WIND_TILES = ROWS * TILE_COLUMNS


def lower_winds(winds, winds_below, edge):
    def reader(field):
        def read(row):
            if row >= 0:
                return winds[field * ROWS + row]
            if row >= -ROWS:
                return winds_below[field * ROWS + row + ROWS]
            return edge[field * ROWS + row + 2 * ROWS]

        return read

    return [reader(field) for field in range(WINDS)]


def lower_forces(forces, forces_below, edge=None):
    def reader(sub):
        def read(row):
            if row >= 0:
                return forces[sub * ROWS + row]
            if row >= -ROWS:
                return forces_below[sub * ROWS + row + ROWS]
            return edge[sub, row + 2 * ROWS]

        return read

    return [reader(sub) for sub in range(SUBS)]


def add_rows(current, other, low, high):
    return {row: current[row] + other(row) for row in range(low, high)}


def fetch(pairs, sems):
    copies = [
        pltpu.make_async_copy(source, target, sems.at[number])
        for number, (source, target) in enumerate(pairs)
    ]
    for copy in copies:
        copy.start()
    return copies


def rows_kernel(*refs):
    forcing_far, courant_far, *records_far = refs[: 2 + RECORD_ARRAYS]
    winds, forces, below, down_edge, *records = refs[2 + RECORD_ARRAYS : 6 + 2 * RECORD_ARRAYS]
    forcing, courant, sems = refs[6 + 2 * RECORD_ARRAYS :]
    copies = fetch(
        [(courant_far.at[field], courant.at[field]) for field in range(WINDS)]
        + [(forcing_far.at[sub], forcing.at[sub]) for sub in range(SUBS)]
        + list(zip(records_far, records)),
        sems,
    )
    for copy in copies[:WINDS]:
        copy.wait()
    for field in range(WINDS):
        winds[pl.ds(field * ROWS, ROWS)] = jnp.swapaxes(courant[field], 0, 1)
    encode_winds(winds, range(ROWS), below, 0)
    encode_winds(winds, range(ROWS), down_edge, 0)
    rows = []
    for sub in range(SUBS):
        copies[WINDS + sub].wait()
        turned = jnp.swapaxes(forcing[sub], 0, 1)
        forces[pl.ds(sub * ROWS, ROWS)] = turned
        rows += [turned[row] for row in range(ROWS)]
    encode(rows, below, WIND_TILES)
    encode([rows[sub * ROWS + row] for sub, row in DOWN_ROWS], down_edge, WIND_TILES)
    for copy in copies[FIELDS:]:
        copy.wait()


def encode_winds(winds, rows, message, start):
    for number, row in enumerate(rows):
        both = encode_wind(winds[row], winds[ROWS + row])
        put_row(message, start + number * TILE_COLUMNS, both)


def unpack_winds(message, rows, result, start=0):
    for row in range(rows):
        first, second = decode_wind(get_row(message, start + row * TILE_COLUMNS))
        result[row] = first
        result[rows + row] = second


def three(value):
    top = value.astype(bf16)
    rest = value - top.astype(f32)
    middle = rest.astype(bf16)
    return top, middle, (rest - middle.astype(f32)).astype(bf16)


def pack_kernel(innovation, cells, weight, owner, channel_weight, rinv, send, mixing):
    sub_id = lax.broadcasted_iota(jnp.int32, (RECORDS, RECORDS), 0)
    lane_id = lax.broadcasted_iota(jnp.int32, (RECORDS, RECORDS), 1)
    not_later = lane_id <= sub_id

    scaled = channel_weight[...] * (rinv[...] * rinv[...])
    matrix = lax.dot_general(
        scaled, channel_weight[...], (((1,), (1,)), ((), ())),
        precision=highest, preferred_element_type=f32,
    )
    for level in range(LEVELS):
        mixing[level] = jnp.broadcast_to(matrix[:, level : level + 1], (LEVELS, LANES))
    scaled = jnp.concatenate(three(scaled), axis=0)

    spread_row = lax.broadcasted_iota(jnp.int32, (2 * LEVELS, LANES), 0)
    spread_lane = lax.broadcasted_iota(jnp.int32, (2 * LEVELS, LANES), 1)
    repeat = jnp.where(
        (spread_lane // 64 == spread_row // LEVELS) & (spread_lane % LEVELS == spread_row % LEVELS),
        1.0,
        0.0,
    ).astype(bf16)
    slot_lane = lax.broadcasted_iota(jnp.int32, (RECORDS, LANES), 1)
    slot_rank = ((slot_lane % 64) // LEVELS) * 2
    tile_id = lax.broadcasted_iota(jnp.int32, (TILES, RECORDS), 0)
    ones = jnp.ones((RECORDS, LANES), bf16)
    for sub in range(SUBS):
        parts = jnp.dot(scaled, innovation[sub], preferred_element_type=f32)
        projected = (parts[:LEVELS] + parts[LEVELS : 2 * LEVELS]) + parts[2 * LEVELS :]
        payload = jnp.concatenate(
            [cells[sub].astype(f32), weight[sub].astype(f32), projected], axis=0
        )
        owner_row = owner[sub]
        owner_rows = jnp.broadcast_to(owner_row, (RECORDS, RECORDS))
        earlier = jnp.where((owner_rows.T == owner_rows) & not_later, 1.0, 0.0).astype(bf16)
        rank = jnp.dot(earlier, ones, preferred_element_type=f32).astype(jnp.int32) - 1
        target = jnp.where(tile_id == owner_row, 1.0, 0.0).astype(bf16)
        repeated = [
            lax.dot_general(part, repeat, (((0,), (0,)), ((), ())), preferred_element_type=f32)
            for part in three(payload)
        ]
        for half in range(2):
            chosen = rank == slot_rank + half
            placed = [
                jnp.dot(
                    target, jnp.where(chosen, part, 0.0).astype(bf16), preferred_element_type=f32
                )
                for part in repeated
            ]
            send[pl.ds(2 * sub + half, TILES, stride=8), :] = (placed[0] + placed[1]) + placed[2]
    for spare in range(2 * SUBS, 8):
        send[pl.ds(spare, TILES, stride=8), :] = jnp.zeros((TILES, LANES), f32)


def stencil_kernel(received, slots, stencil, pieces):
    rows_id = lax.broadcasted_iota(jnp.int32, (HALF, LANES), 0)

    def one_sub(sub, _):
        for half in range(2):
            pieces[pl.ds(half * TILES, TILES), :] = received[
                pl.ds(2 * sub + half, TILES, stride=8), :
            ]
        slots[sub] = pieces[...].T
        for chunk in range(CHUNKS):
            record = slots[sub, pl.ds(chunk * LEVELS, LEVELS), :]
            column = record.astype(jnp.int32) & (HALF - 1)
            for corner in range(CORNERS):
                stencil[sub, chunk, :, corner * LANES : (corner + 1) * LANES] = jnp.where(
                    rows_id == column[corner : corner + 1],
                    record[CORNERS + corner : CORNERS + corner + 1],
                    0.0,
                ).astype(bf16)
        return 0

    lax.fori_loop(0, SUBS, one_sub, 0)


def respond(slots, mixing, sub, chunk, found, spread):
    size = PIECES * LEVELS
    record = slots[sub, pl.ds(chunk * LEVELS, LEVELS), :]
    adjoint = -slots[sub, pl.ds(TILES + chunk * LEVELS, LEVELS), :]
    piece = jnp.right_shift(record.astype(jnp.int32), 8)
    sums = []
    wanted = []
    for corner in range(CORNERS):
        wanted.append(jnp.broadcast_to(piece[corner : corner + 1], (LEVELS, LANES)))
        part = pl.ds(corner * LANES, LANES)
        value = None
        for number in range(PIECES):
            both = (
                found[sub, chunk, pl.ds(number * LEVELS, LEVELS), part]
                + found[sub, chunk, pl.ds(size + number * LEVELS, LEVELS), part]
            )
            value = both if value is None else jnp.where(wanted[corner] == number, both, value)
        sums.append(value)
    values = (sums[0] + sums[1]) + (sums[2] + sums[3])
    for level in range(LEVELS):
        adjoint = adjoint + mixing[level] * values[level : level + 1]
    sources = [part.astype(f32) for part in split(adjoint)]
    for corner in range(CORNERS):
        part = pl.ds(corner * LANES, LANES)
        for place, source in enumerate(sources):
            spread[sub, chunk, pl.ds(place * size, size), part] = jnp.concatenate(
                [jnp.where(wanted[corner] == number, source, 0.0) for number in range(PIECES)],
                axis=0,
            ).astype(bf16)


def interpolate(state, stencil, sub, found):
    left = jnp.concatenate(split(state), axis=0)
    for chunk in range(CHUNKS):
        found[sub, chunk] = jnp.dot(left, stencil[sub, chunk], preferred_element_type=f32)


def scatter(slots, stencil, mixing, sub, found, spread):
    size = PIECES * LEVELS
    for chunk in range(CHUNKS):
        respond(slots, mixing, sub, chunk, found, spread)
    total = jnp.zeros((2 * size, HALF), f32)
    for chunk in range(CHUNKS):
        total = total + lax.dot_general(
            spread[sub, chunk], stencil[sub, chunk], (((1,), (1,)), ((), ())),
            preferred_element_type=f32,
        )
    return total[:size] + total[size:]


def stacked(rows):
    return jnp.concatenate(
        [rows[row][:, half * HALF : (half + 1) * HALF] for row in range(ROWS) for half in range(2)],
        axis=0,
    )


def unstacked(stack, row):
    places = [(2 * row + half) * LEVELS for half in range(2)]
    return jnp.concatenate([stack[place : place + LEVELS] for place in places], axis=1)


def forward_local_kernel(
    winds, forces, below, down_edge, own, mine, winds_below, lower_edge, forces_below
):
    unpack_winds(below, ROWS, winds_below)
    unpack_winds(down_edge, ROWS, lower_edge)
    for number, row in enumerate(decode(below, SUBS * ROWS, WIND_TILES)):
        forces_below[number] = row
    edge = dict(zip(DOWN_ROWS, decode(down_edge, len(DOWN_ROWS), WIND_TILES)))
    across = lower_winds(winds, winds_below, lower_edge)
    forced = lower_forces(forces, forces_below, edge)
    low = -2 * ROWS
    current = {row: forced[0](row) for row in range(low, ROWS)}
    current, low = forward_steps(current, across, low, 2)
    for sub in range(1, SUBS):
        current = add_rows(current, forced[sub], low, ROWS)
        current, low = forward_steps(current, across, low, 2)
    listed = [current[row] for row in range(-REACH, ROWS)]
    for number, row in enumerate(listed):
        mine[number] = row
    encode(listed, own)


def time_is(condition):
    index = jnp.full((LEVELS, WIDTH), lax.axis_index("tm"), jnp.int32)
    return condition(index)


def lower_state(own, extended):
    here = decode(own, ROWS)
    under = decode(extended, ROWS + EXTRA)
    return {
        row: here[row] if row >= 0 else under[row + ROWS + EXTRA]
        for row in range(-(ROWS + EXTRA), ROWS)
    }


def forward_pair_kernel(winds, winds_below, lower_edge, mine, other, own, extended):
    @pl.when(lax.axis_index("tm") < 2)
    def _():
        across = lower_winds(winds, winds_below, lower_edge)
        first = time_is(lambda index: index == 0)
        rows = decode(other, REACH + ROWS)
        current = {
            row: jnp.where(first, mine[row + REACH], rows[row + REACH])
            for row in range(-REACH, ROWS)
        }
        current, low = forward_steps(current, across, -REACH, 6)
        listed = [
            current[row] + jnp.where(first, rows[row + REACH], mine[row + REACH])
            for row in range(-EXTRA, ROWS)
        ]
        encode(listed[EXTRA:], own)
        encode(listed, extended)


def forward_final_kernel(
    winds, forces, winds_below, lower_edge, forces_below,
    before, pair_own, pair_extended, slots, stencil, mixing,
    sources, mine, response,
    found, spread,
):
    across = lower_winds(winds, winds_below, lower_edge)
    forced = lower_forces(forces, forces_below)
    half_way = lower_state(pair_own, pair_extended)
    current, low = forward_steps(half_way, across, -(ROWS + EXTRA), 6)
    before = decode(before, REACH + ROWS)
    third = time_is(lambda index: index == 2)
    odd = time_is(lambda index: (index & 1) == 1)
    current = {
        row: jnp.where(third, half_way[row], value) + jnp.where(odd, before[row + REACH], 0.0)
        for row, value in current.items()
    }
    for sub in range(SUBS):
        current = add_rows(current, forced[sub], low, ROWS)
        current, low = forward_steps(current, across, low, 2)
        interpolate(stacked(current), stencil, sub, found)
    current, low = {}, 0
    for sub in reversed(range(SUBS)):
        stack = scatter(slots, stencil, mixing, sub, found, spread)
        for row in range(ROWS):
            value = unstacked(stack, row)
            sources[sub * ROWS + row] = value
            current[row] = current[row] + value if row in current else value
        current, low = adjoint_steps(current, across, low, 2)
    listed = [current[row] for row in range(low, ROWS)]
    for number, row in enumerate(listed):
        mine[number] = row
    encode(listed, response)


def add_sources(current, sources, sub):
    return {
        row: value + sources[sub * ROWS + row] if row >= 0 else value
        for row, value in current.items()
    }


def adjoint_pair_kernel(winds, winds_below, lower_edge, mine, other, own, extended):
    @pl.when(lax.axis_index("tm") >= 2)
    def _():
        across = lower_winds(winds, winds_below, lower_edge)
        last = time_is(lambda index: index == 3)
        rows = decode(other, DROP + ROWS)
        current = {
            row: jnp.where(last, mine[row + DROP], rows[row + DROP]) for row in range(-DROP, ROWS)
        }
        current, low = adjoint_steps(current, across, -DROP, 6)
        for row in range(-DROP, ROWS):
            current[row] = current[row] + jnp.where(last, rows[row + DROP], mine[row + DROP])
        encode([current[row] for row in range(ROWS)], own)
        encode([current[row] for row in range(low, 0)], extended)


PUSHED = [(sub, row) for sub in range(SUBS) for row in range(ROWS)]
PUSHED_FAR = [(sub, row) for sub in range(SUBS) for row in range(2 * sub, ROWS)]


def adjoint_final_kernel(
    sources, winds, winds_below, lower_edge, after, pair_own, pair_extended,
    gradient, pushed, pushed_far,
):
    across = lower_winds(winds, winds_below, lower_edge)
    own = decode(pair_own, ROWS)
    above = decode(pair_extended, ROWS + EXTRA)
    low = -EXTRA
    half_way = {
        row: above[row + EXTRA] + own[row] if row >= 0 else above[row + EXTRA]
        for row in range(low, ROWS)
    }
    current, low = adjoint_steps(half_way, across, low, 6)
    after = decode(after, DROP + ROWS)
    second = time_is(lambda index: index == 1)
    even = time_is(lambda index: (index & 1) == 0)
    for row in current:
        current[row] = jnp.where(second, half_way.get(row, 0.0), current[row])
        if row >= -DROP:
            current[row] = current[row] + jnp.where(even, after[row + DROP], 0.0)
    results = [None] * SUBS
    for sub in reversed(range(SUBS)):
        current = add_sources(current, sources, sub)
        current, low = adjoint_steps(current, across, low, 2)
        results[sub] = current
        for row in range(ROWS):
            gradient[sub * ROWS + row] = current[row]
    encode([results[sub][row - ROWS] for sub, row in PUSHED], pushed)
    encode([results[sub][row - 2 * ROWS] for sub, row in PUSHED_FAR], pushed_far)


def finish_kernel(part, pushed, pushed_far, gradient_far, gradient, sems):
    near = dict(zip(PUSHED, decode(pushed, len(PUSHED))))
    far = dict(zip(PUSHED_FAR, decode(pushed_far, len(PUSHED_FAR))))
    copies = []
    for sub in range(SUBS):
        rows = []
        for row in range(ROWS):
            value = part[sub * ROWS + row] + near[sub, row]
            rows.append(value + far[sub, row] if (sub, row) in far else value)
        gradient[sub] = jnp.swapaxes(jnp.stack(rows), 0, 1)
        copies.append(
            pltpu.make_async_copy(gradient.at[sub], gradient_far.at[sub], sems.at[sub])
        )
        copies[-1].start()
    for copy in copies:
        copy.wait()


def run(kernel, outputs, arguments, scratch=(), name=None, flops=2_000_000, far=False, far_out=False):
    size = sum(a.size * a.dtype.itemsize for a in arguments)
    place = pltpu.HBM if far else pltpu.VMEM
    if far:
        arguments = [pltpu.with_memory_space_constraint(a, pltpu.HBM) for a in arguments]
    return pl.pallas_call(
        kernel,
        out_shape=outputs,
        in_specs=[pl.BlockSpec(memory_space=place)] * len(arguments),
        **({"out_specs": pl.BlockSpec(memory_space=pltpu.HBM)} if far_out else {}),
        scratch_shapes=scratch,
        compiler_params=pltpu.CompilerParams(vmem_limit_bytes=40 * 1024 * 1024),
        cost_estimate=pl.CostEstimate(flops=flops, bytes_accessed=size, transcendentals=0),
        name=name,
    )(*arguments)


STAY = {part: part for part in range(PARTS)}
FORWARD_FIRST, FORWARD_SECOND = {0: 1, 1: 0, 2: 3}, {1: 2, 0: 3}
ADJOINT_FIRST, ADJOINT_SECOND = {3: 2, 2: 3, 1: 0}, {2: 1, 3: 0}


def moved(array, parts, tiles):
    pairs = [
        (part * TILES + tile, to_part * TILES + tile + tiles)
        for part, to_part in parts.items()
        for tile in range(TILES)
        if 0 <= tile + tiles < TILES
    ]
    return lax.ppermute(array, ("tm", "space"), pairs)


def shards(
    forcing, courant, innovation, obs_cells, obs_weight, obs_owner, channel_weight, channel_rinv
):
    def message(tiles):
        return struct(tiles, LEVELS, LANES, dtype=jnp.int32)

    records = (
        innovation, obs_cells, obs_weight, jnp.swapaxes(obs_owner, 1, 2),
        channel_weight.T, channel_rinv.reshape(1, -1),
    )
    winds, forces, below, down_edge, *records = run(
        rows_kernel,
        (
            struct(WINDS * ROWS, LEVELS, WIDTH),
            struct(SUBS * ROWS, LEVELS, WIDTH),
            message(WIND_TILES + message_tiles(SUBS * ROWS)),
            message(WIND_TILES + message_tiles(len(DOWN_ROWS))),
            *[struct(*array.shape, dtype=array.dtype) for array in records],
        ),
        (forcing, courant, *records),
        scratch=(
            pltpu.VMEM(forcing.shape, f32),
            pltpu.VMEM(courant.shape, f32),
            pltpu.SemaphoreType.DMA((FIELDS + RECORD_ARRAYS,)),
        ),
        name="rows",
        far=True,
    )
    below = moved(below, STAY, 1)
    down_edge = moved(down_edge, STAY, 2)
    send, mixing = run(
        pack_kernel,
        (struct(TILES * 8, LANES), struct(LEVELS, LEVELS, LANES)),
        records,
        name="pack",
    )
    received = lax.all_to_all(
        send.reshape(TILES, 8, LANES), "space", split_axis=0, concat_axis=0, tiled=True
    ).reshape(TILES * 8, LANES)
    below, down_edge, _ = lax.optimization_barrier((below, down_edge, send))
    own, mine, winds_below, lower_edge, forces_below = run(
        forward_local_kernel,
        (
            message(message_tiles(REACH + ROWS)),
            struct(REACH + ROWS, LEVELS, WIDTH),
            struct(WINDS * ROWS, LEVELS, WIDTH),
            struct(WINDS * ROWS, LEVELS, WIDTH),
            struct(SUBS * ROWS, LEVELS, WIDTH),
        ),
        (winds, forces, below, down_edge),
        name="forward_local",
    )
    before = moved(own, FORWARD_FIRST, 0)
    pair_shapes = (message(message_tiles(ROWS)), message(message_tiles(ROWS + EXTRA)))
    own, extended = run(
        forward_pair_kernel,
        pair_shapes,
        (winds, winds_below, lower_edge, mine, before),
        name="forward_pair",
    )
    pair = (moved(own, FORWARD_SECOND, 0), moved(extended, FORWARD_SECOND, 1))
    slots, stencil = run(
        stencil_kernel,
        (
            struct(SUBS, LANES, LANES),
            struct(SUBS, CHUNKS, HALF, CORNERS * LANES, dtype=bf16),
        ),
        (received,),
        scratch=(pltpu.VMEM((LANES, LANES), f32),),
        name="stencil",
    )
    size = PIECES * LEVELS
    sources, mine, response = run(
        forward_final_kernel,
        (
            struct(SUBS * ROWS, LEVELS, WIDTH),
            struct(DROP + ROWS, LEVELS, WIDTH),
            message(message_tiles(DROP + ROWS)),
        ),
        (
            winds, forces, winds_below, lower_edge, forces_below,
            before, *pair, slots, stencil, mixing,
        ),
        scratch=(
            pltpu.VMEM((SUBS, CHUNKS, 2 * size, CORNERS * LANES), f32),
            pltpu.VMEM((SUBS, CHUNKS, 2 * size, CORNERS * LANES), bf16),
        ),
        name="forward_final",
    )

    after = moved(response, ADJOINT_FIRST, 0)
    own, extended = run(
        adjoint_pair_kernel,
        pair_shapes,
        (winds, winds_below, lower_edge, mine, after),
        name="adjoint_pair",
    )
    pair = (moved(own, ADJOINT_SECOND, 0), moved(extended, ADJOINT_SECOND, -1))
    part, pushed, pushed_far = run(
        adjoint_final_kernel,
        (
            struct(SUBS * ROWS, LEVELS, WIDTH),
            message(message_tiles(len(PUSHED))),
            message(message_tiles(len(PUSHED_FAR))),
        ),
        (sources, winds, winds_below, lower_edge, after, *pair),
        name="adjoint_final",
    )
    pushed = moved(pushed, STAY, -1)
    pushed_far = moved(pushed_far, STAY, -2)
    return run(
        finish_kernel,
        struct(SUBS, LEVELS, ROWS, WIDTH),
        (part, pushed, pushed_far),
        scratch=(
            pltpu.VMEM((SUBS, LEVELS, ROWS, WIDTH), f32),
            pltpu.SemaphoreType.DMA((SUBS,)),
        ),
        name="finish",
        far_out=True,
    )


def solution(mesh):
    return jax.shard_map(
        shards,
        mesh=mesh,
        in_specs=(
            P("tm", None, "space", None),
            P(None, None, "space", None),
            P("tm", None, "space"),
            P("tm", None, "space"),
            P("tm", None, "space"),
            P("tm", "space", None),
            P(),
            P(),
        ),
        out_specs=P("tm", None, "space", None),
        check_vma=False,
    )
```

```python
import jax
import jax.numpy as jnp
from jax import lax
from jax.experimental import pallas as pl
from jax.experimental.pallas import tpu as pltpu
from jax.sharding import PartitionSpec as P

LEVELS = 8
ROWS = 8
WIDTH = 512
SUBS = 3
TILES = 64
PARTS = 4
RECORDS = 256
CORNERS = 4
HALF = 256
PIECES = WIDTH // HALF * ROWS
CHUNKS = 8
LANES = 128

f32 = jnp.float32
bf16 = jnp.bfloat16
highest = lax.Precision.HIGHEST


def struct(*shape, dtype=f32):
    return jax.ShapeDtypeStruct(shape, dtype)


def split(value):
    top = value.astype(bf16)
    return top, (value - top.astype(f32)).astype(bf16)


LEVEL_TOP = 32766.0
SCALE_BITS = 22
SCALE_BIAS = 256
WIND_MIDDLE = 0.25
WIND_REACH = 0.21


def nearest(value):
    return jnp.floor(value + 0.5).astype(jnp.int32)


def join(first, second):
    return jnp.left_shift(first, 16) | (second & 0xFFFF)


def parted(both):
    return jnp.right_shift(both, 16), jnp.right_shift(jnp.left_shift(both, 16), 16)


def scale_of(code):
    exponent = (jnp.right_shift(code, SCALE_BITS) - SCALE_BIAS).astype(f32)
    mantissa = (code & ((1 << SCALE_BITS) - 1)).astype(f32) * (0.5 ** 20)
    return mantissa * jnp.exp2(exponent)


TILE_COLUMNS = WIDTH // LANES


def message_tiles(count):
    return count // 2 * TILE_COLUMNS + 1


def put_row(message, start, value):
    for part in range(TILE_COLUMNS):
        message[start + part] = value[:, part * LANES : (part + 1) * LANES]


def get_row(message, start):
    return jnp.concatenate([message[start + part] for part in range(TILE_COLUMNS)], axis=1)


def encode(values, message, start=0):
    count = len(values)
    lane = lax.broadcasted_iota(jnp.int32, (LEVELS, LANES), 1)
    largest = jnp.full((LEVELS, LANES), 1e-30, f32)
    for number, value in enumerate(values):
        top = jnp.max(jnp.abs(value), axis=1, keepdims=True)
        largest = jnp.where(lane == number, jnp.maximum(top, 1e-30), largest)
    exponent = jnp.floor(jnp.log2(largest))
    mantissa = (largest * jnp.exp2(-exponent) * 2.0 ** 20).astype(jnp.int32) + 16
    code = jnp.left_shift(exponent.astype(jnp.int32) + SCALE_BIAS, SCALE_BITS) + mantissa
    factor = LEVEL_TOP / scale_of(code)
    half = count // 2
    whole = [nearest(value * factor[:, n : n + 1]) for n, value in enumerate(values)]
    for number in range(half):
        put_row(message, start + number * TILE_COLUMNS, join(whole[number], whole[number + half]))
    message[start + half * TILE_COLUMNS] = code


def decode(message, count, start=0):
    half = count // 2
    factor = scale_of(message[start + half * TILE_COLUMNS]) * (1.0 / LEVEL_TOP)
    values = [None] * count
    for number in range(half):
        pair = parted(get_row(message, start + number * TILE_COLUMNS))
        for place, value in zip((number, number + half), pair):
            values[place] = value.astype(f32) * factor[:, place : place + 1]
    return values


def encode_wind(first, second):
    steps = LEVEL_TOP / WIND_REACH
    return join(nearest((first - WIND_MIDDLE) * steps), nearest((second - WIND_MIDDLE) * steps))


def decode_wind(both):
    step = WIND_REACH / LEVEL_TOP
    return [value.astype(f32) * step + WIND_MIDDLE for value in parted(both)]


def forward_step(current, wind_x, wind_y, low):
    result = {}
    for row in range(low + 1, ROWS):
        here = current[row]
        left = pltpu.roll(here, 1, 1)
        result[row] = (
            here - wind_x(row) * (here - left) - wind_y(row) * (here - current[row - 1])
        )
    return result


def adjoint_step(current, wind_x, wind_y, low):
    result = {}
    carried = None
    for row in reversed(range(low, ROWS)):
        here = current[row]
        along, across = wind_x(row) * here, wind_y(row) * here
        value = (here - along) + (pltpu.roll(along, WIDTH - 1, 1) - across)
        result[row] = value if carried is None else value + carried
        carried = across
    result[low - 1] = carried
    return result


def forward_steps(current, winds, low, count):
    for _ in range(count):
        current = forward_step(current, winds[0], winds[1], low)
        low += 1
    return current, low


def adjoint_steps(current, winds, low, count):
    for _ in range(count):
        current = adjoint_step(current, winds[0], winds[1], low)
        low -= 1
    return current, low


WINDS = 2
FIELDS = WINDS + SUBS
RECORD_ARRAYS = 6
EXTRA = 4
REACH = 10
DROP = 6
DOWN_ROWS = [(sub, row) for sub in range(SUBS) for row in range(2 * sub, ROWS)]
WIND_TILES = ROWS * TILE_COLUMNS


def lower_winds(winds, winds_below, edge):
    def reader(field):
        def read(row):
            if row >= 0:
                return winds[field * ROWS + row]
            if row >= -ROWS:
                return winds_below[field * ROWS + row + ROWS]
            return edge[field * ROWS + row + 2 * ROWS]

        return read

    return [reader(field) for field in range(WINDS)]


def lower_forces(forces, forces_below, edge=None):
    def reader(sub):
        def read(row):
            if row >= 0:
                return forces[sub * ROWS + row]
            if row >= -ROWS:
                return forces_below[sub * ROWS + row + ROWS]
            return edge[sub, row + 2 * ROWS]

        return read

    return [reader(sub) for sub in range(SUBS)]


def add_rows(current, other, low, high):
    return {row: current[row] + other(row) for row in range(low, high)}


def fetch(pairs, sems):
    copies = [
        pltpu.make_async_copy(source, target, sems.at[number])
        for number, (source, target) in enumerate(pairs)
    ]
    for copy in copies:
        copy.start()
    return copies


def rows_kernel(*refs):
    forcing_far, courant_far, *records_far = refs[: 2 + RECORD_ARRAYS]
    winds, forces, below, down_edge, *records = refs[2 + RECORD_ARRAYS : 6 + 2 * RECORD_ARRAYS]
    forcing, courant, sems = refs[6 + 2 * RECORD_ARRAYS :]
    copies = fetch(
        [(courant_far.at[field], courant.at[field]) for field in range(WINDS)]
        + [(forcing_far.at[sub], forcing.at[sub]) for sub in range(SUBS)]
        + list(zip(records_far, records)),
        sems,
    )
    for copy in copies[:WINDS]:
        copy.wait()
    for field in range(WINDS):
        winds[pl.ds(field * ROWS, ROWS)] = jnp.swapaxes(courant[field], 0, 1)
    encode_winds(winds, range(ROWS), below, 0)
    encode_winds(winds, range(ROWS), down_edge, 0)
    rows = []
    for sub in range(SUBS):
        copies[WINDS + sub].wait()
        turned = jnp.swapaxes(forcing[sub], 0, 1)
        forces[pl.ds(sub * ROWS, ROWS)] = turned
        rows += [turned[row] for row in range(ROWS)]
    encode(rows, below, WIND_TILES)
    encode([rows[sub * ROWS + row] for sub, row in DOWN_ROWS], down_edge, WIND_TILES)
    for copy in copies[FIELDS:]:
        copy.wait()


def encode_winds(winds, rows, message, start):
    for number, row in enumerate(rows):
        both = encode_wind(winds[row], winds[ROWS + row])
        put_row(message, start + number * TILE_COLUMNS, both)


def unpack_winds(message, rows, result, start=0):
    for row in range(rows):
        first, second = decode_wind(get_row(message, start + row * TILE_COLUMNS))
        result[row] = first
        result[rows + row] = second


def three(value):
    top = value.astype(bf16)
    rest = value - top.astype(f32)
    middle = rest.astype(bf16)
    return top, middle, (rest - middle.astype(f32)).astype(bf16)


def pack_kernel(innovation, cells, weight, owner, channel_weight, rinv, send):
    sub_id = lax.broadcasted_iota(jnp.int32, (RECORDS, RECORDS), 0)
    lane_id = lax.broadcasted_iota(jnp.int32, (RECORDS, RECORDS), 1)
    not_later = lane_id <= sub_id

    scaled = jnp.concatenate(three(channel_weight[...] * (rinv[...] * rinv[...])), axis=0)

    spread_row = lax.broadcasted_iota(jnp.int32, (2 * LEVELS, LANES), 0)
    spread_lane = lax.broadcasted_iota(jnp.int32, (2 * LEVELS, LANES), 1)
    repeat = jnp.where(
        (spread_lane // 64 == spread_row // LEVELS) & (spread_lane % LEVELS == spread_row % LEVELS),
        1.0,
        0.0,
    ).astype(bf16)
    slot_lane = lax.broadcasted_iota(jnp.int32, (RECORDS, LANES), 1)
    slot_rank = ((slot_lane % 64) // LEVELS) * 2
    tile_id = lax.broadcasted_iota(jnp.int32, (TILES, RECORDS), 0)
    ones = jnp.ones((RECORDS, LANES), bf16)
    for sub in range(SUBS):
        parts = jnp.dot(scaled, innovation[sub], preferred_element_type=f32)
        projected = (parts[:LEVELS] + parts[LEVELS : 2 * LEVELS]) + parts[2 * LEVELS :]
        payload = jnp.concatenate(
            [cells[sub].astype(f32), weight[sub].astype(f32), projected], axis=0
        )
        owner_row = owner[sub]
        owner_rows = jnp.broadcast_to(owner_row, (RECORDS, RECORDS))
        earlier = jnp.where((owner_rows.T == owner_rows) & not_later, 1.0, 0.0).astype(bf16)
        rank = jnp.dot(earlier, ones, preferred_element_type=f32).astype(jnp.int32) - 1
        target = jnp.where(tile_id == owner_row, 1.0, 0.0).astype(bf16)
        repeated = [
            lax.dot_general(part, repeat, (((0,), (0,)), ((), ())), preferred_element_type=f32)
            for part in three(payload)
        ]
        for half in range(2):
            chosen = rank == slot_rank + half
            placed = [
                jnp.dot(
                    target, jnp.where(chosen, part, 0.0).astype(bf16), preferred_element_type=f32
                )
                for part in repeated
            ]
            send[pl.ds(2 * sub + half, TILES, stride=8), :] = (placed[0] + placed[1]) + placed[2]
    for spare in range(2 * SUBS, 8):
        send[pl.ds(spare, TILES, stride=8), :] = jnp.zeros((TILES, LANES), f32)


def stencil_kernel(received, channel_weight, rinv, slots, stencil, mixing, pieces):
    matrix = lax.dot_general(
        channel_weight[...] * (rinv[...] * rinv[...]), channel_weight[...],
        (((1,), (1,)), ((), ())), precision=highest, preferred_element_type=f32,
    )
    for level in range(LEVELS):
        mixing[level] = jnp.broadcast_to(matrix[:, level : level + 1], (LEVELS, LANES))
    rows_id = lax.broadcasted_iota(jnp.int32, (HALF, LANES), 0)

    def one_sub(sub, _):
        for half in range(2):
            pieces[pl.ds(half * TILES, TILES), :] = received[
                pl.ds(2 * sub + half, TILES, stride=8), :
            ]
        slots[sub] = pieces[...].T
        for chunk in range(CHUNKS):
            record = slots[sub, pl.ds(chunk * LEVELS, LEVELS), :]
            column = record.astype(jnp.int32) & (HALF - 1)
            for corner in range(CORNERS):
                stencil[sub, chunk, :, corner * LANES : (corner + 1) * LANES] = jnp.where(
                    rows_id == column[corner : corner + 1],
                    record[CORNERS + corner : CORNERS + corner + 1],
                    0.0,
                ).astype(bf16)
        return 0

    lax.fori_loop(0, SUBS, one_sub, 0)


def respond(slots, mixing, sub, chunk, found, spread):
    size = PIECES * LEVELS
    record = slots[sub, pl.ds(chunk * LEVELS, LEVELS), :]
    adjoint = -slots[sub, pl.ds(TILES + chunk * LEVELS, LEVELS), :]
    piece = jnp.right_shift(record.astype(jnp.int32), 8)
    sums = []
    wanted = []
    for corner in range(CORNERS):
        wanted.append(jnp.broadcast_to(piece[corner : corner + 1], (LEVELS, LANES)))
        part = pl.ds(corner * LANES, LANES)
        value = None
        for number in range(PIECES):
            both = (
                found[sub, chunk, pl.ds(number * LEVELS, LEVELS), part]
                + found[sub, chunk, pl.ds(size + number * LEVELS, LEVELS), part]
            )
            value = both if value is None else jnp.where(wanted[corner] == number, both, value)
        sums.append(value)
    values = (sums[0] + sums[1]) + (sums[2] + sums[3])
    for level in range(LEVELS):
        adjoint = adjoint + mixing[level] * values[level : level + 1]
    sources = [part.astype(f32) for part in split(adjoint)]
    for corner in range(CORNERS):
        part = pl.ds(corner * LANES, LANES)
        for place, source in enumerate(sources):
            spread[sub, chunk, pl.ds(place * size, size), part] = jnp.concatenate(
                [jnp.where(wanted[corner] == number, source, 0.0) for number in range(PIECES)],
                axis=0,
            ).astype(bf16)


def interpolate(state, stencil, sub, found):
    left = jnp.concatenate(split(state), axis=0)
    for chunk in range(CHUNKS):
        found[sub, chunk] = jnp.dot(left, stencil[sub, chunk], preferred_element_type=f32)


def scatter(slots, stencil, mixing, sub, found, spread):
    size = PIECES * LEVELS
    for chunk in range(CHUNKS):
        respond(slots, mixing, sub, chunk, found, spread)
    total = jnp.zeros((2 * size, HALF), f32)
    for chunk in range(CHUNKS):
        total = total + lax.dot_general(
            spread[sub, chunk], stencil[sub, chunk], (((1,), (1,)), ((), ())),
            preferred_element_type=f32,
        )
    return total[:size] + total[size:]


def stacked(rows):
    return jnp.concatenate(
        [rows[row][:, half * HALF : (half + 1) * HALF] for row in range(ROWS) for half in range(2)],
        axis=0,
    )


def unstacked(stack, row):
    places = [(2 * row + half) * LEVELS for half in range(2)]
    return jnp.concatenate([stack[place : place + LEVELS] for place in places], axis=1)


def forward_local_kernel(
    winds, forces, below, down_edge, own, mine, winds_below, lower_edge, forces_below
):
    unpack_winds(below, ROWS, winds_below)
    unpack_winds(down_edge, ROWS, lower_edge)
    for number, row in enumerate(decode(below, SUBS * ROWS, WIND_TILES)):
        forces_below[number] = row
    edge = dict(zip(DOWN_ROWS, decode(down_edge, len(DOWN_ROWS), WIND_TILES)))
    across = lower_winds(winds, winds_below, lower_edge)
    forced = lower_forces(forces, forces_below, edge)
    low = -2 * ROWS
    current = {row: forced[0](row) for row in range(low, ROWS)}
    current, low = forward_steps(current, across, low, 2)
    for sub in range(1, SUBS):
        current = add_rows(current, forced[sub], low, ROWS)
        current, low = forward_steps(current, across, low, 2)
    listed = [current[row] for row in range(-REACH, ROWS)]
    for number, row in enumerate(listed):
        mine[number] = row
    encode(listed[REACH - DROP :], own)


def time_is(condition):
    index = jnp.full((LEVELS, WIDTH), lax.axis_index("tm"), jnp.int32)
    return condition(index)


def lower_state(own, extended):
    here = decode(own, ROWS)
    under = decode(extended, ROWS + EXTRA)
    return {
        row: here[row] if row >= 0 else under[row + ROWS + EXTRA]
        for row in range(-(ROWS + EXTRA), ROWS)
    }


def forward_pair_kernel(winds, winds_below, lower_edge, mine, other, own, extended):
    @pl.when(lax.axis_index("tm") < 2)
    def _():
        across = lower_winds(winds, winds_below, lower_edge)
        first = time_is(lambda index: index == 0)
        rows = dict(zip(range(-DROP, ROWS), decode(other, DROP + ROWS)))
        current = {
            row: jnp.where(first, mine[row + REACH], rows.get(row, 0.0))
            for row in range(-REACH, ROWS)
        }
        current, low = forward_steps(current, across, -REACH, 6)
        listed = [
            current[row] + jnp.where(first, rows[row], mine[row + REACH])
            for row in range(-EXTRA, ROWS)
        ]
        encode(listed[EXTRA:], own)
        encode(listed, extended)


def forward_final_kernel(
    winds, forces, winds_below, lower_edge, forces_below,
    before, pair_own, pair_extended, slots, stencil, mixing,
    sources, mine, response,
    found, spread,
):
    across = lower_winds(winds, winds_below, lower_edge)
    forced = lower_forces(forces, forces_below)
    half_way = lower_state(pair_own, pair_extended)
    current, low = forward_steps(half_way, across, -(ROWS + EXTRA), 6)
    before = decode(before, DROP + ROWS)
    third = time_is(lambda index: index == 2)
    odd = time_is(lambda index: (index & 1) == 1)
    current = {
        row: jnp.where(third, half_way[row], value) + jnp.where(odd, before[row + DROP], 0.0)
        for row, value in current.items()
    }
    for sub in range(SUBS):
        current = add_rows(current, forced[sub], low, ROWS)
        current, low = forward_steps(current, across, low, 2)
        interpolate(stacked(current), stencil, sub, found)
    current, low = {}, 0
    for sub in reversed(range(SUBS)):
        stack = scatter(slots, stencil, mixing, sub, found, spread)
        for row in range(ROWS):
            value = unstacked(stack, row)
            sources[sub * ROWS + row] = value
            current[row] = current[row] + value if row in current else value
        current, low = adjoint_steps(current, across, low, 2)
    listed = [current[row] for row in range(low, ROWS)]
    for number, row in enumerate(listed):
        mine[number] = row
    encode(listed, response)


def add_sources(current, sources, sub):
    return {
        row: value + sources[sub * ROWS + row] if row >= 0 else value
        for row, value in current.items()
    }


def adjoint_pair_kernel(winds, winds_below, lower_edge, mine, other, own, extended):
    @pl.when(lax.axis_index("tm") >= 2)
    def _():
        across = lower_winds(winds, winds_below, lower_edge)
        last = time_is(lambda index: index == 3)
        rows = decode(other, DROP + ROWS)
        current = {
            row: jnp.where(last, mine[row + DROP], rows[row + DROP]) for row in range(-DROP, ROWS)
        }
        current, low = adjoint_steps(current, across, -DROP, 6)
        for row in range(-DROP, ROWS):
            current[row] = current[row] + jnp.where(last, rows[row + DROP], mine[row + DROP])
        encode([current[row] for row in range(ROWS)], own)
        encode([current[row] for row in range(low, 0)], extended)


PUSHED = [(sub, row) for sub in range(SUBS) for row in range(ROWS)]
PUSHED_FAR = [(sub, row) for sub in range(SUBS) for row in range(2 * sub, ROWS)]


def adjoint_final_kernel(
    sources, winds, winds_below, lower_edge, after, pair_own, pair_extended,
    gradient, pushed, pushed_far,
):
    across = lower_winds(winds, winds_below, lower_edge)
    own = decode(pair_own, ROWS)
    above = decode(pair_extended, ROWS + EXTRA)
    low = -EXTRA
    half_way = {
        row: above[row + EXTRA] + own[row] if row >= 0 else above[row + EXTRA]
        for row in range(low, ROWS)
    }
    current, low = adjoint_steps(half_way, across, low, 6)
    after = decode(after, DROP + ROWS)
    second = time_is(lambda index: index == 1)
    even = time_is(lambda index: (index & 1) == 0)
    for row in current:
        current[row] = jnp.where(second, half_way.get(row, 0.0), current[row])
        if row >= -DROP:
            current[row] = current[row] + jnp.where(even, after[row + DROP], 0.0)
    results = [None] * SUBS
    for sub in reversed(range(SUBS)):
        current = add_sources(current, sources, sub)
        current, low = adjoint_steps(current, across, low, 2)
        results[sub] = current
        for row in range(ROWS):
            gradient[sub * ROWS + row] = current[row]
    encode([results[sub][row - ROWS] for sub, row in PUSHED], pushed)
    encode([results[sub][row - 2 * ROWS] for sub, row in PUSHED_FAR], pushed_far)


def finish_kernel(part, pushed, pushed_far, gradient_far, gradient, sems):
    near = dict(zip(PUSHED, decode(pushed, len(PUSHED))))
    far = dict(zip(PUSHED_FAR, decode(pushed_far, len(PUSHED_FAR))))
    copies = []
    for sub in range(SUBS):
        rows = []
        for row in range(ROWS):
            value = part[sub * ROWS + row] + near[sub, row]
            rows.append(value + far[sub, row] if (sub, row) in far else value)
        gradient[sub] = jnp.swapaxes(jnp.stack(rows), 0, 1)
        copies.append(
            pltpu.make_async_copy(gradient.at[sub], gradient_far.at[sub], sems.at[sub])
        )
        copies[-1].start()
    for copy in copies:
        copy.wait()


def run(kernel, outputs, arguments, scratch=(), name=None, flops=2_000_000, far=False, far_out=False):
    size = sum(a.size * a.dtype.itemsize for a in arguments)
    place = pltpu.HBM if far else pltpu.VMEM
    if far:
        arguments = [pltpu.with_memory_space_constraint(a, pltpu.HBM) for a in arguments]
    return pl.pallas_call(
        kernel,
        out_shape=outputs,
        in_specs=[pl.BlockSpec(memory_space=place)] * len(arguments),
        **({"out_specs": pl.BlockSpec(memory_space=pltpu.HBM)} if far_out else {}),
        scratch_shapes=scratch,
        compiler_params=pltpu.CompilerParams(vmem_limit_bytes=40 * 1024 * 1024),
        cost_estimate=pl.CostEstimate(flops=flops, bytes_accessed=size, transcendentals=0),
        name=name,
    )(*arguments)


STAY = {part: part for part in range(PARTS)}
FORWARD_FIRST, FORWARD_SECOND = {0: 1, 1: 0, 2: 3}, {1: 2, 0: 3}
ADJOINT_FIRST, ADJOINT_SECOND = {3: 2, 2: 3, 1: 0}, {2: 1, 3: 0}


def moved(array, parts, tiles):
    pairs = [
        (part * TILES + tile, to_part * TILES + tile + tiles)
        for part, to_part in parts.items()
        for tile in range(TILES)
        if 0 <= tile + tiles < TILES
    ]
    return lax.ppermute(array, ("tm", "space"), pairs)


def shards(
    forcing, courant, innovation, obs_cells, obs_weight, obs_owner, channel_weight, channel_rinv
):
    def message(tiles):
        return struct(tiles, LEVELS, LANES, dtype=jnp.int32)

    records = (
        innovation, obs_cells, obs_weight, jnp.swapaxes(obs_owner, 1, 2),
        channel_weight.T, channel_rinv.reshape(1, -1),
    )
    winds, forces, below, down_edge, *records = run(
        rows_kernel,
        (
            struct(WINDS * ROWS, LEVELS, WIDTH),
            struct(SUBS * ROWS, LEVELS, WIDTH),
            message(WIND_TILES + message_tiles(SUBS * ROWS)),
            message(WIND_TILES + message_tiles(len(DOWN_ROWS))),
            *[struct(*array.shape, dtype=array.dtype) for array in records],
        ),
        (forcing, courant, *records),
        scratch=(
            pltpu.VMEM(forcing.shape, f32),
            pltpu.VMEM(courant.shape, f32),
            pltpu.SemaphoreType.DMA((FIELDS + RECORD_ARRAYS,)),
        ),
        name="rows",
        far=True,
    )
    below = moved(below, STAY, 1)
    down_edge = moved(down_edge, STAY, 2)
    send = run(
        pack_kernel,
        struct(TILES * 8, LANES),
        records,
        name="pack",
    )
    received = lax.all_to_all(
        send.reshape(TILES, 8, LANES), "space", split_axis=0, concat_axis=0, tiled=True
    ).reshape(TILES * 8, LANES)
    below, down_edge, _ = lax.optimization_barrier((below, down_edge, send))
    own, mine, winds_below, lower_edge, forces_below = run(
        forward_local_kernel,
        (
            message(message_tiles(DROP + ROWS)),
            struct(REACH + ROWS, LEVELS, WIDTH),
            struct(WINDS * ROWS, LEVELS, WIDTH),
            struct(WINDS * ROWS, LEVELS, WIDTH),
            struct(SUBS * ROWS, LEVELS, WIDTH),
        ),
        (winds, forces, below, down_edge),
        name="forward_local",
        flops=2_000_000_000,
    )
    before = moved(own, FORWARD_FIRST, 0)
    pair_shapes = (message(message_tiles(ROWS)), message(message_tiles(ROWS + EXTRA)))
    own, extended = run(
        forward_pair_kernel,
        pair_shapes,
        (winds, winds_below, lower_edge, mine, before),
        name="forward_pair",
    )
    pair = (moved(own, FORWARD_SECOND, 0), moved(extended, FORWARD_SECOND, 1))
    slots, stencil, mixing = run(
        stencil_kernel,
        (
            struct(SUBS, LANES, LANES),
            struct(SUBS, CHUNKS, HALF, CORNERS * LANES, dtype=bf16),
            struct(LEVELS, LEVELS, LANES),
        ),
        (received, *records[-2:]),
        scratch=(pltpu.VMEM((LANES, LANES), f32),),
        name="stencil",
    )
    size = PIECES * LEVELS
    sources, mine, response = run(
        forward_final_kernel,
        (
            struct(SUBS * ROWS, LEVELS, WIDTH),
            struct(DROP + ROWS, LEVELS, WIDTH),
            message(message_tiles(DROP + ROWS)),
        ),
        (
            winds, forces, winds_below, lower_edge, forces_below,
            before, *pair, slots, stencil, mixing,
        ),
        scratch=(
            pltpu.VMEM((SUBS, CHUNKS, 2 * size, CORNERS * LANES), f32),
            pltpu.VMEM((SUBS, CHUNKS, 2 * size, CORNERS * LANES), bf16),
        ),
        name="forward_final",
    )

    after = moved(response, ADJOINT_FIRST, 0)
    own, extended = run(
        adjoint_pair_kernel,
        pair_shapes,
        (winds, winds_below, lower_edge, mine, after),
        name="adjoint_pair",
    )
    pair = (moved(own, ADJOINT_SECOND, 0), moved(extended, ADJOINT_SECOND, -1))
    part, pushed, pushed_far = run(
        adjoint_final_kernel,
        (
            struct(SUBS * ROWS, LEVELS, WIDTH),
            message(message_tiles(len(PUSHED))),
            message(message_tiles(len(PUSHED_FAR))),
        ),
        (sources, winds, winds_below, lower_edge, after, *pair),
        name="adjoint_final",
    )
    pushed = moved(pushed, STAY, -1)
    pushed_far = moved(pushed_far, STAY, -2)
    return run(
        finish_kernel,
        struct(SUBS, LEVELS, ROWS, WIDTH),
        (part, pushed, pushed_far),
        scratch=(
            pltpu.VMEM((SUBS, LEVELS, ROWS, WIDTH), f32),
            pltpu.SemaphoreType.DMA((SUBS,)),
        ),
        name="finish",
        far_out=True,
    )


def solution(mesh):
    return jax.shard_map(
        shards,
        mesh=mesh,
        in_specs=(
            P("tm", None, "space", None),
            P(None, None, "space", None),
            P("tm", None, "space"),
            P("tm", None, "space"),
            P("tm", None, "space"),
            P("tm", "space", None),
            P(),
            P(),
        ),
        out_specs=P("tm", None, "space", None),
        check_vma=False,
    )
```

```python
import jax
import jax.numpy as jnp
from jax import lax
from jax.experimental import pallas as pl
from jax.experimental.pallas import tpu as pltpu
from jax.sharding import PartitionSpec as P

LEVELS = 8
ROWS = 8
WIDTH = 512
SUBS = 3
TILES = 64
PARTS = 4
RECORDS = 256
CORNERS = 4
HALF = 256
PIECES = WIDTH // HALF * ROWS
CHUNKS = 8
LANES = 128

f32 = jnp.float32
bf16 = jnp.bfloat16
highest = lax.Precision.HIGHEST


def struct(*shape, dtype=f32):
    return jax.ShapeDtypeStruct(shape, dtype)


def split(value):
    top = value.astype(bf16)
    return top, (value - top.astype(f32)).astype(bf16)


LEVEL_TOP = 32766.0
SCALE_BITS = 22
SCALE_BIAS = 256
WIND_MIDDLE = 0.25
WIND_REACH = 0.21


def nearest(value):
    return jnp.floor(value + 0.5).astype(jnp.int32)


def join(first, second):
    return jnp.left_shift(first, 16) | (second & 0xFFFF)


def parted(both):
    return jnp.right_shift(both, 16), jnp.right_shift(jnp.left_shift(both, 16), 16)


def scale_of(code):
    exponent = (jnp.right_shift(code, SCALE_BITS) - SCALE_BIAS).astype(f32)
    mantissa = (code & ((1 << SCALE_BITS) - 1)).astype(f32) * (0.5 ** 20)
    return mantissa * jnp.exp2(exponent)


TILE_COLUMNS = WIDTH // LANES


def message_tiles(count):
    return count // 2 * TILE_COLUMNS + 1


def put_row(message, start, value):
    for part in range(TILE_COLUMNS):
        message[start + part] = value[:, part * LANES : (part + 1) * LANES]


def get_row(message, start):
    return jnp.concatenate([message[start + part] for part in range(TILE_COLUMNS)], axis=1)


def encode(values, message, start=0):
    count = len(values)
    lane = lax.broadcasted_iota(jnp.int32, (LEVELS, LANES), 1)
    largest = jnp.full((LEVELS, LANES), 1e-30, f32)
    for number, value in enumerate(values):
        top = jnp.max(jnp.abs(value), axis=1, keepdims=True)
        largest = jnp.where(lane == number, jnp.maximum(top, 1e-30), largest)
    exponent = jnp.floor(jnp.log2(largest))
    mantissa = (largest * jnp.exp2(-exponent) * 2.0 ** 20).astype(jnp.int32) + 16
    code = jnp.left_shift(exponent.astype(jnp.int32) + SCALE_BIAS, SCALE_BITS) + mantissa
    factor = LEVEL_TOP / scale_of(code)
    half = count // 2
    whole = [nearest(value * factor[:, n : n + 1]) for n, value in enumerate(values)]
    for number in range(half):
        put_row(message, start + number * TILE_COLUMNS, join(whole[number], whole[number + half]))
    message[start + half * TILE_COLUMNS] = code


def decode(message, count, start=0):
    half = count // 2
    factor = scale_of(message[start + half * TILE_COLUMNS]) * (1.0 / LEVEL_TOP)
    values = [None] * count
    for number in range(half):
        pair = parted(get_row(message, start + number * TILE_COLUMNS))
        for place, value in zip((number, number + half), pair):
            values[place] = value.astype(f32) * factor[:, place : place + 1]
    return values


def encode_wind(first, second):
    steps = LEVEL_TOP / WIND_REACH
    return join(nearest((first - WIND_MIDDLE) * steps), nearest((second - WIND_MIDDLE) * steps))


def decode_wind(both):
    step = WIND_REACH / LEVEL_TOP
    return [value.astype(f32) * step + WIND_MIDDLE for value in parted(both)]


def forward_step(current, wind_x, wind_y, low):
    result = {}
    for row in range(low + 1, ROWS):
        here = current[row]
        left = pltpu.roll(here, 1, 1)
        result[row] = (
            here - wind_x(row) * (here - left) - wind_y(row) * (here - current[row - 1])
        )
    return result


def adjoint_step(current, wind_x, wind_y, low):
    result = {low - 1: wind_y(low) * current[low]}
    for row in range(low, ROWS):
        here = current[row]
        along = wind_x(row)
        value = here * (1.0 - along - wind_y(row)) + pltpu.roll(along * here, WIDTH - 1, 1)
        if row + 1 < ROWS:
            value = value + wind_y(row + 1) * current[row + 1]
        result[row] = value
    return result


def forward_steps(current, winds, low, count):
    for _ in range(count):
        current = forward_step(current, winds[0], winds[1], low)
        low += 1
    return current, low


def adjoint_steps(current, winds, low, count):
    for _ in range(count):
        current = adjoint_step(current, winds[0], winds[1], low)
        low -= 1
    return current, low


WINDS = 2
FIELDS = WINDS + SUBS
RECORD_ARRAYS = 6
EXTRA = 4
REACH = 10
DROP = 6
DOWN_ROWS = [(sub, row) for sub in range(SUBS) for row in range(2 * sub, ROWS)]
WIND_TILES = ROWS * TILE_COLUMNS


def lower_winds(winds, winds_below, edge):
    def reader(field):
        def read(row):
            if row >= 0:
                return winds[field * ROWS + row]
            if row >= -ROWS:
                return winds_below[field * ROWS + row + ROWS]
            return edge[field * ROWS + row + 2 * ROWS]

        return read

    return [reader(field) for field in range(WINDS)]


def lower_forces(forces, forces_below, edge=None):
    def reader(sub):
        def read(row):
            if row >= 0:
                return forces[sub * ROWS + row]
            if row >= -ROWS:
                return forces_below[sub * ROWS + row + ROWS]
            return edge[sub, row + 2 * ROWS]

        return read

    return [reader(sub) for sub in range(SUBS)]


def add_rows(current, other, low, high):
    return {row: current[row] + other(row) for row in range(low, high)}


def fetch(pairs, sems):
    copies = [
        pltpu.make_async_copy(source, target, sems.at[number])
        for number, (source, target) in enumerate(pairs)
    ]
    for copy in copies:
        copy.start()
    return copies


def rows_kernel(*refs):
    forcing_far, courant_far, *records_far = refs[: 2 + RECORD_ARRAYS]
    winds, forces, below, down_edge, *records = refs[2 + RECORD_ARRAYS : 6 + 2 * RECORD_ARRAYS]
    forcing, courant, sems = refs[6 + 2 * RECORD_ARRAYS :]
    copies = fetch(
        [(courant_far.at[field], courant.at[field]) for field in range(WINDS)]
        + [(forcing_far.at[sub], forcing.at[sub]) for sub in range(SUBS)]
        + list(zip(records_far, records)),
        sems,
    )
    for copy in copies[:WINDS]:
        copy.wait()
    for field in range(WINDS):
        winds[pl.ds(field * ROWS, ROWS)] = jnp.swapaxes(courant[field], 0, 1)
    encode_winds(winds, range(ROWS), below, 0)
    encode_winds(winds, range(ROWS), down_edge, 0)
    rows = []
    for sub in range(SUBS):
        copies[WINDS + sub].wait()
        turned = jnp.swapaxes(forcing[sub], 0, 1)
        forces[pl.ds(sub * ROWS, ROWS)] = turned
        rows += [turned[row] for row in range(ROWS)]
    encode(rows, below, WIND_TILES)
    encode([rows[sub * ROWS + row] for sub, row in DOWN_ROWS], down_edge, WIND_TILES)
    for copy in copies[FIELDS:]:
        copy.wait()


def encode_winds(winds, rows, message, start):
    for number, row in enumerate(rows):
        both = encode_wind(winds[row], winds[ROWS + row])
        put_row(message, start + number * TILE_COLUMNS, both)


def unpack_winds(message, rows, result, start=0):
    for row in range(rows):
        first, second = decode_wind(get_row(message, start + row * TILE_COLUMNS))
        result[row] = first
        result[rows + row] = second


def three(value):
    top = value.astype(bf16)
    rest = value - top.astype(f32)
    middle = rest.astype(bf16)
    return top, middle, (rest - middle.astype(f32)).astype(bf16)


def pack_kernel(innovation, cells, weight, owner, channel_weight, rinv, send):
    sub_id = lax.broadcasted_iota(jnp.int32, (RECORDS, RECORDS), 0)
    lane_id = lax.broadcasted_iota(jnp.int32, (RECORDS, RECORDS), 1)
    not_later = lane_id <= sub_id

    scaled = jnp.concatenate(three(channel_weight[...] * (rinv[...] * rinv[...])), axis=0)

    spread_row = lax.broadcasted_iota(jnp.int32, (2 * LEVELS, LANES), 0)
    spread_lane = lax.broadcasted_iota(jnp.int32, (2 * LEVELS, LANES), 1)
    repeat = jnp.where(
        (spread_lane // 64 == spread_row // LEVELS) & (spread_lane % LEVELS == spread_row % LEVELS),
        1.0,
        0.0,
    ).astype(bf16)
    slot_lane = lax.broadcasted_iota(jnp.int32, (RECORDS, LANES), 1)
    slot_rank = ((slot_lane % 64) // LEVELS) * 2
    tile_id = lax.broadcasted_iota(jnp.int32, (TILES, RECORDS), 0)
    ones = jnp.ones((RECORDS, LANES), bf16)
    for sub in range(SUBS):
        parts = jnp.dot(scaled, innovation[sub], preferred_element_type=f32)
        projected = (parts[:LEVELS] + parts[LEVELS : 2 * LEVELS]) + parts[2 * LEVELS :]
        payload = jnp.concatenate(
            [cells[sub].astype(f32), weight[sub].astype(f32), projected], axis=0
        )
        owner_row = owner[sub]
        owner_rows = jnp.broadcast_to(owner_row, (RECORDS, RECORDS))
        earlier = jnp.where((owner_rows.T == owner_rows) & not_later, 1.0, 0.0).astype(bf16)
        rank = jnp.dot(earlier, ones, preferred_element_type=f32).astype(jnp.int32) - 1
        target = jnp.where(tile_id == owner_row, 1.0, 0.0).astype(bf16)
        repeated = [
            lax.dot_general(part, repeat, (((0,), (0,)), ((), ())), preferred_element_type=f32)
            for part in three(payload)
        ]
        for half in range(2):
            chosen = rank == slot_rank + half
            placed = [
                jnp.dot(
                    target, jnp.where(chosen, part, 0.0).astype(bf16), preferred_element_type=f32
                )
                for part in repeated
            ]
            send[pl.ds(2 * sub + half, TILES, stride=8), :] = (placed[0] + placed[1]) + placed[2]
    for spare in range(2 * SUBS, 8):
        send[pl.ds(spare, TILES, stride=8), :] = jnp.zeros((TILES, LANES), f32)


def stencil_kernel(received, channel_weight, rinv, slots, stencil, mixing, pieces):
    matrix = lax.dot_general(
        channel_weight[...] * (rinv[...] * rinv[...]), channel_weight[...],
        (((1,), (1,)), ((), ())), precision=highest, preferred_element_type=f32,
    )
    for level in range(LEVELS):
        mixing[level] = jnp.broadcast_to(matrix[:, level : level + 1], (LEVELS, LANES))
    rows_id = lax.broadcasted_iota(jnp.int32, (HALF, LANES), 0)

    def one_sub(sub, _):
        for half in range(2):
            pieces[pl.ds(half * TILES, TILES), :] = received[
                pl.ds(2 * sub + half, TILES, stride=8), :
            ]
        slots[sub] = pieces[...].T
        for chunk in range(CHUNKS):
            record = slots[sub, pl.ds(chunk * LEVELS, LEVELS), :]
            column = record.astype(jnp.int32) & (HALF - 1)
            for corner in range(CORNERS):
                stencil[sub, chunk, :, corner * LANES : (corner + 1) * LANES] = jnp.where(
                    rows_id == column[corner : corner + 1],
                    record[CORNERS + corner : CORNERS + corner + 1],
                    0.0,
                ).astype(bf16)
        return 0

    lax.fori_loop(0, SUBS, one_sub, 0)


def respond(slots, mixing, sub, chunk, found, spread):
    size = PIECES * LEVELS
    record = slots[sub, pl.ds(chunk * LEVELS, LEVELS), :]
    adjoint = -slots[sub, pl.ds(TILES + chunk * LEVELS, LEVELS), :]
    piece = jnp.right_shift(record.astype(jnp.int32), 8)
    sums = []
    wanted = []
    for corner in range(CORNERS):
        wanted.append(jnp.broadcast_to(piece[corner : corner + 1], (LEVELS, LANES)))
        part = pl.ds(corner * LANES, LANES)
        value = None
        for number in range(PIECES):
            both = (
                found[sub, chunk, pl.ds(number * LEVELS, LEVELS), part]
                + found[sub, chunk, pl.ds(size + number * LEVELS, LEVELS), part]
            )
            value = both if value is None else jnp.where(wanted[corner] == number, both, value)
        sums.append(value)
    values = (sums[0] + sums[1]) + (sums[2] + sums[3])
    for level in range(LEVELS):
        adjoint = adjoint + mixing[level] * values[level : level + 1]
    sources = [part.astype(f32) for part in split(adjoint)]
    for corner in range(CORNERS):
        part = pl.ds(corner * LANES, LANES)
        for place, source in enumerate(sources):
            spread[sub, chunk, pl.ds(place * size, size), part] = jnp.concatenate(
                [jnp.where(wanted[corner] == number, source, 0.0) for number in range(PIECES)],
                axis=0,
            ).astype(bf16)


def interpolate(state, stencil, sub, found):
    left = jnp.concatenate(split(state), axis=0)
    for chunk in range(CHUNKS):
        found[sub, chunk] = jnp.dot(left, stencil[sub, chunk], preferred_element_type=f32)


def scatter(slots, stencil, mixing, sub, found, spread):
    size = PIECES * LEVELS
    for chunk in range(CHUNKS):
        respond(slots, mixing, sub, chunk, found, spread)
    total = jnp.zeros((2 * size, HALF), f32)
    for chunk in range(CHUNKS):
        total = total + lax.dot_general(
            spread[sub, chunk], stencil[sub, chunk], (((1,), (1,)), ((), ())),
            preferred_element_type=f32,
        )
    return total[:size] + total[size:]


def stacked(rows):
    return jnp.concatenate(
        [rows[row][:, half * HALF : (half + 1) * HALF] for row in range(ROWS) for half in range(2)],
        axis=0,
    )


def unstacked(stack, row):
    places = [(2 * row + half) * LEVELS for half in range(2)]
    return jnp.concatenate([stack[place : place + LEVELS] for place in places], axis=1)


def forward_local_kernel(
    winds, forces, below, down_edge, own, mine, winds_below, lower_edge, forces_below
):
    unpack_winds(below, ROWS, winds_below)
    unpack_winds(down_edge, ROWS, lower_edge)
    for number, row in enumerate(decode(below, SUBS * ROWS, WIND_TILES)):
        forces_below[number] = row
    edge = dict(zip(DOWN_ROWS, decode(down_edge, len(DOWN_ROWS), WIND_TILES)))
    across = lower_winds(winds, winds_below, lower_edge)
    forced = lower_forces(forces, forces_below, edge)
    low = -2 * ROWS
    current = {row: forced[0](row) for row in range(low, ROWS)}
    current, low = forward_steps(current, across, low, 2)
    for sub in range(1, SUBS):
        current = add_rows(current, forced[sub], low, ROWS)
        current, low = forward_steps(current, across, low, 2)
    listed = [current[row] for row in range(-REACH, ROWS)]
    for number, row in enumerate(listed):
        mine[number] = row
    encode(listed[REACH - DROP :], own)


def time_is(condition):
    index = jnp.full((LEVELS, WIDTH), lax.axis_index("tm"), jnp.int32)
    return condition(index)


def lower_state(own, extended):
    here = decode(own, ROWS)
    under = decode(extended, ROWS + EXTRA)
    return {
        row: here[row] if row >= 0 else under[row + ROWS + EXTRA]
        for row in range(-(ROWS + EXTRA), ROWS)
    }


def forward_pair_kernel(winds, winds_below, lower_edge, mine, other, own, extended):
    @pl.when(lax.axis_index("tm") < 2)
    def _():
        across = lower_winds(winds, winds_below, lower_edge)
        first = time_is(lambda index: index == 0)
        rows = dict(zip(range(-DROP, ROWS), decode(other, DROP + ROWS)))
        current = {
            row: jnp.where(first, mine[row + REACH], rows.get(row, 0.0))
            for row in range(-REACH, ROWS)
        }
        current, low = forward_steps(current, across, -REACH, 6)
        listed = [
            current[row] + jnp.where(first, rows[row], mine[row + REACH])
            for row in range(-EXTRA, ROWS)
        ]
        encode(listed[EXTRA:], own)
        encode(listed, extended)


def forward_final_kernel(
    winds, forces, winds_below, lower_edge, forces_below,
    before, pair_own, pair_extended, slots, stencil, mixing,
    sources, mine, response,
    found, spread,
):
    across = lower_winds(winds, winds_below, lower_edge)
    forced = lower_forces(forces, forces_below)
    half_way = lower_state(pair_own, pair_extended)
    current, low = forward_steps(half_way, across, -(ROWS + EXTRA), 6)
    before = decode(before, DROP + ROWS)
    third = time_is(lambda index: index == 2)
    odd = time_is(lambda index: (index & 1) == 1)
    current = {
        row: jnp.where(third, half_way[row], value) + jnp.where(odd, before[row + DROP], 0.0)
        for row, value in current.items()
    }
    for sub in range(SUBS):
        current = add_rows(current, forced[sub], low, ROWS)
        current, low = forward_steps(current, across, low, 2)
        interpolate(stacked(current), stencil, sub, found)
    current, low = {}, 0
    for sub in reversed(range(SUBS)):
        stack = scatter(slots, stencil, mixing, sub, found, spread)
        for row in range(ROWS):
            value = unstacked(stack, row)
            sources[sub * ROWS + row] = value
            current[row] = current[row] + value if row in current else value
        current, low = adjoint_steps(current, across, low, 2)
    listed = [current[row] for row in range(low, ROWS)]
    for number, row in enumerate(listed):
        mine[number] = row
    encode(listed, response)


def add_sources(current, sources, sub):
    return {
        row: value + sources[sub * ROWS + row] if row >= 0 else value
        for row, value in current.items()
    }


def adjoint_pair_kernel(winds, winds_below, lower_edge, mine, other, own, near, far):
    @pl.when(lax.axis_index("tm") >= 2)
    def _():
        across = lower_winds(winds, winds_below, lower_edge)
        last = time_is(lambda index: index == 3)
        rows = decode(other, DROP + ROWS)
        current = {
            row: jnp.where(last, mine[row + DROP], rows[row + DROP]) for row in range(-DROP, ROWS)
        }
        current, low = adjoint_steps(current, across, -DROP, 6)
        for row in range(-DROP, ROWS):
            current[row] = current[row] + jnp.where(last, rows[row + DROP], mine[row + DROP])
        encode([current[row] for row in range(ROWS)], own)
        encode([current[row] for row in range(-ROWS, 0)], near)
        encode([current[row] for row in range(low, -ROWS)], far)


PUSHED = [(sub, row) for sub in range(SUBS) for row in range(ROWS)]
PUSHED_FAR = [(sub, row) for sub in range(SUBS) for row in range(EXTRA + 2 * sub, ROWS)]


def adjoint_final_kernel(
    sources, winds, winds_below, lower_edge, after, pair_own, pair_near, pair_far,
    gradient, pushed, pushed_far,
):
    across = lower_winds(winds, winds_below, lower_edge)
    own = decode(pair_own, ROWS)
    near = decode(pair_near, ROWS)
    far = decode(pair_far, EXTRA)
    half_way = {row: own[row] + near[row] for row in range(ROWS)}
    for number, value in enumerate(far):
        half_way[ROWS - EXTRA + number] = half_way[ROWS - EXTRA + number] + value
    current, low = adjoint_steps(half_way, across, 0, 6)
    after = decode(after, DROP + ROWS)
    second = time_is(lambda index: index == 1)
    even = time_is(lambda index: (index & 1) == 0)
    for row in current:
        current[row] = jnp.where(second, half_way.get(row, 0.0), current[row])
        current[row] = current[row] + jnp.where(even, after[row + DROP], 0.0)
    results = [None] * SUBS
    for sub in reversed(range(SUBS)):
        current = add_sources(current, sources, sub)
        current, low = adjoint_steps(current, across, low, 2)
        results[sub] = current
        for row in range(ROWS):
            gradient[sub * ROWS + row] = current[row]
    encode([results[sub][row - ROWS] for sub, row in PUSHED], pushed)
    encode([results[sub][row - 2 * ROWS] for sub, row in PUSHED_FAR], pushed_far)


def finish_kernel(part, pushed, pushed_far, gradient_far, gradient, sems):
    near = dict(zip(PUSHED, decode(pushed, len(PUSHED))))
    far = dict(zip(PUSHED_FAR, decode(pushed_far, len(PUSHED_FAR))))
    copies = []
    for sub in range(SUBS):
        rows = []
        for row in range(ROWS):
            value = part[sub * ROWS + row] + near[sub, row]
            rows.append(value + far[sub, row] if (sub, row) in far else value)
        gradient[sub] = jnp.swapaxes(jnp.stack(rows), 0, 1)
        copies.append(
            pltpu.make_async_copy(gradient.at[sub], gradient_far.at[sub], sems.at[sub])
        )
        copies[-1].start()
    for copy in copies:
        copy.wait()


def run(kernel, outputs, arguments, scratch=(), name=None, flops=2_000_000, far=False, far_out=False):
    size = sum(a.size * a.dtype.itemsize for a in arguments)
    place = pltpu.HBM if far else pltpu.VMEM
    if far:
        arguments = [pltpu.with_memory_space_constraint(a, pltpu.HBM) for a in arguments]
    return pl.pallas_call(
        kernel,
        out_shape=outputs,
        in_specs=[pl.BlockSpec(memory_space=place)] * len(arguments),
        **({"out_specs": pl.BlockSpec(memory_space=pltpu.HBM)} if far_out else {}),
        scratch_shapes=scratch,
        compiler_params=pltpu.CompilerParams(vmem_limit_bytes=40 * 1024 * 1024),
        cost_estimate=pl.CostEstimate(flops=flops, bytes_accessed=size, transcendentals=0),
        name=name,
    )(*arguments)


STAY = {part: part for part in range(PARTS)}
FORWARD_FIRST, FORWARD_SECOND = {0: 1, 1: 0, 2: 3}, {1: 2, 0: 3}
ADJOINT_FIRST, ADJOINT_SECOND = {3: 2, 2: 3, 1: 0}, {2: 1, 3: 0}


def moved(array, parts, tiles):
    pairs = [
        (part * TILES + tile, to_part * TILES + tile + tiles)
        for part, to_part in parts.items()
        for tile in range(TILES)
        if 0 <= tile + tiles < TILES
    ]
    return lax.ppermute(array, ("tm", "space"), pairs)


def shards(
    forcing, courant, innovation, obs_cells, obs_weight, obs_owner, channel_weight, channel_rinv
):
    def message(tiles):
        return struct(tiles, LEVELS, LANES, dtype=jnp.int32)

    records = (
        innovation, obs_cells, obs_weight, jnp.swapaxes(obs_owner, 1, 2),
        channel_weight.T, channel_rinv.reshape(1, -1),
    )
    winds, forces, below, down_edge, *records = run(
        rows_kernel,
        (
            struct(WINDS * ROWS, LEVELS, WIDTH),
            struct(SUBS * ROWS, LEVELS, WIDTH),
            message(WIND_TILES + message_tiles(SUBS * ROWS)),
            message(WIND_TILES + message_tiles(len(DOWN_ROWS))),
            *[struct(*array.shape, dtype=array.dtype) for array in records],
        ),
        (forcing, courant, *records),
        scratch=(
            pltpu.VMEM(forcing.shape, f32),
            pltpu.VMEM(courant.shape, f32),
            pltpu.SemaphoreType.DMA((FIELDS + RECORD_ARRAYS,)),
        ),
        name="rows",
        far=True,
    )
    below = moved(below, STAY, 1)
    down_edge = moved(down_edge, STAY, 2)
    send = run(
        pack_kernel,
        struct(TILES * 8, LANES),
        records,
        name="pack",
    )
    received = lax.all_to_all(
        send.reshape(TILES, 8, LANES), "space", split_axis=0, concat_axis=0, tiled=True
    ).reshape(TILES * 8, LANES)
    below, down_edge, _ = lax.optimization_barrier((below, down_edge, send))
    own, mine, winds_below, lower_edge, forces_below = run(
        forward_local_kernel,
        (
            message(message_tiles(DROP + ROWS)),
            struct(REACH + ROWS, LEVELS, WIDTH),
            struct(WINDS * ROWS, LEVELS, WIDTH),
            struct(WINDS * ROWS, LEVELS, WIDTH),
            struct(SUBS * ROWS, LEVELS, WIDTH),
        ),
        (winds, forces, below, down_edge),
        name="forward_local",
        flops=2_000_000_000,
    )
    before = moved(own, FORWARD_FIRST, 0)
    pair_shapes = (message(message_tiles(ROWS)), message(message_tiles(ROWS + EXTRA)))
    own, extended = run(
        forward_pair_kernel,
        pair_shapes,
        (winds, winds_below, lower_edge, mine, before),
        name="forward_pair",
    )
    pair = (moved(own, FORWARD_SECOND, 0), moved(extended, FORWARD_SECOND, 1))
    slots, stencil, mixing = run(
        stencil_kernel,
        (
            struct(SUBS, LANES, LANES),
            struct(SUBS, CHUNKS, HALF, CORNERS * LANES, dtype=bf16),
            struct(LEVELS, LEVELS, LANES),
        ),
        (received, *records[-2:]),
        scratch=(pltpu.VMEM((LANES, LANES), f32),),
        name="stencil",
    )
    size = PIECES * LEVELS
    sources, mine, response = run(
        forward_final_kernel,
        (
            struct(SUBS * ROWS, LEVELS, WIDTH),
            struct(DROP + ROWS, LEVELS, WIDTH),
            message(message_tiles(DROP + ROWS)),
        ),
        (
            winds, forces, winds_below, lower_edge, forces_below,
            before, *pair, slots, stencil, mixing,
        ),
        scratch=(
            pltpu.VMEM((SUBS, CHUNKS, 2 * size, CORNERS * LANES), f32),
            pltpu.VMEM((SUBS, CHUNKS, 2 * size, CORNERS * LANES), bf16),
        ),
        name="forward_final",
    )

    after = moved(response, ADJOINT_FIRST, 0)
    own, near, far = run(
        adjoint_pair_kernel,
        tuple(message(message_tiles(count)) for count in (ROWS, ROWS, EXTRA)),
        (winds, winds_below, lower_edge, mine, after),
        name="adjoint_pair",
    )
    pair = (
        moved(own, ADJOINT_SECOND, 0),
        moved(near, ADJOINT_SECOND, -1),
        moved(far, ADJOINT_SECOND, -2),
    )
    part, pushed, pushed_far = run(
        adjoint_final_kernel,
        (
            struct(SUBS * ROWS, LEVELS, WIDTH),
            message(message_tiles(len(PUSHED))),
            message(message_tiles(len(PUSHED_FAR))),
        ),
        (sources, winds, winds_below, lower_edge, after, *pair),
        name="adjoint_final",
    )
    pushed = moved(pushed, STAY, -1)
    pushed_far = moved(pushed_far, STAY, -2)
    return run(
        finish_kernel,
        struct(SUBS, LEVELS, ROWS, WIDTH),
        (part, pushed, pushed_far),
        scratch=(
            pltpu.VMEM((SUBS, LEVELS, ROWS, WIDTH), f32),
            pltpu.SemaphoreType.DMA((SUBS,)),
        ),
        name="finish",
        far_out=True,
    )


def solution(mesh):
    return jax.shard_map(
        shards,
        mesh=mesh,
        in_specs=(
            P("tm", None, "space", None),
            P(None, None, "space", None),
            P("tm", None, "space"),
            P("tm", None, "space"),
            P("tm", None, "space"),
            P("tm", "space", None),
            P(),
            P(),
        ),
        out_specs=P("tm", None, "space", None),
        check_vma=False,
    )
```

```python
import jax
import jax.numpy as jnp
from jax import lax
from jax.experimental import pallas as pl
from jax.experimental.pallas import tpu as pltpu
from jax.sharding import PartitionSpec as P

LEVELS = 8
ROWS = 8
WIDTH = 512
SUBS = 3
TILES = 64
PARTS = 4
RECORDS = 256
CORNERS = 4
HALF = 256
PIECES = WIDTH // HALF * ROWS
CHUNKS = 8
LANES = 128

f32 = jnp.float32
bf16 = jnp.bfloat16
highest = lax.Precision.HIGHEST


def struct(*shape, dtype=f32):
    return jax.ShapeDtypeStruct(shape, dtype)


def split(value):
    top = value.astype(bf16)
    return top, (value - top.astype(f32)).astype(bf16)


LEVEL_TOP = 32766.0
SCALE_BITS = 22
SCALE_BIAS = 256
WIND_MIDDLE = 0.25
WIND_REACH = 0.21


def nearest(value):
    return jnp.floor(value + 0.5).astype(jnp.int32)


def join(first, second):
    return jnp.left_shift(first, 16) | (second & 0xFFFF)


def parted(both):
    return jnp.right_shift(both, 16), jnp.right_shift(jnp.left_shift(both, 16), 16)


def scale_of(code):
    exponent = (jnp.right_shift(code, SCALE_BITS) - SCALE_BIAS).astype(f32)
    mantissa = (code & ((1 << SCALE_BITS) - 1)).astype(f32) * (0.5 ** 20)
    return mantissa * jnp.exp2(exponent)


TILE_COLUMNS = WIDTH // LANES


def message_tiles(count):
    return count // 2 * TILE_COLUMNS + 1


def put_row(message, start, value):
    for part in range(TILE_COLUMNS):
        message[start + part] = value[:, part * LANES : (part + 1) * LANES]


def get_row(message, start):
    return jnp.concatenate([message[start + part] for part in range(TILE_COLUMNS)], axis=1)


def encode(values, message, start=0):
    count = len(values)
    lane = lax.broadcasted_iota(jnp.int32, (LEVELS, LANES), 1)
    largest = jnp.full((LEVELS, LANES), 1e-30, f32)
    for number, value in enumerate(values):
        top = jnp.max(jnp.abs(value), axis=1, keepdims=True)
        largest = jnp.where(lane == number, jnp.maximum(top, 1e-30), largest)
    exponent = jnp.floor(jnp.log2(largest))
    mantissa = (largest * jnp.exp2(-exponent) * 2.0 ** 20).astype(jnp.int32) + 16
    code = jnp.left_shift(exponent.astype(jnp.int32) + SCALE_BIAS, SCALE_BITS) + mantissa
    factor = LEVEL_TOP / scale_of(code)
    half = count // 2
    whole = [nearest(value * factor[:, n : n + 1]) for n, value in enumerate(values)]
    for number in range(half):
        put_row(message, start + number * TILE_COLUMNS, join(whole[number], whole[number + half]))
    message[start + half * TILE_COLUMNS] = code


def decode(message, count, start=0):
    half = count // 2
    factor = scale_of(message[start + half * TILE_COLUMNS]) * (1.0 / LEVEL_TOP)
    values = [None] * count
    for number in range(half):
        pair = parted(get_row(message, start + number * TILE_COLUMNS))
        for place, value in zip((number, number + half), pair):
            values[place] = value.astype(f32) * factor[:, place : place + 1]
    return values


def encode_wind(first, second):
    steps = LEVEL_TOP / WIND_REACH
    return join(nearest((first - WIND_MIDDLE) * steps), nearest((second - WIND_MIDDLE) * steps))


def decode_wind(both):
    step = WIND_REACH / LEVEL_TOP
    return [value.astype(f32) * step + WIND_MIDDLE for value in parted(both)]


def forward_step(current, wind_x, wind_y, low):
    result = {}
    for row in range(low + 1, ROWS):
        here = current[row]
        left = pltpu.roll(here, 1, 1)
        result[row] = (
            here - wind_x(row) * (here - left) - wind_y(row) * (here - current[row - 1])
        )
    return result


def adjoint_step(current, wind_x, wind_y, low):
    result = {low - 1: wind_y(low) * current[low]}
    for row in range(low, ROWS):
        here = current[row]
        along = wind_x(row)
        value = here * (1.0 - along - wind_y(row)) + pltpu.roll(along * here, WIDTH - 1, 1)
        if row + 1 < ROWS:
            value = value + wind_y(row + 1) * current[row + 1]
        result[row] = value
    return result


def forward_steps(current, winds, low, count):
    for _ in range(count):
        current = forward_step(current, winds[0], winds[1], low)
        low += 1
    return current, low


def adjoint_steps(current, winds, low, count):
    for _ in range(count):
        current = adjoint_step(current, winds[0], winds[1], low)
        low -= 1
    return current, low


WINDS = 2
FIELDS = WINDS + SUBS
RECORD_ARRAYS = 6
EXTRA = 4
REACH = 10
DROP = 6
DOWN_ROWS = [(sub, row) for sub in range(SUBS) for row in range(2 * sub, ROWS)]
WIND_TILES = ROWS * TILE_COLUMNS


def lower_winds(winds, winds_below, edge):
    def reader(field):
        def read(row):
            if row >= 0:
                return winds[field * ROWS + row]
            if row >= -ROWS:
                return winds_below[field * ROWS + row + ROWS]
            return edge[field * ROWS + row + 2 * ROWS]

        return read

    return [reader(field) for field in range(WINDS)]


def lower_forces(forces, forces_below, edge=None):
    def reader(sub):
        def read(row):
            if row >= 0:
                return forces[sub * ROWS + row]
            if row >= -ROWS:
                return forces_below[sub * ROWS + row + ROWS]
            return edge[sub, row + 2 * ROWS]

        return read

    return [reader(sub) for sub in range(SUBS)]


def add_rows(current, other, low, high):
    return {row: current[row] + other(row) for row in range(low, high)}


def fetch(pairs, sems):
    copies = [
        pltpu.make_async_copy(source, target, sems.at[number])
        for number, (source, target) in enumerate(pairs)
    ]
    for copy in copies:
        copy.start()
    return copies


def rows_kernel(*refs):
    forcing_far, courant_far, *records_far = refs[: 2 + RECORD_ARRAYS]
    winds, forces, below, down_edge, *records = refs[2 + RECORD_ARRAYS : 6 + 2 * RECORD_ARRAYS]
    forcing, courant, sems = refs[6 + 2 * RECORD_ARRAYS :]
    copies = fetch(
        [(courant_far.at[field], courant.at[field]) for field in range(WINDS)]
        + [(forcing_far.at[sub], forcing.at[sub]) for sub in range(SUBS)]
        + list(zip(records_far, records)),
        sems,
    )
    for copy in copies[:WINDS]:
        copy.wait()
    for field in range(WINDS):
        winds[pl.ds(field * ROWS, ROWS)] = jnp.swapaxes(courant[field], 0, 1)
    encode_winds(winds, range(ROWS), below, 0)
    encode_winds(winds, range(ROWS), down_edge, 0)
    rows = []
    for sub in range(SUBS):
        copies[WINDS + sub].wait()
        turned = jnp.swapaxes(forcing[sub], 0, 1)
        forces[pl.ds(sub * ROWS, ROWS)] = turned
        rows += [turned[row] for row in range(ROWS)]
    encode(rows, below, WIND_TILES)
    encode([rows[sub * ROWS + row] for sub, row in DOWN_ROWS], down_edge, WIND_TILES)
    for copy in copies[FIELDS:]:
        copy.wait()


def encode_winds(winds, rows, message, start):
    for number, row in enumerate(rows):
        both = encode_wind(winds[row], winds[ROWS + row])
        put_row(message, start + number * TILE_COLUMNS, both)


def unpack_winds(message, rows, result, start=0):
    for row in range(rows):
        first, second = decode_wind(get_row(message, start + row * TILE_COLUMNS))
        result[row] = first
        result[rows + row] = second


def three(value):
    top = value.astype(bf16)
    rest = value - top.astype(f32)
    middle = rest.astype(bf16)
    return top, middle, (rest - middle.astype(f32)).astype(bf16)


def pack_kernel(innovation, cells, weight, owner, channel_weight, rinv, send):
    sub_id = lax.broadcasted_iota(jnp.int32, (RECORDS, RECORDS), 0)
    lane_id = lax.broadcasted_iota(jnp.int32, (RECORDS, RECORDS), 1)
    not_later = lane_id <= sub_id

    scaled = jnp.concatenate(three(channel_weight[...] * (rinv[...] * rinv[...])), axis=0)

    spread_row = lax.broadcasted_iota(jnp.int32, (2 * LEVELS, LANES), 0)
    spread_lane = lax.broadcasted_iota(jnp.int32, (2 * LEVELS, LANES), 1)
    repeat = jnp.where(
        (spread_lane // 64 == spread_row // LEVELS) & (spread_lane % LEVELS == spread_row % LEVELS),
        1.0,
        0.0,
    ).astype(bf16)
    slot_lane = lax.broadcasted_iota(jnp.int32, (RECORDS, LANES), 1)
    slot_rank = ((slot_lane % 64) // LEVELS) * 2
    tile_id = lax.broadcasted_iota(jnp.int32, (TILES, RECORDS), 0)
    ones = jnp.ones((RECORDS, LANES), bf16)
    for sub in range(SUBS):
        parts = jnp.dot(scaled, innovation[sub], preferred_element_type=f32)
        projected = (parts[:LEVELS] + parts[LEVELS : 2 * LEVELS]) + parts[2 * LEVELS :]
        payload = jnp.concatenate(
            [cells[sub].astype(f32), weight[sub].astype(f32), projected], axis=0
        )
        owner_row = owner[sub]
        owner_rows = jnp.broadcast_to(owner_row, (RECORDS, RECORDS))
        earlier = jnp.where((owner_rows.T == owner_rows) & not_later, 1.0, 0.0).astype(bf16)
        rank = jnp.dot(earlier, ones, preferred_element_type=f32).astype(jnp.int32) - 1
        target = jnp.where(tile_id == owner_row, 1.0, 0.0).astype(bf16)
        repeated = [
            lax.dot_general(part, repeat, (((0,), (0,)), ((), ())), preferred_element_type=f32)
            for part in three(payload)
        ]
        for half in range(2):
            chosen = rank == slot_rank + half
            placed = [
                jnp.dot(
                    target, jnp.where(chosen, part, 0.0).astype(bf16), preferred_element_type=f32
                )
                for part in repeated
            ]
            send[pl.ds(2 * sub + half, TILES, stride=8), :] = (placed[0] + placed[1]) + placed[2]
    for spare in range(2 * SUBS, 8):
        send[pl.ds(spare, TILES, stride=8), :] = jnp.zeros((TILES, LANES), f32)


def stencil_kernel(received, channel_weight, rinv, slots, stencil, mixing, pieces):
    matrix = lax.dot_general(
        channel_weight[...] * (rinv[...] * rinv[...]), channel_weight[...],
        (((1,), (1,)), ((), ())), precision=highest, preferred_element_type=f32,
    )
    for level in range(LEVELS):
        mixing[level] = jnp.broadcast_to(matrix[:, level : level + 1], (LEVELS, LANES))
    rows_id = lax.broadcasted_iota(jnp.int32, (HALF, LANES), 0)

    def one_sub(sub, _):
        for half in range(2):
            pieces[pl.ds(half * TILES, TILES), :] = received[
                pl.ds(2 * sub + half, TILES, stride=8), :
            ]
        slots[sub] = pieces[...].T
        for chunk in range(CHUNKS):
            record = slots[sub, pl.ds(chunk * LEVELS, LEVELS), :]
            column = record.astype(jnp.int32) & (HALF - 1)
            for corner in range(CORNERS):
                stencil[sub, chunk, :, corner * LANES : (corner + 1) * LANES] = jnp.where(
                    rows_id == column[corner : corner + 1],
                    record[CORNERS + corner : CORNERS + corner + 1],
                    0.0,
                ).astype(bf16)
        return 0

    lax.fori_loop(0, SUBS, one_sub, 0)


def respond(slots, mixing, sub, chunk, found, spread):
    size = PIECES * LEVELS
    record = slots[sub, pl.ds(chunk * LEVELS, LEVELS), :]
    adjoint = -slots[sub, pl.ds(TILES + chunk * LEVELS, LEVELS), :]
    piece = jnp.right_shift(record.astype(jnp.int32), 8)
    sums = []
    wanted = []
    for corner in range(CORNERS):
        wanted.append(jnp.broadcast_to(piece[corner : corner + 1], (LEVELS, LANES)))
        part = pl.ds(corner * LANES, LANES)
        value = None
        for number in range(PIECES):
            both = (
                found[sub, chunk, pl.ds(number * LEVELS, LEVELS), part]
                + found[sub, chunk, pl.ds(size + number * LEVELS, LEVELS), part]
            )
            value = both if value is None else jnp.where(wanted[corner] == number, both, value)
        sums.append(value)
    values = (sums[0] + sums[1]) + (sums[2] + sums[3])
    for level in range(LEVELS):
        adjoint = adjoint + mixing[level] * values[level : level + 1]
    sources = [part.astype(f32) for part in split(adjoint)]
    for corner in range(CORNERS):
        part = pl.ds(corner * LANES, LANES)
        for place, source in enumerate(sources):
            spread[sub, chunk, pl.ds(place * size, size), part] = jnp.concatenate(
                [jnp.where(wanted[corner] == number, source, 0.0) for number in range(PIECES)],
                axis=0,
            ).astype(bf16)


def interpolate(state, stencil, sub, found):
    left = jnp.concatenate(split(state), axis=0)
    for chunk in range(CHUNKS):
        found[sub, chunk] = jnp.dot(left, stencil[sub, chunk], preferred_element_type=f32)


def scatter(slots, stencil, mixing, sub, found, spread):
    size = PIECES * LEVELS
    for chunk in range(CHUNKS):
        respond(slots, mixing, sub, chunk, found, spread)
    total = jnp.zeros((2 * size, HALF), f32)
    for chunk in range(CHUNKS):
        total = total + lax.dot_general(
            spread[sub, chunk], stencil[sub, chunk], (((1,), (1,)), ((), ())),
            preferred_element_type=f32,
        )
    return total[:size] + total[size:]


def stacked(rows):
    return jnp.concatenate(
        [rows[row][:, half * HALF : (half + 1) * HALF] for row in range(ROWS) for half in range(2)],
        axis=0,
    )


def unstacked(stack, row):
    places = [(2 * row + half) * LEVELS for half in range(2)]
    return jnp.concatenate([stack[place : place + LEVELS] for place in places], axis=1)


def forward_local_kernel(
    winds, forces, below, down_edge, own, mine, winds_below, lower_edge, forces_below
):
    unpack_winds(below, ROWS, winds_below)
    unpack_winds(down_edge, ROWS, lower_edge)
    for number, row in enumerate(decode(below, SUBS * ROWS, WIND_TILES)):
        forces_below[number] = row
    edge = dict(zip(DOWN_ROWS, decode(down_edge, len(DOWN_ROWS), WIND_TILES)))
    across = lower_winds(winds, winds_below, lower_edge)
    forced = lower_forces(forces, forces_below, edge)
    low = -2 * ROWS
    current = {row: forced[0](row) for row in range(low, ROWS)}
    current, low = forward_steps(current, across, low, 2)
    for sub in range(1, SUBS):
        current = add_rows(current, forced[sub], low, ROWS)
        current, low = forward_steps(current, across, low, 2)
    listed = [current[row] for row in range(-REACH, ROWS)]
    for number, row in enumerate(listed):
        mine[number] = row
    encode(listed[REACH - DROP :], own)


def time_is(condition):
    index = jnp.full((LEVELS, WIDTH), lax.axis_index("tm"), jnp.int32)
    return condition(index)


def lower_state(own, extended):
    here = decode(own, ROWS)
    under = decode(extended, ROWS + EXTRA)
    return {
        row: here[row] if row >= 0 else under[row + ROWS + EXTRA]
        for row in range(-(ROWS + EXTRA), ROWS)
    }


def forward_ahead_kernel(winds, winds_below, lower_edge, mine, ahead):
    @pl.when(lax.axis_index("tm") == 0)
    def _():
        across = lower_winds(winds, winds_below, lower_edge)
        current = {row: mine[row + REACH] for row in range(-REACH, ROWS)}
        current, low = forward_steps(current, across, -REACH, 6)
        for row in range(low, ROWS):
            ahead[row - low] = current[row]


def forward_pair_kernel(winds, winds_below, lower_edge, mine, ahead, other, own, extended):
    def finish(listed):
        encode(listed[EXTRA:], own)
        encode(listed, extended)

    @pl.when(lax.axis_index("tm") == 0)
    def _():
        rows = dict(zip(range(-DROP, ROWS), decode(other, DROP + ROWS)))
        finish([ahead[row + EXTRA] + rows[row] for row in range(-EXTRA, ROWS)])

    @pl.when(lax.axis_index("tm") == 1)
    def _():
        across = lower_winds(winds, winds_below, lower_edge)
        current = dict(zip(range(-DROP, ROWS), decode(other, DROP + ROWS)))
        current, low = forward_steps(current, across, -DROP, 6)
        listed = [mine[row + REACH] for row in range(-EXTRA, ROWS)]
        finish([
            value if row < low else value + current[row]
            for row, value in zip(range(-EXTRA, ROWS), listed)
        ])


def forward_final_kernel(
    winds, forces, winds_below, lower_edge, forces_below,
    before, pair_own, pair_extended, slots, stencil, mixing,
    sources, mine, response,
    found, spread, reached,
):
    across = lower_winds(winds, winds_below, lower_edge)
    forced = lower_forces(forces, forces_below)
    low = -DROP

    def keep(rows):
        for row in range(low, ROWS):
            reached[row - low] = rows[row]

    third = lax.axis_index("tm") == 2
    pl.when(third)(lambda: keep(lower_state(pair_own, pair_extended)))
    pl.when(jnp.logical_not(third))(
        lambda: keep(
            forward_steps(lower_state(pair_own, pair_extended), across, -(ROWS + EXTRA), 6)[0]
        )
    )
    before = decode(before, DROP + ROWS)
    odd = time_is(lambda index: (index & 1) == 1)
    current = {
        row: reached[row - low] + jnp.where(odd, before[row + DROP], 0.0)
        for row in range(low, ROWS)
    }
    for sub in range(SUBS):
        current = add_rows(current, forced[sub], low, ROWS)
        current, low = forward_steps(current, across, low, 2)
        interpolate(stacked(current), stencil, sub, found)
    current, low = {}, 0
    for sub in reversed(range(SUBS)):
        stack = scatter(slots, stencil, mixing, sub, found, spread)
        for row in range(ROWS):
            value = unstacked(stack, row)
            sources[sub * ROWS + row] = value
            current[row] = current[row] + value if row in current else value
        current, low = adjoint_steps(current, across, low, 2)
    listed = [current[row] for row in range(low, ROWS)]
    for number, row in enumerate(listed):
        mine[number] = row
    encode(listed, response)


def add_sources(current, sources, sub):
    return {
        row: value + sources[sub * ROWS + row] if row >= 0 else value
        for row, value in current.items()
    }


def adjoint_ahead_kernel(winds, winds_below, lower_edge, mine, ahead):
    @pl.when(lax.axis_index("tm") == 3)
    def _():
        across = lower_winds(winds, winds_below, lower_edge)
        current = {row: mine[row + DROP] for row in range(-DROP, ROWS)}
        current, low = adjoint_steps(current, across, -DROP, 6)
        for row in range(low, ROWS):
            ahead[row - low] = current[row]


def adjoint_pair_kernel(winds, winds_below, lower_edge, mine, ahead, other, own, near, far):
    low = -2 * DROP

    def finish(current):
        encode([current[row] for row in range(ROWS)], own)
        encode([current[row] for row in range(-ROWS, 0)], near)
        encode([current[row] for row in range(low, -ROWS)], far)

    @pl.when(lax.axis_index("tm") == 3)
    def _():
        rows = decode(other, DROP + ROWS)
        current = {row: ahead[row - low] for row in range(low, ROWS)}
        for row in range(-DROP, ROWS):
            current[row] = current[row] + rows[row + DROP]
        finish(current)

    @pl.when(lax.axis_index("tm") == 2)
    def _():
        across = lower_winds(winds, winds_below, lower_edge)
        current = dict(zip(range(-DROP, ROWS), decode(other, DROP + ROWS)))
        current, _ = adjoint_steps(current, across, -DROP, 6)
        for row in range(-DROP, ROWS):
            current[row] = current[row] + mine[row + DROP]
        finish(current)


PUSHED = [(sub, row) for sub in range(SUBS) for row in range(ROWS)]
PUSHED_FAR = [(sub, row) for sub in range(SUBS) for row in range(EXTRA + 2 * sub, ROWS)]


def adjoint_final_kernel(
    sources, winds, winds_below, lower_edge, after, pair_own, pair_near, pair_far,
    gradient, pushed, pushed_far,
):
    across = lower_winds(winds, winds_below, lower_edge)
    own = decode(pair_own, ROWS)
    near = decode(pair_near, ROWS)
    far = decode(pair_far, EXTRA)
    half_way = {row: own[row] + near[row] for row in range(ROWS)}
    for number, value in enumerate(far):
        half_way[ROWS - EXTRA + number] = half_way[ROWS - EXTRA + number] + value
    current, low = adjoint_steps(half_way, across, 0, 6)
    after = decode(after, DROP + ROWS)
    second = time_is(lambda index: index == 1)
    even = time_is(lambda index: (index & 1) == 0)
    for row in current:
        current[row] = jnp.where(second, half_way.get(row, 0.0), current[row])
        current[row] = current[row] + jnp.where(even, after[row + DROP], 0.0)
    results = [None] * SUBS
    for sub in reversed(range(SUBS)):
        current = add_sources(current, sources, sub)
        current, low = adjoint_steps(current, across, low, 2)
        results[sub] = current
        for row in range(ROWS):
            gradient[sub * ROWS + row] = current[row]
    encode([results[sub][row - ROWS] for sub, row in PUSHED], pushed)
    encode([results[sub][row - 2 * ROWS] for sub, row in PUSHED_FAR], pushed_far)


def finish_kernel(part, pushed, pushed_far, gradient_far, gradient, sems):
    near = dict(zip(PUSHED, decode(pushed, len(PUSHED))))
    far = dict(zip(PUSHED_FAR, decode(pushed_far, len(PUSHED_FAR))))
    copies = []
    for sub in range(SUBS):
        rows = []
        for row in range(ROWS):
            value = part[sub * ROWS + row] + near[sub, row]
            rows.append(value + far[sub, row] if (sub, row) in far else value)
        gradient[sub] = jnp.swapaxes(jnp.stack(rows), 0, 1)
        copies.append(
            pltpu.make_async_copy(gradient.at[sub], gradient_far.at[sub], sems.at[sub])
        )
        copies[-1].start()
    for copy in copies:
        copy.wait()


def run(kernel, outputs, arguments, scratch=(), name=None, flops=2_000_000, far=False, far_out=False):
    size = sum(a.size * a.dtype.itemsize for a in arguments)
    place = pltpu.HBM if far else pltpu.VMEM
    if far:
        arguments = [pltpu.with_memory_space_constraint(a, pltpu.HBM) for a in arguments]
    return pl.pallas_call(
        kernel,
        out_shape=outputs,
        in_specs=[pl.BlockSpec(memory_space=place)] * len(arguments),
        **({"out_specs": pl.BlockSpec(memory_space=pltpu.HBM)} if far_out else {}),
        scratch_shapes=scratch,
        compiler_params=pltpu.CompilerParams(vmem_limit_bytes=40 * 1024 * 1024),
        cost_estimate=pl.CostEstimate(flops=flops, bytes_accessed=size, transcendentals=0),
        name=name,
    )(*arguments)


STAY = {part: part for part in range(PARTS)}
FORWARD_FIRST, FORWARD_SECOND = {0: 1, 1: 0, 2: 3}, {1: 2, 0: 3}
ADJOINT_FIRST, ADJOINT_SECOND = {3: 2, 2: 3, 1: 0}, {2: 1, 3: 0}


def moved(array, parts, tiles):
    pairs = [
        (part * TILES + tile, to_part * TILES + tile + tiles)
        for part, to_part in parts.items()
        for tile in range(TILES)
        if 0 <= tile + tiles < TILES
    ]
    return lax.ppermute(array, ("tm", "space"), pairs)


def shards(
    forcing, courant, innovation, obs_cells, obs_weight, obs_owner, channel_weight, channel_rinv
):
    def message(tiles):
        return struct(tiles, LEVELS, LANES, dtype=jnp.int32)

    records = (
        innovation, obs_cells, obs_weight, jnp.swapaxes(obs_owner, 1, 2),
        channel_weight.T, channel_rinv.reshape(1, -1),
    )
    winds, forces, below, down_edge, *records = run(
        rows_kernel,
        (
            struct(WINDS * ROWS, LEVELS, WIDTH),
            struct(SUBS * ROWS, LEVELS, WIDTH),
            message(WIND_TILES + message_tiles(SUBS * ROWS)),
            message(WIND_TILES + message_tiles(len(DOWN_ROWS))),
            *[struct(*array.shape, dtype=array.dtype) for array in records],
        ),
        (forcing, courant, *records),
        scratch=(
            pltpu.VMEM(forcing.shape, f32),
            pltpu.VMEM(courant.shape, f32),
            pltpu.SemaphoreType.DMA((FIELDS + RECORD_ARRAYS,)),
        ),
        name="rows",
        far=True,
    )
    below = moved(below, STAY, 1)
    down_edge = moved(down_edge, STAY, 2)
    send = run(
        pack_kernel,
        struct(TILES * 8, LANES),
        records,
        name="pack",
    )
    received = lax.all_to_all(
        send.reshape(TILES, 8, LANES), "space", split_axis=0, concat_axis=0, tiled=True
    ).reshape(TILES * 8, LANES)
    below, down_edge, _ = lax.optimization_barrier((below, down_edge, send))
    own, mine, winds_below, lower_edge, forces_below = run(
        forward_local_kernel,
        (
            message(message_tiles(DROP + ROWS)),
            struct(REACH + ROWS, LEVELS, WIDTH),
            struct(WINDS * ROWS, LEVELS, WIDTH),
            struct(WINDS * ROWS, LEVELS, WIDTH),
            struct(SUBS * ROWS, LEVELS, WIDTH),
        ),
        (winds, forces, below, down_edge),
        name="forward_local",
        flops=2_000_000_000,
    )
    before = moved(own, FORWARD_FIRST, 0)
    pair_shapes = (message(message_tiles(ROWS)), message(message_tiles(ROWS + EXTRA)))
    ahead = run(
        forward_ahead_kernel,
        struct(EXTRA + ROWS, LEVELS, WIDTH),
        (winds, winds_below, lower_edge, mine),
        name="forward_ahead",
    )
    own, extended = run(
        forward_pair_kernel,
        pair_shapes,
        (winds, winds_below, lower_edge, mine, ahead, before),
        name="forward_pair",
    )
    pair = (moved(own, FORWARD_SECOND, 0), moved(extended, FORWARD_SECOND, 1))
    slots, stencil, mixing = run(
        stencil_kernel,
        (
            struct(SUBS, LANES, LANES),
            struct(SUBS, CHUNKS, HALF, CORNERS * LANES, dtype=bf16),
            struct(LEVELS, LEVELS, LANES),
        ),
        (received, *records[-2:]),
        scratch=(pltpu.VMEM((LANES, LANES), f32),),
        name="stencil",
    )
    size = PIECES * LEVELS
    sources, mine, response = run(
        forward_final_kernel,
        (
            struct(SUBS * ROWS, LEVELS, WIDTH),
            struct(DROP + ROWS, LEVELS, WIDTH),
            message(message_tiles(DROP + ROWS)),
        ),
        (
            winds, forces, winds_below, lower_edge, forces_below,
            before, *pair, slots, stencil, mixing,
        ),
        scratch=(
            pltpu.VMEM((SUBS, CHUNKS, 2 * size, CORNERS * LANES), f32),
            pltpu.VMEM((SUBS, CHUNKS, 2 * size, CORNERS * LANES), bf16),
            pltpu.VMEM((DROP + ROWS, LEVELS, WIDTH), f32),
        ),
        name="forward_final",
    )

    after = moved(response, ADJOINT_FIRST, 0)
    ahead = run(
        adjoint_ahead_kernel,
        struct(2 * DROP + ROWS, LEVELS, WIDTH),
        (winds, winds_below, lower_edge, mine),
        name="adjoint_ahead",
    )
    own, near, far = run(
        adjoint_pair_kernel,
        tuple(message(message_tiles(count)) for count in (ROWS, ROWS, EXTRA)),
        (winds, winds_below, lower_edge, mine, ahead, after),
        name="adjoint_pair",
    )
    pair = (
        moved(own, ADJOINT_SECOND, 0),
        moved(near, ADJOINT_SECOND, -1),
        moved(far, ADJOINT_SECOND, -2),
    )
    part, pushed, pushed_far = run(
        adjoint_final_kernel,
        (
            struct(SUBS * ROWS, LEVELS, WIDTH),
            message(message_tiles(len(PUSHED))),
            message(message_tiles(len(PUSHED_FAR))),
        ),
        (sources, winds, winds_below, lower_edge, after, *pair),
        name="adjoint_final",
    )
    pushed = moved(pushed, STAY, -1)
    pushed_far = moved(pushed_far, STAY, -2)
    return run(
        finish_kernel,
        struct(SUBS, LEVELS, ROWS, WIDTH),
        (part, pushed, pushed_far),
        scratch=(
            pltpu.VMEM((SUBS, LEVELS, ROWS, WIDTH), f32),
            pltpu.SemaphoreType.DMA((SUBS,)),
        ),
        name="finish",
        far_out=True,
    )


def solution(mesh):
    return jax.shard_map(
        shards,
        mesh=mesh,
        in_specs=(
            P("tm", None, "space", None),
            P(None, None, "space", None),
            P("tm", None, "space"),
            P("tm", None, "space"),
            P("tm", None, "space"),
            P("tm", "space", None),
            P(),
            P(),
        ),
        out_specs=P("tm", None, "space", None),
        check_vma=False,
    )
```
